32 devices in a mesh: dp: 8 (over y, x, core), fsdp: 4 (over z).
Axes of the slice: x: 2, y: 2, z: 4, core: 2. Of those that a mesh axis runs over, the one named last changes fastest.
Arguments:
- pixels: bfloat16 [12800, 512], P(('dp', 'fsdp')), may hold values from -6 to 6
- cotangent: bfloat16 [12800, 512], P(('dp', 'fsdp')), may hold values from -6 to 6
- image_plan: int32 [32, 2], P(('dp', 'fsdp')), may hold values from 0 to 4, as said below
- keep_mask: int32 [32, 16], P(('dp', 'fsdp')), may hold values 0 or 1
- norm_gains: bfloat16 [2, 1024], P(None, ('dp', 'fsdp')), may hold values from 0.5 to 1.5
- norm_biases: bfloat16 [2, 1024], P(None, ('dp', 'fsdp')), may hold values from -2 to 2
- layer_scales: bfloat16 [2, 1024], P(None, ('dp', 'fsdp')), may hold values from 0.5 to 1.5
- in_proj: bfloat16 [2, 512, 1024], P(None, ('dp', 'fsdp')), may hold values from -0.25 to 0.25
- depth_kernel: bfloat16 [2, 992, 49], P(None, 'fsdp'), may hold values from -2.5 to 2.5
- gated_weights: bfloat16 [2, 174080], P(None, ('dp', 'fsdp')), may hold values from -0.5 to 0.5
- out_proj: bfloat16 [2, 512, 512], P(None, ('dp', 'fsdp')), may hold values from -0.25 to 0.25
- up_proj: bfloat16 [2, 512, 2048], P(None, ('dp', 'fsdp')), may hold values from -0.25 to 0.25
- down_proj: bfloat16 [2, 2048, 512], P(None, ('dp', 'fsdp')), may hold values from -0.125 to 0.125
Outputs:
- result: bfloat16 [12800, 512], P(('dp', 'fsdp'))
- pixel_grad: float32 [12800, 512], P(('dp', 'fsdp'))
- gain_grad: float32 [2, 1024], P(None, ('dp', 'fsdp'))
- bias_grad: float32 [2, 1024], P(None, ('dp', 'fsdp'))
- scale_grad: float32 [2, 1024], P(None, ('dp', 'fsdp'))
- in_grad: float32 [2, 512, 1024], P(None, ('dp', 'fsdp'))
- kernel_grad: float32 [2, 992, 49], P(None, 'fsdp')
- gated_grad: float32 [2, 174080], P(None, ('dp', 'fsdp'))
- out_grad: float32 [2, 512, 512], P(None, ('dp', 'fsdp'))
- up_grad: float32 [2, 512, 2048], P(None, ('dp', 'fsdp'))
- down_grad: float32 [2, 2048, 512], P(None, ('dp', 'fsdp'))
The draws below stay inside these ranges and needn't reach their ends.
Inputs may be any that keep to these rules, and one draw needn't show every extreme that they name: `image_plan`: row r belongs to device r. Entry 0 is 1 if the device holds one image of 20 x 2 * 10 pixels, else 0 and its images are 10 x 10, one a quarter tile in row-major order. Entry 1 is the number of images: 1 when entry 0 is 1, else 1 to 4. In every draw some device holds one large image and some other device holds four small ones. `keep_mask`: row r belongs to device r; entry t * 2 * 2 + 2 * l + b keeps (1) or drops (0) branch b of block l for the image in quarter tile t (tile 0 for a large image).
All inputs are finite; a program needn't handle non-finite values.
Results may differ from the reference program's by a relative error of at most 0.025.
Values may be sent and summed in bfloat16 or wider, within the bound.
No kernel may reach another device: no remote copies, remote signals or barrier semaphores. Data moves between devices by JAX's collectives and lax.ppermute only.
A program may use at most 320 MiB of HBM per device.

```python
import math
import jax
import jax.numpy as jnp
from jax import lax

D = 512
FF = 2048
TILE = 10
LAYERS = 2
PIX_DEV = 400
PIX = 12800
DW_CH = 992
GATED = 174080
DEVICES = 32


def draw_image_plan(key, part):
    key = jax.random.fold_in(key, 11)
    key_large, key_count, key_full, key_big = jax.random.split(key, 4)
    device_ids = jnp.arange(DEVICES, dtype=jnp.int32)
    large = (jax.random.randint(key_large, (DEVICES,), 0, 4) == 0).astype(jnp.int32)
    counts = jax.random.randint(key_count, (DEVICES,), 1, 5).astype(jnp.int32)
    full_at = jax.random.randint(key_full, (), 0, DEVICES).astype(jnp.int32)
    big_at = (full_at + 1 + jax.random.randint(key_big, (), 0, DEVICES - 1).astype(jnp.int32)) % DEVICES
    large = jnp.where(device_ids == big_at, 1, jnp.where(device_ids == full_at, 0, large))
    counts = jnp.where(large == 1, 1, jnp.where(device_ids == full_at, 4, counts))
    return jnp.stack([large, counts], axis=1).astype(jnp.int32)


def with_ends(values, rng, low, largest):
    longest = values.shape.index(max(values.shape))
    spots = []
    for shift in (0, 1):
        where = [jax.random.randint(jax.random.fold_in(rng, axis), (), 0, length) for axis, length in enumerate(values.shape)]
        where[longest] = (where[longest] + shift) % values.shape[longest]
        spots.append(tuple(where))
    return values.at[spots[0]].set(low).at[spots[1]].set(largest)


def block_scale(rng, dims, shards, least, high):
    factor_of, own = 1.0, jax.random.fold_in(rng, 6)
    for axis_at, blocks in shards:
        steps = jnp.exp(jax.random.uniform(jax.random.fold_in(own, axis_at), (blocks,), jnp.float32, least / len(shards), high / len(shards)))
        factor_of = factor_of * jnp.repeat(steps, dims[axis_at] // blocks).reshape([-1 if axis == axis_at else 1 for axis in range(len(dims))])
    return factor_of


def noise(key, extent, scale, bound, pieces=(), kind=jnp.bfloat16):
    level = block_scale(key, extent, pieces, -0.22, 0.18) if pieces else 1.0
    result = jax.random.normal(key, extent, jnp.float32) * scale * level
    return jnp.minimum(jnp.maximum(result, -bound), bound).astype(kind)


def setup_inputs(seed: int = 0) -> dict:
    arg_keys = jax.random.split(jax.random.key(seed), 14)
    return {
        "pixels": noise(arg_keys[0], (PIX, D), 1.0, 6.0, ((0, 32),)),
        "cotangent": noise(arg_keys[1], (PIX, D), 1.0, 6.0, ((0, 32),)),
        "image_plan": draw_image_plan(jax.random.fold_in(arg_keys[13], 71), 0),
        "keep_mask": with_ends((jax.random.randint(arg_keys[3], (DEVICES, 8 * LAYERS), 0, 5) < 4).astype(jnp.int32), jax.random.fold_in(arg_keys[3], 1), 0, 1),
        "norm_gains": jnp.clip(1.0 + 0.1 * jax.random.normal(arg_keys[4], (LAYERS, 2 * D), jnp.float32), 0.5, 1.5).astype(jnp.bfloat16),
        "norm_biases": noise(arg_keys[5], (LAYERS, 2 * D), 0.3, 2.0, ((1, 32),)),
        "layer_scales": jnp.clip(jnp.exp(math.log(1.5) - 1.0986123 * jax.random.uniform(arg_keys[6], (LAYERS, 2 * D), jnp.float32) ** block_scale(arg_keys[6], (LAYERS, 2 * D), ((1, 32),), -0.2, 0.2)), 0.5, 1.5).astype(jnp.bfloat16),
        "in_proj": noise(arg_keys[7], (LAYERS, D, 2 * D), D ** -0.5, 0.25, ((1, 32),)),
        "depth_kernel": noise(arg_keys[8], (LAYERS, DW_CH, 49), 5 ** -0.5, 2.5, ((1, 4),)),
        "gated_weights": noise(arg_keys[9], (LAYERS, GATED), (D // 4) ** -0.5, 0.5, ((1, 32),)),
        "out_proj": noise(arg_keys[10], (LAYERS, D, D), D ** -0.5, 0.25, ((1, 32),)),
        "up_proj": noise(arg_keys[11], (LAYERS, D, FF), D ** -0.5, 0.25, ((1, 32),)),
        "down_proj": noise(arg_keys[12], (LAYERS, FF, D), FF ** -0.5, 0.125, ((1, 32),)),
    }


@jax.custom_vjp
def low(v):
    return lax.optimization_barrier(v.astype(jnp.bfloat16)).astype(jnp.float32)

@jax.custom_vjp
def low_back(v):
    return v

def low_keep(v):
    return (low(v), None)

def low_pass(kept, grad):
    return (grad,)

def back_keep(v):
    return (v, None)

def back_low(kept, grad):
    return (low(grad),)
low.defvjp(low_keep, low_pass)
low_back.defvjp(back_keep, back_low)

def matmul(left_op, right_op):
    return jnp.dot(left_op, right_op, precision=lax.Precision.HIGHEST)

def layer_norm(values, gain_vec, bias_vec):
    center = values - lax.optimization_barrier(jnp.mean(values, axis=-1, keepdims=True))
    spread = lax.optimization_barrier(jnp.mean(center * center, axis=-1, keepdims=True))
    return center * lax.rsqrt(spread + 1e-06) * gain_vec + bias_vec

def image_layout(layout_plan, edge_cells, tile_edge):
    row_ids = jnp.arange(edge_cells, dtype=jnp.int32)[:, None]
    col_ids = jnp.arange(edge_cells, dtype=jnp.int32)[None, :]
    quarter = row_ids // tile_edge * 2 + col_ids // tile_edge
    image_ids = jnp.where(layout_plan[0] == 1, jnp.zeros_like(quarter), quarter)
    occupied = jnp.where(layout_plan[0] == 1, jnp.ones_like(quarter), (quarter < layout_plan[1]).astype(jnp.int32))
    return (image_ids, occupied.astype(jnp.float32))

def branch_factors(layout_plan, keep_row, edge_cells, tile_edge):
    image_ids, occupied = image_layout(layout_plan, edge_cells, tile_edge)
    onehot = (image_ids.reshape(-1, 1) == jnp.arange(4, dtype=jnp.int32)[None, :]).astype(jnp.float32)
    keep_table = keep_row.reshape(4, -1).astype(jnp.float32)
    chosen = jnp.dot(onehot, keep_table, precision=lax.Precision.HIGHEST)
    return (image_ids, chosen * occupied.reshape(-1, 1) * 1.25)

def depthwise(values_in, kernel, image_ids):
    edge_cells = image_ids.shape[0]
    spatial = values_in.reshape(edge_cells, edge_cells, -1)
    padded = jnp.pad(spatial, ((3, 3), (3, 3), (0, 0)))
    padded_ids = jnp.pad(image_ids, 3, constant_values=-1)
    summed = jnp.zeros_like(spatial)
    for offset in range(49):
        row_off = offset // 7
        col_off = offset % 7
        nearby = padded[row_off:row_off + edge_cells, col_off:col_off + edge_cells]
        matched = (padded_ids[row_off:row_off + edge_cells, col_off:col_off + edge_cells] == image_ids).astype(jnp.float32)
        summed = summed + nearby * matched[:, :, None] * kernel[:, offset]
    return summed.reshape(values_in.shape) / 3.0

def gated_widths(model_width):
    return [model_width // 16, model_width // 8, model_width // 4, model_width // 2, model_width]

def split_gated(flat_weights, model_width):
    widths = gated_widths(model_width)
    matrices = []
    cursor = 0
    for section_idx in range(4):
        amount = widths[section_idx] * widths[section_idx + 1]
        matrices.append(flat_weights[cursor:cursor + amount].reshape(widths[section_idx], widths[section_idx + 1]))
        cursor = cursor + amount
    return matrices

def block(residual, layer_params, kernel, image_ids, factors):
    gain_vec, bias_vec, scale_vec, in_weight, gated_flat, out_weight, up_weight, down_weight = layer_params
    model_width = residual.shape[1]
    widths = gated_widths(model_width)
    normed = low(layer_norm(residual, gain_vec[:model_width], bias_vec[:model_width]))
    mixed_all = low_back(matmul(normed, in_weight))
    scaled = depthwise(mixed_all[:, widths[0]:], kernel, image_ids)
    product = mixed_all[:, :widths[0]] * scaled[:, :widths[0]]
    cursor = widths[0]
    for section_idx, matrix in enumerate(split_gated(gated_flat, model_width)):
        inner_out = low_back(matmul(low(product), matrix))
        product = inner_out * scaled[:, cursor:cursor + widths[section_idx + 1]]
        cursor = cursor + widths[section_idx + 1]
    branch = low_back(matmul(low(product), out_weight))
    middle = residual + factors[:, 0:1] * scale_vec[:model_width] * branch
    normed_two = low(layer_norm(middle, gain_vec[model_width:], bias_vec[model_width:]))
    hidden = low_back(matmul(normed_two, up_weight))
    activated = low(jax.nn.gelu(hidden))
    expanded = low_back(matmul(activated, down_weight))
    return middle + factors[:, 1:2] * scale_vec[model_width:] * expanded

def forward_buffer(residual, layout_plan, keep_row, params, edge_cells, tile_edge):
    image_ids, factors = branch_factors(layout_plan, keep_row, edge_cells, tile_edge)
    gains_all, biases_all, scales_all, in_all, kernel_all, gated_all, out_all, up_all, down_all = params
    for layer_idx in range(LAYERS):
        layer_params = (gains_all[layer_idx], biases_all[layer_idx], scales_all[layer_idx], in_all[layer_idx], gated_all[layer_idx], out_all[layer_idx], up_all[layer_idx], down_all[layer_idx])
        residual = block(residual, layer_params, kernel_all[layer_idx], image_ids, factors[:, 2 * layer_idx:2 * layer_idx + 2])
    return residual

def reference(pixels, cotangent, image_plan, keep_mask, norm_gains, norm_biases, layer_scales, in_proj, depth_kernel, gated_weights, out_proj, up_proj, down_proj):
    edge_cells = 2 * TILE
    params = (norm_gains.astype(jnp.float32), norm_biases.astype(jnp.float32), layer_scales.astype(jnp.float32), in_proj.astype(jnp.float32), depth_kernel.astype(jnp.float32), gated_weights.astype(jnp.float32), out_proj.astype(jnp.float32), up_proj.astype(jnp.float32), down_proj.astype(jnp.float32))
    groups = DEVICES // 4
    stacked_pixels = pixels.astype(jnp.float32).reshape(groups, 4, PIX_DEV, D)
    stacked_cot = cotangent.astype(jnp.float32).reshape(groups, 4, PIX_DEV, D)
    stacked_plans = image_plan.reshape(groups, 4, 2)
    stacked_keeps = keep_mask.reshape(groups, 4, 8 * LAYERS)

    def one_group(totals, inputs):
        group_pixels, group_cot, group_plans, group_keeps = inputs

        def run_forward(pixels_in, params_in):

            def single(residual, layout_plan, keep_row):
                return forward_buffer(residual, layout_plan, keep_row, params_in, edge_cells, TILE)
            return jax.vmap(single)(pixels_in, group_plans, group_keeps)
        outputs, pullback = jax.vjp(run_forward, group_pixels, params)
        pixel_grads, param_grads = pullback(group_cot)
        return (jax.tree.map(jnp.add, totals, param_grads), (outputs, pixel_grads))
    zero_grads = jax.tree.map(jnp.zeros_like, params)
    totals, (outputs, pixel_grads) = lax.scan(one_group, zero_grads, (stacked_pixels, stacked_cot, stacked_plans, stacked_keeps))
    gains_grad, biases_grad, scales_grad, in_grad, kernel_grad, gated_grad, out_grad, up_grad, down_grad = totals
    return (outputs.reshape(-1, D).astype(jnp.bfloat16), pixel_grads.reshape(-1, D), gains_grad, biases_grad, scales_grad, in_grad, kernel_grad, gated_grad, out_grad, up_grad, down_grad)
```

```python
from functools import partial
import math

import jax
import jax.numpy as jnp
import numpy as np
from jax import lax
from jax.experimental import pallas as pl
from jax.experimental.pallas import tpu as pltpu
from jax.sharding import PartitionSpec as P

BF = jnp.bfloat16
F32 = jnp.float32
HALF = 352
SIDE = 512
WIN = 12
VMEM_BYTES = 56 * 1024 * 1024


def half_spectrum(size):
    seen = set()
    kept = []
    for row in range(size):
        for col in range(size):
            if ((-row) % size, (-col) % size) in seen:
                continue
            seen.add((row, col))
            kept.append((row, col))
    return kept


def fourier_tables(edge):
    tile = edge // 2
    plans = [
        [(0, 0, tile), (0, tile, tile), (tile, 0, tile), (tile, tile, tile)],
        [(0, 0, edge)],
    ]
    forward = np.zeros((2, 2 * HALF, edge * edge), np.float32)
    taps = np.zeros((2, 2 * HALF, 64), np.float32)
    for which, tiles in enumerate(plans):
        at = 0
        for top, left, extent in tiles:
            size = extent + 3
            rows, cols = np.meshgrid(np.arange(extent), np.arange(extent), indexing="ij")
            slots = ((rows + top) * edge + cols + left).reshape(-1)
            tap_rows, tap_cols = np.meshgrid(np.arange(7) - 3, np.arange(7) - 3, indexing="ij")
            for fr, fc in half_spectrum(size):
                angle = 2 * np.pi * ((fr * rows + fc * cols) % size) / size
                forward[which, at, slots] = np.cos(angle).reshape(-1)
                forward[which, HALF + at, slots] = np.sin(angle).reshape(-1)
                weight = (1.0 if (fr, fc) == (0, 0) else 2.0) / (3.0 * size * size)
                angle = 2 * np.pi * ((fr * tap_rows + fc * tap_cols) % size) / size
                taps[which, at, :49] = weight * np.cos(angle).reshape(-1)
                taps[which, HALF + at, :49] = weight * np.sin(angle).reshape(-1)
                at += 1
        assert at <= HALF
    return (
        forward,
        np.ascontiguousarray(forward.transpose(0, 2, 1)),
        taps,
        np.ascontiguousarray(taps.transpose(0, 2, 1)),
    )


def mm(left, right):
    return lax.dot_general(left, right, (((1,), (0,)), ((), ())), preferred_element_type=F32)


def mm_nt(left, right):
    return lax.dot_general(left, right, (((1,), (1,)), ((), ())), preferred_element_type=F32)


def mm_tn(left, right):
    return lax.dot_general(left, right, (((0,), (0,)), ((), ())), preferred_element_type=F32)


def iota2(shape, dim):
    return lax.broadcasted_iota(jnp.int32, shape, dim)


def pixel_factor(plan_ref, keep_ref, column, edge, tile):
    slot = iota2((edge * edge, 1), 0)
    row = jnp.floor((slot.astype(F32) + 0.5) * (1.0 / edge)).astype(jnp.int32)
    col = slot - row * edge
    quarter = jnp.where(row >= tile, 2, 0) + jnp.where(col >= tile, 1, 0)
    large = plan_ref[0, 0]
    count = plan_ref[0, 1]
    width = keep_ref.shape[1] // 4
    total = jnp.zeros((edge * edge, 1), F32)
    for t in range(4):
        kept = keep_ref[0, t * width + column].astype(F32) * 1.25
        first = keep_ref[0, column].astype(F32) * 1.25
        here = jnp.where(t < count, kept, 0.0)
        here = jnp.where(large == 1, first, here)
        total = jnp.where(quarter == t, here, total)
    return total


def norm_stats(values):
    center = values - jnp.mean(values, axis=-1, keepdims=True)
    rstd = lax.rsqrt(jnp.mean(center * center, axis=-1, keepdims=True) + 1e-06)
    return center * rstd, rstd


def norm_back(grad, normal, rstd, gain):
    inner = grad * gain
    return rstd * (
        inner
        - jnp.mean(inner, axis=-1, keepdims=True)
        - normal * jnp.mean(inner * normal, axis=-1, keepdims=True)
    )


def window_map(shards, per):
    shape = (HALF, shards * 16)
    r = iota2(shape, 0)
    c = iota2(shape, 1)
    shard = lax.shift_right_logical(c, 4)
    t = c & 15
    flat_row = jnp.where(
        r < 256, r + 84, jnp.where(r < 320, r - 236, jnp.where(r < 336, r - 316, r - 336))
    )
    start = lax.shift_right_logical(shard * (per // 64), 3)
    gated = (t < WIN) & (r < 340) & (flat_row == start + t)
    norm = r - 344
    second = jnp.where(shard >= shards // 2, 1, 0)
    vec = (norm >= 0) & (norm < 6) & (t == WIN + lax.shift_right_arithmetic(norm, 1)) & ((norm & 1) == second)
    return jnp.where(gated | vec, 1.0, 0.0).astype(BF)


def spread(rows, cols, stride, offset, shift):
    r = iota2((rows, cols), 0) - shift
    c = iota2((rows, cols), 1)
    return jnp.where(r == stride * c + offset, 1.0, 0.0).astype(BF)


def lanes_from(values, low, high):
    lane = iota2(values.shape, 1)
    return jnp.where((lane >= low) & (lane < high), values, jnp.zeros_like(values))


def gated_matrices(flat):
    g2 = mm(spread(128, 64, 2, 0, 0), flat[256:320, 0:256]) + mm(
        spread(128, 64, 2, 1, 0), flat[256:320, 256:512]
    )
    g1 = jnp.zeros((128, 128), F32)
    for h in range(4):
        g1 = g1 + mm(spread(128, 16, 4, h, 64), flat[320:336, 128 * h : 128 * h + 128])
    g0 = jnp.zeros((128, 128), F32)
    for t in range(4):
        part = flat[336:352, 128 * t : 128 * t + 128].astype(F32)
        part = jnp.where(iota2(part.shape, 0) < 4, part, 0.0)
        odd = lanes_from(part, 64, 128).astype(BF)
        even = lanes_from(pltpu.roll(part, 64, 1), 64, 128).astype(BF)
        g0 = g0 + mm(spread(128, 16, 8, 2 * t, 32), even) + mm(spread(128, 16, 8, 2 * t + 1, 32), odd)
    return g0.astype(BF), g1.astype(BF), g2.astype(BF)


def start_pieces(pieces, place, spots, sems, copies):
    yx = place[0]
    core = place[1]
    for number, piece in enumerate(pieces):
        source = core if number < 4 else 1 - core
        r1 = number & 1
        r2 = (number >> 1) & 1
        first = jnp.where(source == 0, 1, 2)
        spot = yx ^ (r1 * first) ^ (r2 * (3 - first))
        for row, rows, target in spots:
            copy = pltpu.make_async_copy(piece.at[:, pl.ds(row, rows), :], target(spot, source), sems.at[len(copies)])
            copy.start()
            copies.append(copy)


def grad_place(place, shard):
    yx = place[0]
    core = place[1]
    z = place[2]
    zrel = (shard % 4) ^ z
    dest = (shard // 4) % 2
    rel = (shard // 8) ^ yx
    if dest == 0:
        r1, r2 = rel & 1, rel >> 1
    else:
        r1, r2 = rel >> 1, rel & 1
    return dest ^ core, r1, r2, zrel


def gelu_parts(hidden):
    root = math.sqrt(2.0 / math.pi)
    square = hidden * hidden
    bent = jnp.tanh(root * hidden * (1.0 + 0.044715 * square))
    half = 0.5 * (1.0 + bent)
    value = hidden * half
    slope = half + 0.5 * hidden * (1.0 - bent * bent) * (root * (1.0 + 0.134145 * square))
    return value, slope


def emit_rows(value, rows_ref, keep_ref, send_ref, row, place):
    rows_ref[...] = value.astype(BF).reshape(rows_ref.shape)
    yx = place[0]
    z = place[2]
    for sel, ref in ((0, keep_ref), (1, send_ref)):
        dest = place[1] ^ sel
        first = jnp.where(dest == 0, 1, 2)
        for r1 in range(2):
            for r2 in range(2):
                spot = yx ^ (r1 * first) ^ (r2 * (3 - first))
                for zrel in range(4):
                    ref[r1, r2, zrel, pl.ds(row, 16), :] = rows_ref[spot * 8 + dest * 4 + (z ^ zrel)]


def mix_forward_kernel(
    layer, edge, per, place, plan, keep, x_ref, taps_ref, forward_hbm, back_hbm, tapmap_hbm, *rest
):
    pieces = rest[:8]
    m1_ref, a0_ref, q_ref, z_ref, y_ref, spec_ref, flat_ref, g0_ref, g1_ref, g2_ref, norm_ref = rest[8:19]
    w_ref, forward, back, tapmap, a_low, sems = rest[19:]
    shards = 32
    copies = []
    mode = plan[0, 0]
    spots = [
        (16 * b, 16, (lambda spot, source, b=b: w_ref.at[b, spot, source])) for b in (3, 0, 1, 2)
    ]
    start_pieces(pieces, place, spots, sems, copies)
    tables = []
    for n, (src, dst) in enumerate(((forward_hbm, forward), (tapmap_hbm, tapmap), (back_hbm, back))):
        tables.append(pltpu.make_async_copy(src.at[mode], dst, sems.at[len(copies) + n]))
        tables[-1].start()
    factor = pixel_factor(plan, keep, 2 * layer, edge, edge // 2)
    picks = window_map(shards, per)
    for copy in copies:
        copy.wait()
    flat = mm(picks, w_ref[3].reshape(SIDE, SIDE))
    norm_ref[...] = flat[344:352]
    flat_low = flat.astype(BF)
    flat_ref[...] = flat_low
    g0, g1, g2 = gated_matrices(flat_low)
    g0_ref[...] = g0
    g1_ref[...] = g1
    g2_ref[...] = g2
    x = x_ref[...].astype(F32)
    normal, unused = norm_stats(x)
    u = (normal * flat[344:345] + flat[346:347]).astype(BF)
    for half in range(2):
        a = mm(u, w_ref[half].reshape(SIDE, SIDE))
        a_low[:, SIDE * half : SIDE * half + SIDE] = a.astype(BF)
        if half == 0:
            a0_ref[...] = a[:, :128]
    for copy in tables:
        copy.wait()

    def channels(j, carry):
        at = pl.ds(pl.multiple_of(j * 256, 256), 256)
        kernel = mm(tapmap[...], taps_ref[:, at])
        spec = mm(forward[...], a_low[:, at])
        spec_ref[:, at] = spec.astype(BF)
        kr, ki = kernel[:HALF], kernel[HALF:]
        xc, xs = spec[:HALF], spec[HALF:]
        product = jnp.concatenate([xc * kr + xs * ki, xs * kr - xc * ki], axis=0).astype(BF)
        q_ref[:, at] = mm(back[...], product)
        return carry

    lax.fori_loop(0, 4, channels, 0)
    a0 = a0_ref[...]
    q0 = q_ref[:, 0:128]
    p = lanes_from(pltpu.roll(a0, 32, 1) * q0, 32, 64).astype(BF)
    z0 = mm(p, g0)
    z_ref[:, 0:128] = z0
    p = (z0 * q0).astype(BF)
    z1 = mm(p, g1)
    z_ref[:, 128:256] = z1
    p = (z1 * q_ref[:, 128:256]).astype(BF)
    z2 = mm(p, g2)
    z_ref[:, 256:512] = z2
    p = (z2 * q_ref[:, 256:512]).astype(BF)
    z3 = mm(p, flat_ref[0:256, :])
    z_ref[:, 512:1024] = z3
    p = (z3 * q_ref[:, 512:1024]).astype(BF)
    y = mm(p, w_ref[2].reshape(SIDE, SIDE))
    y_ref[...] = y
    m1_ref[...] = x + factor * flat[348:349] * y


def feed_spots(up_ref, down_ref):
    spots = [(16 * b, 16, (lambda spot, source, b=b: up_ref.at[b, spot, source])) for b in range(4)]
    spots.append((64, 64, lambda spot, source: down_ref.at[spot, source]))
    return spots


def feed_forward_kernel(layer, edge, last, place, plan, keep, m1_ref, norm_ref, *rest):
    pieces = rest[:8]
    x_ref, h_ref, f_ref = rest[8:11]
    up_ref, down_ref, sems = rest[11:]
    copies = []
    start_pieces(pieces, place, feed_spots(up_ref, down_ref), sems, copies)
    factor = pixel_factor(plan, keep, 2 * layer + 1, edge, edge // 2)
    m1 = m1_ref[...]
    normal, unused = norm_stats(m1)
    v = (normal * norm_ref[1:2] + norm_ref[3:4]).astype(BF)
    f_ref[...] = jnp.zeros_like(f_ref)
    for copy in copies:
        copy.wait()

    def hidden(j, carry):
        at = pl.ds(pl.multiple_of(j * SIDE, SIDE), SIDE)
        h = mm(v, up_ref[j].reshape(SIDE, SIDE))
        h_ref[:, at] = h
        e = gelu_parts(h)[0].astype(BF)
        f_ref[...] += mm(e, down_ref[j].reshape(SIDE, SIDE))
        return carry

    lax.fori_loop(0, 4, hidden, 0)
    x_ref[...] = (m1 + factor * norm_ref[5:6] * f_ref[...]).astype(x_ref.dtype)


def feed_back_kernel(layer, edge, place, plan, keep, dx_ref, m1_ref, h_ref, f_ref, norm_ref, *rest):
    pieces = rest[:8]
    dm1_ref, keep_out, send_out, small_ref = rest[8:12]
    up_ref, down_ref, dv_ref, rows_ref, sems = rest[12:]
    copies = []
    start_pieces(pieces, place, feed_spots(up_ref, down_ref), sems, copies)
    factor = pixel_factor(plan, keep, 2 * layer + 1, edge, edge // 2)
    dx = dx_ref[...].astype(F32)
    scaled = dx * factor
    small_ref[...] = jnp.zeros_like(small_ref)
    small_ref[5:6] = jnp.sum(scaled * f_ref[...], axis=0, keepdims=True)
    df = (scaled * norm_ref[5:6]).astype(BF)
    normal, rstd = norm_stats(m1_ref[...])
    v = (normal * norm_ref[1:2] + norm_ref[3:4]).astype(BF)
    dv_ref[...] = jnp.zeros_like(dv_ref)
    for copy in copies:
        copy.wait()
    yx = place[0]
    z = place[2]

    def hidden(j, carry):
        at = pl.ds(pl.multiple_of(j * SIDE, SIDE), SIDE)
        h = h_ref[:, at]
        value, slope = gelu_parts(h)
        e = value.astype(BF)
        dh = (slope * mm_nt(df, down_ref[j].reshape(SIDE, SIDE))).astype(BF)
        dv_ref[...] += mm_nt(dh, up_ref[j].reshape(SIDE, SIDE))
        emit_rows(mm_tn(v, dh), rows_ref, keep_out, send_out, pl.multiple_of(j * 16, 16), place)
        rows_ref[...] = mm_tn(e, df).astype(BF).reshape(rows_ref.shape)
        rel = j ^ yx
        for sel, ref in ((0, keep_out), (1, send_out)):
            dest = place[1] ^ sel
            r1 = jnp.where(dest == 0, rel & 1, rel >> 1)
            r2 = jnp.where(dest == 0, rel >> 1, rel & 1)
            for zrel in range(4):
                part = rows_ref[pl.ds((dest * 4 + (z ^ zrel)) * 4, 4)]
                ref[r1, r2, zrel, 64:128, :] = part.reshape(64, SIDE)
        return carry

    lax.fori_loop(0, 4, hidden, 0)
    dv = dv_ref[...]
    small_ref[1:2] = jnp.sum(dv * normal, axis=0, keepdims=True)
    small_ref[3:4] = jnp.sum(dv, axis=0, keepdims=True)
    dm1_ref[...] = dx + norm_back(dv, normal, rstd, norm_ref[1:2])


def mix_back_kernel(
    layer,
    edge,
    per,
    place,
    plan,
    keep,
    dm1_ref,
    x_ref,
    a0_ref,
    q_ref,
    z_ref,
    y_ref,
    spec_ref,
    flat_ref,
    g0_ref,
    g1_ref,
    g2_ref,
    norm_ref,
    small_ref,
    taps_ref,
    spreads_ref,
    forward_hbm,
    back_hbm,
    tapmap_hbm,
    tapback_hbm,
    *rest,
):
    pieces = rest[:8]
    dx_ref, keep_out, send_out, kernel_out = rest[8:12]
    w_ref, forward, back, tapmap, tapback, dq_ref, da_ref, dflat_ref, dtaps_ref, rows_ref, sems = rest[12:]
    copies = []
    mode = plan[0, 0]
    spots = [(16 * b, 16, (lambda spot, source, b=b: w_ref.at[b, spot, source])) for b in (2, 0, 1)]
    start_pieces(pieces, place, spots, sems, copies)
    for src, dst in (
        (forward_hbm, forward),
        (back_hbm, back),
        (tapmap_hbm, tapmap),
        (tapback_hbm, tapback),
    ):
        copies.append(pltpu.make_async_copy(src.at[mode], dst, sems.at[len(copies)]))
        copies[-1].start()
    factor = pixel_factor(plan, keep, 2 * layer, edge, edge // 2)
    dm1 = dm1_ref[...]
    scaled = dm1 * factor
    dscale = jnp.sum(scaled * y_ref[...], axis=0, keepdims=True)
    dy = (scaled * norm_ref[4:5]).astype(BF)
    q4 = q_ref[:, 512:1024]
    z3 = z_ref[:, 512:1024]
    p4 = (z3 * q4).astype(BF)
    for copy in copies:
        copy.wait()
    emit_rows(mm_tn(p4, dy), rows_ref, keep_out, send_out, 32, place)
    dp = mm_nt(dy, w_ref[2].reshape(SIDE, SIDE))
    dz = (dp * q4).astype(BF)
    dq_ref[:, 512:1024] = (dp * z3).astype(BF)
    z2 = z_ref[:, 256:512]
    q3 = q_ref[:, 256:512]
    dflat_ref[0:256, :] = mm_tn((z2 * q3).astype(BF), dz)
    dp = mm_nt(dz, flat_ref[0:256, :])
    dz = (dp * q3).astype(BF)
    dq_ref[:, 256:512] = (dp * z2).astype(BF)
    z1 = z_ref[:, 128:256]
    q2 = q_ref[:, 128:256]
    dg2 = mm_tn((z1 * q2).astype(BF), dz).astype(BF)
    for h in range(2):
        dflat_ref[256:320, 256 * h : 256 * h + 256] = mm_tn(spread(128, 64, 2, h, 0), dg2)
    dp = mm_nt(dz, g2_ref[...])
    dz = (dp * q2).astype(BF)
    dq_ref[:, 128:256] = (dp * z1).astype(BF)
    z0 = z_ref[:, 0:128]
    q01 = q_ref[:, 0:128]
    dg1 = mm_tn((z0 * q01).astype(BF), dz).astype(BF)
    for h in range(4):
        dflat_ref[320:336, 128 * h : 128 * h + 128] = mm_tn(spread(128, 16, 4, h, 64), dg1)
    dp = mm_nt(dz, g1_ref[...])
    dz = (dp * q01).astype(BF)
    dq1 = dp * z0
    head = lanes_from(pltpu.roll(a0_ref[...], 32, 1), 32, 64)
    dg0 = mm_tn((head * q01).astype(BF), dz).astype(BF)
    for t in range(4):
        even = mm_tn(spread(128, 16, 8, 2 * t, 32), dg0)
        odd = mm_tn(spread(128, 16, 8, 2 * t + 1, 32), dg0)
        dflat_ref[336:352, 128 * t : 128 * t + 128] = lanes_from(odd, 64, 128) + pltpu.roll(
            lanes_from(even, 64, 128), 64, 1
        )
    dp = mm_nt(dz, g0_ref[...])
    dq_ref[:, 0:128] = (dq1 + dp * head).astype(BF)
    dhead = pltpu.roll(lanes_from(dp * q01, 32, 64), 96, 1)

    def channels(j, carry):
        at = pl.ds(pl.multiple_of(j * 256, 256), 256)
        kernel = mm(tapmap[...], taps_ref[:, at])
        grad = mm(forward[...], dq_ref[:, at])
        spec = spec_ref[:, at].astype(F32)
        kr, ki = kernel[:HALF], kernel[HALF:]
        dc, ds = grad[:HALF], grad[HALF:]
        xc, xs = spec[:HALF], spec[HALF:]
        dspec = jnp.concatenate([dc * kr - ds * ki, dc * ki + ds * kr], axis=0).astype(BF)
        da_ref[:, at] = mm(back[...], dspec).astype(BF)
        dkernel = jnp.concatenate([dc * xc + ds * xs, dc * xs - ds * xc], axis=0).astype(BF)
        dtaps_ref[:, at] = mm(tapback[...], dkernel).astype(BF)
        return carry

    lax.fori_loop(0, 4, channels, 0)
    da_ref[:, 0:128] = (da_ref[:, 0:128].astype(F32) + dhead).astype(BF)
    z = place[2]
    for zrel in range(4):
        kernel_out[zrel] = mm_nt(dtaps_ref[...], spreads_ref[z ^ zrel]).astype(BF)
    normal, rstd = norm_stats(x_ref[...].astype(F32))
    gain = norm_ref[0:1]
    u = (normal * gain + norm_ref[2:3]).astype(BF)
    du = jnp.zeros(dm1.shape, F32)
    for half in range(2):
        da = da_ref[:, SIDE * half : SIDE * half + SIDE]
        emit_rows(mm_tn(u, da), rows_ref, keep_out, send_out, 16 * half, place)
        du = du + mm_nt(da, w_ref[half].reshape(SIDE, SIDE))
    dflat_ref[344:352, :] = small_ref[...]
    dflat_ref[344:345, :] = jnp.sum(du * normal, axis=0, keepdims=True)
    dflat_ref[346:347, :] = jnp.sum(du, axis=0, keepdims=True)
    dflat_ref[348:349, :] = dscale
    picks = window_map(32, per)
    emit_rows(mm_tn(picks, dflat_ref[...].astype(BF)), rows_ref, keep_out, send_out, 48, place)
    dx_ref[...] = dm1 + norm_back(du, normal, rstd, gain)


def whole(shape, dtype):
    return jax.ShapeDtypeStruct(shape, dtype)


VM = pl.BlockSpec(memory_space=pltpu.VMEM)
SM = pl.BlockSpec(memory_space=pltpu.SMEM)
HB = pl.BlockSpec(memory_space=pl.ANY)


def call(kernel, ins, in_specs, outs, scratch, flops, moved, name):
    return pl.pallas_call(
        kernel,
        out_shape=outs,
        in_specs=in_specs,
        out_specs=jax.tree.map(lambda unused: VM, outs),
        scratch_shapes=scratch,
        compiler_params=pltpu.CompilerParams(vmem_limit_bytes=VMEM_BYTES),
        cost_estimate=pl.CostEstimate(flops=flops, bytes_accessed=moved, transcendentals=0),
        name=name,
    )(*ins)


def z_assemble_kernel(place, *rest):
    pieces, out, sems = rest[:4], rest[4], rest[5]
    copies = [
        pltpu.make_async_copy(piece, out.at[place[2] ^ k], sems.at[k]) for k, piece in enumerate(pieces)
    ]
    for copy in copies:
        copy.start()
    for copy in copies:
        copy.wait()


def z_assemble(place, pieces):
    return pl.pallas_call(
        z_assemble_kernel,
        out_shape=whole((4, *pieces[0].shape), pieces[0].dtype),
        in_specs=[SM] + [HB] * 4,
        out_specs=HB,
        scratch_shapes=[pltpu.SemaphoreType.DMA((4,))],
        cost_estimate=pl.CostEstimate(flops=0, bytes_accessed=8 * pieces[0].size * 2, transcendentals=0),
        name="z_assemble",
    )(place, *pieces)


CORE = [(i, i ^ 1) for i in range(8)]
FIRST = [(i, i ^ (4 if i & 1 else 2)) for i in range(8)]
SECOND = [(i, i ^ (2 if i & 1 else 4)) for i in range(8)]
AXIS_X = [(i, i ^ 2) for i in range(8)]
AXIS_Y = [(i, i ^ 4) for i in range(8)]


def along(values, perm):
    return lax.ppermute(values, "dp", perm)


def along_z(values, k):
    return lax.ppermute(values, "fsdp", [(i, i ^ k) for i in range(4)])


def gather_pack(place, pack):
    own = z_assemble(place, [pack] + [along_z(pack, k) for k in (1, 2, 3)])
    first = along(own, FIRST)
    second = along(own, SECOND)
    both = along(first, SECOND)
    mine = [own, first, second, both]
    return mine + [along(piece, CORE) for piece in mine]


def add(*terms):
    total = terms[0].astype(F32)
    for term in terms[1:]:
        total = total + term.astype(F32)
    return total


def scatter_pack(keep, send):
    recv = along(send, CORE)
    got1 = along(add(keep[1], recv[1]).astype(BF), FIRST)
    got2 = along(add(keep[0, 1], recv[0, 1], got1[1]).astype(BF), SECOND)
    parts = [add(keep[0, 0, k], recv[0, 0, k], got1[0, k], got2[k]) for k in range(4)]
    return add(parts[0], *[along_z(parts[k].astype(BF), k) for k in (1, 2, 3)])


def fast_device(
    pixels,
    cotangent,
    image_plan,
    keep_mask,
    norm_gains,
    norm_biases,
    layer_scales,
    in_proj,
    depth_kernel,
    gated_weights,
    out_proj,
    up_proj,
    down_proj,
):
    pix, width = pixels.shape
    edge = math.isqrt(pix)
    layers = in_proj.shape[0]
    per = gated_weights.shape[1]
    dp = lax.axis_index("dp")
    z = lax.axis_index("fsdp")
    me = dp * 4 + z
    place = jnp.stack([dp >> 1, dp & 1, z, me]).astype(jnp.int32)
    phase = 64 * ((me * (per // 64)) % 8)
    lane = 32 * (me % 16)
    forward, back, tapmap, tapback = [jnp.asarray(t, BF) for t in fourier_tables(edge)]

    padded = lax.dynamic_update_slice(
        jnp.zeros((layers, WIN * SIDE), BF), gated_weights, (jnp.int32(0), phase)
    ).reshape(layers, WIN, SIDE)
    vectors = lax.dynamic_update_slice(
        jnp.zeros((layers, 4, SIDE), BF),
        jnp.stack([norm_gains, norm_biases, layer_scales], axis=1),
        (jnp.int32(0), jnp.int32(0), lane),
    )
    packs = []
    for l in range(layers):
        packs.append(
            jnp.concatenate(
                [in_proj[l, :, :SIDE], in_proj[l, :, SIDE:], out_proj[l], padded[l], vectors[l]], axis=0
            )
        )
        packs.append(
            jnp.concatenate([up_proj[l, :, SIDE * b : SIDE * b + SIDE] for b in range(4)] + [down_proj[l]], axis=0)
        )
    count = depth_kernel.shape[1]
    tap_shard = jnp.pad(jnp.swapaxes(depth_kernel, 1, 2), ((0, 0), (0, 15), (0, 256 - count)))
    gathered = [gather_pack(place, packs[0])]
    taps = z_assemble(place, [tap_shard] + [along_z(tap_shard, k) for k in (1, 2, 3)])
    taps = jnp.concatenate(
        [jnp.zeros((layers, 64, 32), BF)] + [taps[k, :, :, :count] for k in range(4)], axis=2
    )
    gathered += [gather_pack(place, pack) for pack in packs[1:]]
    spread_rows = np.zeros((4, 256, 1024), np.float32)
    for k in range(4):
        spread_rows[k, np.arange(count), 32 + count * k + np.arange(count)] = 1.0
    spreads = jnp.asarray(spread_rows, BF)

    x = pixels
    kept = []
    for l in range(layers):
        mix_pieces = gathered[2 * l]
        feed_pieces = gathered[2 * l + 1]
        mixed = call(
            partial(mix_forward_kernel, l, edge, per),
            (place, image_plan, keep_mask, x, taps[l], forward, back, tapmap, *mix_pieces),
            [SM, SM, SM, VM, VM, HB, HB, HB] + [HB] * 8,
            (
                whole((pix, width), F32),
                whole((pix, 128), F32),
                whole((pix, 1024), F32),
                whole((pix, 1024), F32),
                whole((pix, width), F32),
                whole((2 * HALF, 1024), BF),
                whole((HALF, SIDE), BF),
                whole((128, 128), BF),
                whole((128, 128), BF),
                whole((128, 256), BF),
                whole((8, SIDE), F32),
            ),
            [
                pltpu.VMEM((4, 4, 2, 4, 16, SIDE), BF),
                pltpu.VMEM((2 * HALF, pix), BF),
                pltpu.VMEM((pix, 2 * HALF), BF),
                pltpu.VMEM((2 * HALF, 64), BF),
                pltpu.VMEM((pix, 1024), BF),
                pltpu.SemaphoreType.DMA((40,)),
            ],
            4_000_000_000,
            10_000_000,
            "mix_forward",
        )
        m1, norms = mixed[0], mixed[10]
        last = l == layers - 1
        new_x, h, f = call(
            partial(feed_forward_kernel, l, edge, last),
            (place, image_plan, keep_mask, m1, norms, *feed_pieces),
            [SM, SM, SM, VM, VM] + [HB] * 8,
            (
                whole((pix, width), BF if last else F32),
                whole((pix, 4 * SIDE), F32),
                whole((pix, width), F32),
            ),
            [
                pltpu.VMEM((4, 4, 2, 4, 16, SIDE), BF),
                pltpu.VMEM((4, 2, 4, 64, SIDE), BF),
                pltpu.SemaphoreType.DMA((48,)),
            ],
            2_000_000_000,
            10_000_000,
            "feed_forward",
        )
        kept.append((x, mixed, h, f))
        x = new_x
    result = x

    dx = cotangent
    sums = [None] * (2 * layers)
    kernel_sums = [None] * layers
    for l in reversed(range(layers)):
        x, mixed, h, f = kept[l]
        m1, a0, q, zs, y, spec, flat, g0, g1, g2, norms = mixed
        dm1, keep_b, send_b, small = call(
            partial(feed_back_kernel, l, edge),
            (place, image_plan, keep_mask, dx, m1, h, f, norms, *gathered[2 * l + 1]),
            [SM, SM, SM, VM, VM, VM, VM, VM] + [HB] * 8,
            (
                whole((pix, width), F32),
                whole((2, 2, 4, 128, SIDE), BF),
                whole((2, 2, 4, 128, SIDE), BF),
                whole((8, SIDE), F32),
            ),
            [
                pltpu.VMEM((4, 4, 2, 4, 16, SIDE), BF),
                pltpu.VMEM((4, 2, 4, 64, SIDE), BF),
                pltpu.VMEM((pix, width), F32),
                pltpu.VMEM((32, 16, SIDE), BF),
                pltpu.SemaphoreType.DMA((48,)),
            ],
            4_000_000_000,
            16_000_000,
            "feed_back",
        )
        sums[2 * l + 1] = scatter_pack(keep_b, send_b)
        dx, keep_a, send_a, dtaps = call(
            partial(mix_back_kernel, l, edge, per),
            (
                place,
                image_plan,
                keep_mask,
                dm1,
                x,
                a0,
                q,
                zs,
                y,
                spec,
                flat,
                g0,
                g1,
                g2,
                norms,
                small,
                taps[l],
                spreads,
                forward,
                back,
                tapmap,
                tapback,
                *gathered[2 * l],
            ),
            [SM] * 3 + [VM] * 15 + [HB] * 4 + [HB] * 8,
            (
                whole((pix, width), F32),
                whole((2, 2, 4, 64, SIDE), BF),
                whole((2, 2, 4, 64, SIDE), BF),
                whole((4, 64, 256), BF),
            ),
            [
                pltpu.VMEM((3, 4, 2, 4, 16, SIDE), BF),
                pltpu.VMEM((2 * HALF, pix), BF),
                pltpu.VMEM((pix, 2 * HALF), BF),
                pltpu.VMEM((2 * HALF, 64), BF),
                pltpu.VMEM((64, 2 * HALF), BF),
                pltpu.VMEM((pix, 1024), BF),
                pltpu.VMEM((pix, 1024), BF),
                pltpu.VMEM((HALF, SIDE), F32),
                pltpu.VMEM((64, 1024), BF),
                pltpu.VMEM((32, 16, SIDE), BF),
                pltpu.SemaphoreType.DMA((40,)),
            ],
            6_000_000_000,
            16_000_000,
            "mix_back",
        )
        sums[2 * l] = scatter_pack(keep_a, send_a)
        shared = add(dtaps[0], *[along_z(dtaps[k], k) for k in (1, 2, 3)])
        for perm in (CORE, AXIS_X, AXIS_Y):
            low = shared.astype(BF)
            shared = add(low, along(low, perm))
        kernel_sums[l] = shared
    pieces_a = jnp.stack(sums[0::2])
    pieces_b = jnp.stack(sums[1::2])
    window = pieces_a[:, 48 : 48 + WIN].reshape(layers, WIN * SIDE)
    gated_grad = lax.dynamic_slice(window, (jnp.int32(0), phase), (layers, per))
    vec_grad = lax.dynamic_slice(
        pieces_a[:, 48 + WIN : 48 + WIN + 3], (jnp.int32(0), jnp.int32(0), lane), (layers, 3, 32)
    )
    kernel_grad = jnp.swapaxes(jnp.stack(kernel_sums)[:, :49, :count], 1, 2)
    return (
        result,
        dx,
        vec_grad[:, 0],
        vec_grad[:, 1],
        vec_grad[:, 2],
        jnp.concatenate([pieces_a[:, 0:16], pieces_a[:, 16:32]], axis=2),
        kernel_grad,
        gated_grad,
        pieces_a[:, 32:48],
        jnp.concatenate([pieces_b[:, 16 * b : 16 * b + 16] for b in range(4)], axis=2),
        pieces_b[:, 64:128],
    )


def fits(mesh):
    return dict(mesh.shape) == {"dp": 8, "fsdp": 4}


def layer_norm(values, gain_vec, bias_vec):
    center = values - jnp.mean(values, axis=-1, keepdims=True)
    spread = jnp.mean(center * center, axis=-1, keepdims=True)
    return center * lax.rsqrt(spread + 1e-06) * gain_vec + bias_vec


def branch_factors(layout_plan, keep_row, edge_cells, tile_edge):
    row_ids = jnp.arange(edge_cells, dtype=jnp.int32)[:, None]
    col_ids = jnp.arange(edge_cells, dtype=jnp.int32)[None, :]
    quarter = row_ids // tile_edge * 2 + col_ids // tile_edge
    image_ids = jnp.where(layout_plan[0] == 1, jnp.zeros_like(quarter), quarter)
    occupied = jnp.where(
        layout_plan[0] == 1, jnp.ones_like(quarter), (quarter < layout_plan[1]).astype(jnp.int32)
    )
    onehot = (image_ids.reshape(-1, 1) == jnp.arange(4, dtype=jnp.int32)[None, :]).astype(
        jnp.float32
    )
    keep_table = keep_row.reshape(4, -1).astype(jnp.float32)
    chosen = jnp.dot(onehot, keep_table, precision=lax.Precision.HIGHEST)
    return (image_ids, chosen * occupied.astype(jnp.float32).reshape(-1, 1) * 1.25)


def depthwise(values_in, kernel, image_ids):
    edge_cells = image_ids.shape[0]
    spatial = values_in.reshape(edge_cells, edge_cells, -1)
    padded = jnp.pad(spatial, ((3, 3), (3, 3), (0, 0)))
    padded_ids = jnp.pad(image_ids, 3, constant_values=-1)
    summed = jnp.zeros_like(spatial)
    for offset in range(49):
        row_off = offset // 7
        col_off = offset % 7
        nearby = padded[row_off : row_off + edge_cells, col_off : col_off + edge_cells]
        matched = (
            padded_ids[row_off : row_off + edge_cells, col_off : col_off + edge_cells] == image_ids
        ).astype(jnp.float32)
        summed = summed + nearby * matched[:, :, None] * kernel[:, offset]
    return summed.reshape(values_in.shape) / 3.0


def gated_widths(model_width):
    return [model_width // 16, model_width // 8, model_width // 4, model_width // 2, model_width]


def split_gated(flat_weights, model_width):
    widths = gated_widths(model_width)
    matrices = []
    cursor = 0
    for section_idx in range(4):
        amount = widths[section_idx] * widths[section_idx + 1]
        matrices.append(
            flat_weights[cursor : cursor + amount].reshape(
                widths[section_idx], widths[section_idx + 1]
            )
        )
        cursor = cursor + amount
    return matrices


def outer_sum(left_op, right_op):
    return lax.dot_general(
        left_op, right_op, (((0,), (0,)), ((), ())), preferred_element_type=jnp.float32
    )


def times_transpose(left_op, right_op):
    return lax.dot_general(
        left_op, right_op, (((1,), (1,)), ((), ())), preferred_element_type=jnp.float32
    )


def forward_block(residual, weights, kernel, image_ids, factors):
    in_weight, out_weight, up_weight, down_weight, gated_flat, gain_vec, bias_vec, scale_vec = (
        weights
    )
    model_width = residual.shape[1]
    widths = gated_widths(model_width)
    gain_full = gain_vec.astype(jnp.float32)
    bias_full = bias_vec.astype(jnp.float32)
    scale_full = scale_vec.astype(jnp.float32)
    normed = layer_norm(residual, gain_full[:model_width], bias_full[:model_width]).astype(
        jnp.bfloat16
    )
    mixed_all = jnp.dot(normed, in_weight, preferred_element_type=jnp.float32)
    scaled = depthwise(mixed_all[:, widths[0] :], kernel.astype(jnp.float32), image_ids)
    product = mixed_all[:, : widths[0]] * scaled[:, : widths[0]]
    lowered = []
    inners = []
    cursor = widths[0]
    for section_idx, matrix in enumerate(split_gated(gated_flat, model_width)):
        product_low = product.astype(jnp.bfloat16)
        inner_out = jnp.dot(product_low, matrix, preferred_element_type=jnp.float32)
        lowered.append(product_low)
        inners.append(inner_out)
        product = inner_out * scaled[:, cursor : cursor + widths[section_idx + 1]]
        cursor = cursor + widths[section_idx + 1]
    lowered.append(product.astype(jnp.bfloat16))
    branch = jnp.dot(lowered[4], out_weight, preferred_element_type=jnp.float32)
    middle = residual + factors[:, 0:1] * scale_full[:model_width] * branch
    normed_two = layer_norm(middle, gain_full[model_width:], bias_full[model_width:]).astype(
        jnp.bfloat16
    )
    hidden = jnp.dot(normed_two, up_weight, preferred_element_type=jnp.float32)
    activated = jax.nn.gelu(hidden).astype(jnp.bfloat16)
    expanded = jnp.dot(activated, down_weight, preferred_element_type=jnp.float32)
    output = middle + factors[:, 1:2] * scale_full[model_width:] * expanded
    retained = (
        residual,
        normed,
        mixed_all,
        scaled,
        lowered,
        inners,
        branch,
        middle,
        normed_two,
        hidden,
        activated,
        expanded,
    )
    return (output, retained)


def backward_block(grad_out, retained, weights, kernel, image_ids, factors):
    (
        residual,
        normed,
        mixed_all,
        scaled,
        lowered,
        inners,
        branch,
        middle,
        normed_two,
        hidden,
        activated,
        expanded,
    ) = retained
    in_weight, out_weight, up_weight, down_weight, gated_flat, gain_vec, bias_vec, scale_vec = (
        weights
    )
    model_width = residual.shape[1]
    widths = gated_widths(model_width)
    gain_full = gain_vec.astype(jnp.float32)
    bias_full = bias_vec.astype(jnp.float32)
    scale_full = scale_vec.astype(jnp.float32)
    first_factor = factors[:, 0:1]
    second_factor = factors[:, 1:2]
    scale_two_grad = jnp.sum(grad_out * second_factor * expanded, axis=0)
    expanded_grad = (grad_out * second_factor * scale_full[model_width:]).astype(jnp.bfloat16)
    down_weight_grad = outer_sum(activated, expanded_grad)
    activated_grad = times_transpose(expanded_grad, down_weight)
    unused_gelu, gelu_pull = jax.vjp(jax.nn.gelu, hidden)
    hidden_grad = gelu_pull(activated_grad)[0].astype(jnp.bfloat16)
    up_weight_grad = outer_sum(normed_two, hidden_grad)
    normed_two_grad = times_transpose(hidden_grad, up_weight)
    unused_two, second_pull = jax.vjp(
        layer_norm, middle, gain_full[model_width:], bias_full[model_width:]
    )
    middle_extra, gain_two_grad, bias_two_grad = second_pull(normed_two_grad)
    middle_grad = grad_out + middle_extra
    scale_one_grad = jnp.sum(middle_grad * first_factor * branch, axis=0)
    branch_grad = (middle_grad * first_factor * scale_full[:model_width]).astype(jnp.bfloat16)
    out_weight_grad = outer_sum(lowered[4], branch_grad)
    product_grad = times_transpose(branch_grad, out_weight)
    matrices = split_gated(gated_flat, model_width)
    starts = [0]
    for width_here in widths:
        starts.append(starts[-1] + width_here)
    gated_parts = [None, None, None, None]
    scaled_parts = [None, None, None, None, None]
    for section_idx in reversed(range(4)):
        scaled_part = scaled[:, starts[section_idx + 1] : starts[section_idx + 2]]
        inner_grad = (product_grad * scaled_part).astype(jnp.bfloat16)
        scaled_parts[section_idx + 1] = product_grad * inners[section_idx]
        gated_parts[section_idx] = outer_sum(lowered[section_idx], inner_grad)
        product_grad = times_transpose(inner_grad, matrices[section_idx])
    head_grad = product_grad * scaled[:, : widths[0]]
    scaled_parts[0] = product_grad * mixed_all[:, : widths[0]]
    scaled_grad = jnp.concatenate(scaled_parts, axis=1)
    unused_conv, conv_pull = jax.vjp(
        partial(depthwise, image_ids=image_ids),
        mixed_all[:, widths[0] :],
        kernel.astype(jnp.float32),
    )
    rest_grad, kernel_weight_grad = conv_pull(scaled_grad)
    mixed_grad = jnp.concatenate([head_grad, rest_grad], axis=1).astype(jnp.bfloat16)
    in_weight_grad = outer_sum(normed, mixed_grad)
    normed_grad = times_transpose(mixed_grad, in_weight)
    unused_one, first_pull = jax.vjp(
        layer_norm, residual, gain_full[:model_width], bias_full[:model_width]
    )
    residual_extra, gain_one_grad, bias_one_grad = first_pull(normed_grad)
    input_grad = middle_grad + residual_extra
    gated_grad = jnp.concatenate([matrix_grad.reshape(-1) for matrix_grad in gated_parts])
    weight_grads = (
        in_weight_grad,
        out_weight_grad,
        up_weight_grad,
        down_weight_grad,
        gated_grad,
        jnp.concatenate([gain_one_grad, gain_two_grad]),
        jnp.concatenate([bias_one_grad, bias_two_grad]),
        jnp.concatenate([scale_one_grad, scale_two_grad]),
    )
    return (input_grad, weight_grads, kernel_weight_grad)


def per_device(
    pixels,
    cotangent,
    image_plan,
    keep_mask,
    norm_gains,
    norm_biases,
    layer_scales,
    in_proj,
    depth_kernel,
    gated_weights,
    out_proj,
    up_proj,
    down_proj,
):
    tokens_here = pixels.shape[0]
    edge_cells = math.isqrt(tokens_here)
    tile_edge = edge_cells // 2
    layer_count = in_proj.shape[0]
    image_ids, factors = branch_factors(image_plan[0], keep_mask[0], edge_cells, tile_edge)
    residual = pixels.astype(jnp.float32)
    retained_all = []
    for layer_idx in range(layer_count):
        weights = (
            lax.all_gather(in_proj[layer_idx], ("dp", "fsdp"), axis=0, tiled=True),
            lax.all_gather(out_proj[layer_idx], ("dp", "fsdp"), axis=0, tiled=True),
            lax.all_gather(up_proj[layer_idx], ("dp", "fsdp"), axis=0, tiled=True),
            lax.all_gather(down_proj[layer_idx], ("dp", "fsdp"), axis=0, tiled=True),
            lax.all_gather(gated_weights[layer_idx], ("dp", "fsdp"), axis=0, tiled=True),
            lax.all_gather(norm_gains[layer_idx], ("dp", "fsdp"), axis=0, tiled=True),
            lax.all_gather(norm_biases[layer_idx], ("dp", "fsdp"), axis=0, tiled=True),
            lax.all_gather(layer_scales[layer_idx], ("dp", "fsdp"), axis=0, tiled=True),
        )
        kernel = lax.all_gather(depth_kernel[layer_idx], "fsdp", axis=0, tiled=True)
        residual, retained = forward_block(
            residual, weights, kernel, image_ids, factors[:, 2 * layer_idx : 2 * layer_idx + 2]
        )
        retained_all.append(retained)
    result = residual.astype(jnp.bfloat16)
    grad_now = cotangent.astype(jnp.float32)
    layer_grads = [None] * layer_count
    kernel_grads = [None] * layer_count
    for layer_idx in reversed(range(layer_count)):
        weights = (
            lax.all_gather(in_proj[layer_idx], ("dp", "fsdp"), axis=0, tiled=True),
            lax.all_gather(out_proj[layer_idx], ("dp", "fsdp"), axis=0, tiled=True),
            lax.all_gather(up_proj[layer_idx], ("dp", "fsdp"), axis=0, tiled=True),
            lax.all_gather(down_proj[layer_idx], ("dp", "fsdp"), axis=0, tiled=True),
            lax.all_gather(gated_weights[layer_idx], ("dp", "fsdp"), axis=0, tiled=True),
            lax.all_gather(norm_gains[layer_idx], ("dp", "fsdp"), axis=0, tiled=True),
            lax.all_gather(norm_biases[layer_idx], ("dp", "fsdp"), axis=0, tiled=True),
            lax.all_gather(layer_scales[layer_idx], ("dp", "fsdp"), axis=0, tiled=True),
        )
        kernel = lax.all_gather(depth_kernel[layer_idx], "fsdp", axis=0, tiled=True)
        grad_now, weight_grads, kernel_weight_grad = backward_block(
            grad_now,
            retained_all[layer_idx],
            weights,
            kernel,
            image_ids,
            factors[:, 2 * layer_idx : 2 * layer_idx + 2],
        )
        kernel_grads[layer_idx] = kernel_weight_grad
        layer_grads[layer_idx] = (
            lax.psum_scatter(weight_grads[0], ("dp", "fsdp"), scatter_dimension=0, tiled=True),
            lax.psum_scatter(weight_grads[1], ("dp", "fsdp"), scatter_dimension=0, tiled=True),
            lax.psum_scatter(weight_grads[2], ("dp", "fsdp"), scatter_dimension=0, tiled=True),
            lax.psum_scatter(weight_grads[3], ("dp", "fsdp"), scatter_dimension=0, tiled=True),
            lax.psum_scatter(weight_grads[4], ("dp", "fsdp"), scatter_dimension=0, tiled=True),
            lax.psum_scatter(weight_grads[5], ("dp", "fsdp"), scatter_dimension=0, tiled=True),
            lax.psum_scatter(weight_grads[6], ("dp", "fsdp"), scatter_dimension=0, tiled=True),
            lax.psum_scatter(weight_grads[7], ("dp", "fsdp"), scatter_dimension=0, tiled=True),
        )
    stacked = tuple(
        (
            jnp.stack([layer_grads[layer_idx][member] for layer_idx in range(layer_count)])
            for member in range(8)
        )
    )
    kernel_stack = jnp.stack(kernel_grads)
    kernel_share = lax.psum_scatter(
        kernel_stack.astype(jnp.bfloat16), "fsdp", scatter_dimension=1, tiled=True
    ).astype(jnp.float32)
    kernel_summed = lax.psum(kernel_share, "dp")
    return (
        result,
        grad_now,
        stacked[5],
        stacked[6],
        stacked[7],
        stacked[0],
        kernel_summed,
        stacked[4],
        stacked[1],
        stacked[2],
        stacked[3],
    )


def solution(mesh):
    in_specs = (
        P(("dp", "fsdp"), None),
        P(("dp", "fsdp"), None),
        P(("dp", "fsdp"), None),
        P(("dp", "fsdp"), None),
        P(None, ("dp", "fsdp")),
        P(None, ("dp", "fsdp")),
        P(None, ("dp", "fsdp")),
        P(None, ("dp", "fsdp"), None),
        P(None, "fsdp", None),
        P(None, ("dp", "fsdp")),
        P(None, ("dp", "fsdp"), None),
        P(None, ("dp", "fsdp"), None),
        P(None, ("dp", "fsdp"), None),
    )
    out_specs = (
        P(("dp", "fsdp"), None),
        P(("dp", "fsdp"), None),
        P(None, ("dp", "fsdp")),
        P(None, ("dp", "fsdp")),
        P(None, ("dp", "fsdp")),
        P(None, ("dp", "fsdp"), None),
        P(None, "fsdp", None),
        P(None, ("dp", "fsdp")),
        P(None, ("dp", "fsdp"), None),
        P(None, ("dp", "fsdp"), None),
        P(None, ("dp", "fsdp"), None),
    )
    return jax.shard_map(
        fast_device if fits(mesh) else per_device, mesh=mesh, in_specs=in_specs, out_specs=out_specs, check_vma=False
    )
```

```python
from functools import partial
import math

import jax
import jax.numpy as jnp
import numpy as np
from jax import lax
from jax.experimental import pallas as pl
from jax.experimental.pallas import tpu as pltpu
from jax.sharding import PartitionSpec as P

BF = jnp.bfloat16
F32 = jnp.float32
HALF = 352
SIDE = 512
Z_ORDER = (0, 2, 1, 3)
WIN = 12
VMEM_BYTES = 24 * 1024 * 1024


def half_spectrum(size):
    seen = set()
    kept = []
    for row in range(size):
        for col in range(size):
            if ((-row) % size, (-col) % size) in seen:
                continue
            seen.add((row, col))
            kept.append((row, col))
    return kept


def fourier_tables(edge):
    tile = edge // 2
    plans = [
        [(0, 0, tile), (0, tile, tile), (tile, 0, tile), (tile, tile, tile)],
        [(0, 0, edge)],
    ]
    forward = np.zeros((2, 2 * HALF, edge * edge), np.float32)
    taps = np.zeros((2, 2 * HALF, 64), np.float32)
    for which, tiles in enumerate(plans):
        at = 0
        for top, left, extent in tiles:
            size = extent + 3
            rows, cols = np.meshgrid(np.arange(extent), np.arange(extent), indexing="ij")
            slots = ((rows + top) * edge + cols + left).reshape(-1)
            tap_rows, tap_cols = np.meshgrid(np.arange(7) - 3, np.arange(7) - 3, indexing="ij")
            for fr, fc in half_spectrum(size):
                angle = 2 * np.pi * ((fr * rows + fc * cols) % size) / size
                forward[which, at, slots] = np.cos(angle).reshape(-1)
                forward[which, HALF + at, slots] = np.sin(angle).reshape(-1)
                weight = (1.0 if (fr, fc) == (0, 0) else 2.0) / (3.0 * size * size)
                angle = 2 * np.pi * ((fr * tap_rows + fc * tap_cols) % size) / size
                taps[which, at, :49] = weight * np.cos(angle).reshape(-1)
                taps[which, HALF + at, :49] = weight * np.sin(angle).reshape(-1)
                at += 1
        assert at <= HALF
    return (
        forward,
        np.ascontiguousarray(forward.transpose(0, 2, 1)),
        taps,
        np.ascontiguousarray(taps.transpose(0, 2, 1)),
    )


def mm(left, right):
    return lax.dot_general(left, right, (((1,), (0,)), ((), ())), preferred_element_type=F32)


def mm_nt(left, right):
    return lax.dot_general(left, right, (((1,), (1,)), ((), ())), preferred_element_type=F32)


def mm_tn(left, right):
    return lax.dot_general(left, right, (((0,), (0,)), ((), ())), preferred_element_type=F32)


def iota2(shape, dim):
    return lax.broadcasted_iota(jnp.int32, shape, dim)


def pixel_factor(plan_ref, keep_ref, column, edge, tile):
    slot = iota2((edge * edge, 1), 0)
    row = jnp.floor((slot.astype(F32) + 0.5) * (1.0 / edge)).astype(jnp.int32)
    col = slot - row * edge
    quarter = jnp.where(row >= tile, 2, 0) + jnp.where(col >= tile, 1, 0)
    large = plan_ref[0, 0]
    count = plan_ref[0, 1]
    width = keep_ref.shape[1] // 4
    total = jnp.zeros((edge * edge, 1), F32)
    for t in range(4):
        kept = keep_ref[0, t * width + column].astype(F32) * 1.25
        first = keep_ref[0, column].astype(F32) * 1.25
        here = jnp.where(t < count, kept, 0.0)
        here = jnp.where(large == 1, first, here)
        total = jnp.where(quarter == t, here, total)
    return total


def norm_stats(values):
    center = values - jnp.mean(values, axis=-1, keepdims=True)
    rstd = lax.rsqrt(jnp.mean(center * center, axis=-1, keepdims=True) + 1e-06)
    return center * rstd, rstd


def norm_back(grad, normal, rstd, gain):
    inner = grad * gain
    return rstd * (
        inner
        - jnp.mean(inner, axis=-1, keepdims=True)
        - normal * jnp.mean(inner * normal, axis=-1, keepdims=True)
    )


def window_map(shards, per):
    shape = (HALF, shards * 16)
    r = iota2(shape, 0)
    c = iota2(shape, 1)
    shard = lax.shift_right_logical(c, 4)
    t = c & 15
    flat_row = jnp.where(
        r < 256, r + 84, jnp.where(r < 320, r - 236, jnp.where(r < 336, r - 316, r - 336))
    )
    start = lax.shift_right_logical(shard * (per // 64), 3)
    gated = (t < WIN) & (r < 340) & (flat_row == start + t)
    norm = r - 344
    second = jnp.where(shard >= shards // 2, 1, 0)
    vec = (norm >= 0) & (norm < 6) & (t == WIN + lax.shift_right_arithmetic(norm, 1)) & ((norm & 1) == second)
    return jnp.where(gated | vec, 1.0, 0.0).astype(BF)


def spread(rows, cols, stride, offset, shift):
    r = iota2((rows, cols), 0) - shift
    c = iota2((rows, cols), 1)
    return jnp.where(r == stride * c + offset, 1.0, 0.0).astype(BF)


def lanes_from(values, low, high):
    lane = iota2(values.shape, 1)
    return jnp.where((lane >= low) & (lane < high), values, jnp.zeros_like(values))


def gated_matrices(flat):
    g2 = mm(spread(128, 64, 2, 0, 0), flat[256:320, 0:256]) + mm(
        spread(128, 64, 2, 1, 0), flat[256:320, 256:512]
    )
    g1 = jnp.zeros((128, 128), F32)
    for h in range(4):
        g1 = g1 + mm(spread(128, 16, 4, h, 64), flat[320:336, 128 * h : 128 * h + 128])
    g0 = jnp.zeros((128, 128), F32)
    for t in range(4):
        part = flat[336:352, 128 * t : 128 * t + 128].astype(F32)
        part = jnp.where(iota2(part.shape, 0) < 4, part, 0.0)
        odd = lanes_from(part, 64, 128).astype(BF)
        even = lanes_from(pltpu.roll(part, 64, 1), 64, 128).astype(BF)
        g0 = g0 + mm(spread(128, 16, 8, 2 * t, 32), even) + mm(spread(128, 16, 8, 2 * t + 1, 32), odd)
    return g0.astype(BF), g1.astype(BF), g2.astype(BF)


def matrix(w_ref, row):
    return w_ref[:, :, :, pl.ds(row, 16), :].reshape(SIDE, SIDE)


def down_rows(w_ref, j):
    return w_ref[j, :, :, 64:128, :].reshape(SIDE, SIDE)


def gelu_parts(hidden):
    root = math.sqrt(2.0 / math.pi)
    square = hidden * hidden
    bent = jnp.tanh(root * hidden * (1.0 + 0.044715 * square))
    half = 0.5 * (1.0 + bent)
    value = hidden * half
    slope = half + 0.5 * hidden * (1.0 - bent * bent) * (root * (1.0 + 0.134145 * square))
    return value, slope


def emit_rows(value, rows_ref, keep_ref, send_ref, row, place):
    rows_ref[...] = value.astype(BF).reshape(rows_ref.shape)
    yx = place[0]
    z = place[2]
    for sel, ref in ((0, keep_ref), (1, send_ref)):
        dest = place[1] ^ sel
        first = jnp.where(dest == 0, 1, 2)
        for r1 in range(2):
            for r2 in range(2):
                spot = yx ^ (r1 * first) ^ (r2 * (3 - first))
                for at, zrel in enumerate(Z_ORDER):
                    ref[r1 * 8 + r2 * 4 + at, pl.ds(row, 16), :] = rows_ref[spot * 8 + dest * 4 + (z ^ zrel)]


def mix_forward_kernel(
    layer, edge, per, place, plan, keep, x_ref, taps_ref, w_ref, forward_hbm, back_hbm, tapmap_hbm, *rest
):
    m1_ref, a0_ref, q_ref, z_ref, y_ref, spec_ref, flat_ref, g0_ref, g1_ref, g2_ref, norm_ref = rest[-16:-5]
    forward, back, tapmap, a_low, sems = rest[-5:]
    shards = 32
    mode = plan[0, 0]
    tables = []
    for n, (src, dst) in enumerate(((forward_hbm, forward), (tapmap_hbm, tapmap), (back_hbm, back))):
        tables.append(pltpu.make_async_copy(src.at[mode], dst, sems.at[n]))
        tables[-1].start()
    factor = pixel_factor(plan, keep, 2 * layer, edge, edge // 2)
    picks = window_map(shards, per)
    flat = mm(picks, matrix(w_ref, 48))
    norm_ref[...] = flat[344:352]
    flat_low = flat.astype(BF)
    flat_ref[...] = flat_low
    g0, g1, g2 = gated_matrices(flat_low)
    g0_ref[...] = g0
    g1_ref[...] = g1
    g2_ref[...] = g2
    x = x_ref[...].astype(F32)
    normal, unused = norm_stats(x)
    u = (normal * flat[344:345] + flat[346:347]).astype(BF)
    for half in range(2):
        a = mm(u, matrix(w_ref, 16 * half))
        a_low[:, SIDE * half : SIDE * half + SIDE] = a.astype(BF)
        if half == 0:
            a0_ref[...] = a[:, :128]
    for copy in tables:
        copy.wait()

    def channels(j, carry):
        at = pl.ds(pl.multiple_of(j * 256, 256), 256)
        kernel = mm(tapmap[...], taps_ref[:, at])
        spec = mm(forward[...], a_low[:, at])
        spec_ref[:, at] = spec.astype(BF)
        kr, ki = kernel[:HALF], kernel[HALF:]
        xc, xs = spec[:HALF], spec[HALF:]
        product = jnp.concatenate([xc * kr + xs * ki, xs * kr - xc * ki], axis=0).astype(BF)
        q_ref[:, at] = mm(back[...], product)
        return carry

    lax.fori_loop(0, 4, channels, 0)
    a0 = a0_ref[...]
    q0 = q_ref[:, 0:128]
    p = lanes_from(pltpu.roll(a0, 32, 1) * q0, 32, 64).astype(BF)
    z0 = mm(p, g0)
    z_ref[:, 0:128] = z0
    p = (z0 * q0).astype(BF)
    z1 = mm(p, g1)
    z_ref[:, 128:256] = z1
    p = (z1 * q_ref[:, 128:256]).astype(BF)
    z2 = mm(p, g2)
    z_ref[:, 256:512] = z2
    p = (z2 * q_ref[:, 256:512]).astype(BF)
    z3 = mm(p, flat_ref[0:256, :])
    z_ref[:, 512:1024] = z3
    p = (z3 * q_ref[:, 512:1024]).astype(BF)
    y = mm(p, matrix(w_ref, 32))
    y_ref[...] = y
    m1_ref[...] = x + factor * flat[348:349] * y


def feed_forward_kernel(layer, edge, last, place, plan, keep, m1_ref, norm_ref, w_ref, *rest):
    x_ref, h_ref, f_ref = rest[-3:]
    factor = pixel_factor(plan, keep, 2 * layer + 1, edge, edge // 2)
    m1 = m1_ref[...]
    normal, unused = norm_stats(m1)
    v = (normal * norm_ref[1:2] + norm_ref[3:4]).astype(BF)
    f_ref[...] = jnp.zeros_like(f_ref)

    def hidden(j, carry):
        at = pl.ds(pl.multiple_of(j * SIDE, SIDE), SIDE)
        h = mm(v, matrix(w_ref, pl.multiple_of(j * 16, 16)))
        h_ref[:, at] = h
        e = gelu_parts(h)[0].astype(BF)
        f_ref[...] += mm(e, down_rows(w_ref, j))
        return carry

    lax.fori_loop(0, 4, hidden, 0)
    x_ref[...] = (m1 + factor * norm_ref[5:6] * f_ref[...]).astype(x_ref.dtype)


def feed_back_kernel(layer, edge, place, plan, keep, dx_ref, m1_ref, h_ref, f_ref, norm_ref, w_ref, *rest):
    dm1_ref, keep_out, send_out, small_ref, dv_ref, rows_ref = rest[-6:]
    factor = pixel_factor(plan, keep, 2 * layer + 1, edge, edge // 2)
    dx = dx_ref[...].astype(F32)
    scaled = dx * factor
    small_ref[...] = jnp.zeros_like(small_ref)
    small_ref[5:6] = jnp.sum(scaled * f_ref[...], axis=0, keepdims=True)
    df = (scaled * norm_ref[5:6]).astype(BF)
    normal, rstd = norm_stats(m1_ref[...])
    v = (normal * norm_ref[1:2] + norm_ref[3:4]).astype(BF)
    dv_ref[...] = jnp.zeros_like(dv_ref)
    yx = place[0]
    z = place[2]

    def hidden(j, carry):
        at = pl.ds(pl.multiple_of(j * SIDE, SIDE), SIDE)
        h = h_ref[:, at]
        value, slope = gelu_parts(h)
        e = value.astype(BF)
        dh = (slope * mm_nt(df, down_rows(w_ref, j))).astype(BF)
        dv_ref[...] += mm_nt(dh, matrix(w_ref, pl.multiple_of(j * 16, 16)))
        emit_rows(mm_tn(v, dh), rows_ref, keep_out, send_out, pl.multiple_of(j * 16, 16), place)
        rows_ref[...] = mm_tn(e, df).astype(BF).reshape(rows_ref.shape)
        rel = j ^ yx
        for sel, ref in ((0, keep_out), (1, send_out)):
            dest = place[1] ^ sel
            r1 = jnp.where(dest == 0, rel & 1, rel >> 1)
            r2 = jnp.where(dest == 0, rel >> 1, rel & 1)
            for at, zrel in enumerate(Z_ORDER):
                part = rows_ref[pl.ds((dest * 4 + (z ^ zrel)) * 4, 4)]
                ref[r1 * 8 + r2 * 4 + at, 64:128, :] = part.reshape(64, SIDE)
        return carry

    lax.fori_loop(0, 4, hidden, 0)
    dv = dv_ref[...]
    small_ref[1:2] = jnp.sum(dv * normal, axis=0, keepdims=True)
    small_ref[3:4] = jnp.sum(dv, axis=0, keepdims=True)
    dm1_ref[...] = dx + norm_back(dv, normal, rstd, norm_ref[1:2])


def chain_back_kernel(
    layer,
    edge,
    place,
    plan,
    keep,
    dm1_ref,
    a0_ref,
    q_ref,
    z_ref,
    y_ref,
    flat_ref,
    g0_ref,
    g1_ref,
    g2_ref,
    norm_ref,
    small_ref,
    w_ref,
    *rest,
):
    dq_ref, dhead_ref, dflat_ref, dout_ref = rest[-4:]
    factor = pixel_factor(plan, keep, 2 * layer, edge, edge // 2)
    scaled = dm1_ref[...] * factor
    dscale = jnp.sum(scaled * y_ref[...], axis=0, keepdims=True)
    dy = (scaled * norm_ref[4:5]).astype(BF)
    q4 = q_ref[:, 512:1024]
    z3 = z_ref[:, 512:1024]
    p4 = (z3 * q4).astype(BF)
    dout_ref[...] = mm_tn(p4, dy).astype(BF)
    dp = mm_nt(dy, matrix(w_ref, 32))
    dz = (dp * q4).astype(BF)
    dq_ref[:, 512:1024] = (dp * z3).astype(BF)
    z2 = z_ref[:, 256:512]
    q3 = q_ref[:, 256:512]
    dflat_ref[0:256, :] = mm_tn((z2 * q3).astype(BF), dz).astype(BF)
    dp = mm_nt(dz, flat_ref[0:256, :])
    dz = (dp * q3).astype(BF)
    dq_ref[:, 256:512] = (dp * z2).astype(BF)
    z1 = z_ref[:, 128:256]
    q2 = q_ref[:, 128:256]
    dg2 = mm_tn((z1 * q2).astype(BF), dz).astype(BF)
    for h in range(2):
        dflat_ref[256:320, 256 * h : 256 * h + 256] = mm_tn(spread(128, 64, 2, h, 0), dg2).astype(BF)
    dp = mm_nt(dz, g2_ref[...])
    dz = (dp * q2).astype(BF)
    dq_ref[:, 128:256] = (dp * z1).astype(BF)
    z0 = z_ref[:, 0:128]
    q01 = q_ref[:, 0:128]
    dg1 = mm_tn((z0 * q01).astype(BF), dz).astype(BF)
    for h in range(4):
        dflat_ref[320:336, 128 * h : 128 * h + 128] = mm_tn(spread(128, 16, 4, h, 64), dg1).astype(BF)
    dp = mm_nt(dz, g1_ref[...])
    dz = (dp * q01).astype(BF)
    dq1 = dp * z0
    head = lanes_from(pltpu.roll(a0_ref[...], 32, 1), 32, 64)
    dg0 = mm_tn((head * q01).astype(BF), dz).astype(BF)
    norm_rows = jnp.concatenate(
        [jnp.zeros((8, SIDE), F32), small_ref[0:4], dscale, small_ref[5:8]], axis=0
    )
    for t in range(4):
        even = mm_tn(spread(128, 16, 8, 2 * t, 32), dg0)
        odd = mm_tn(spread(128, 16, 8, 2 * t + 1, 32), dg0)
        at = slice(128 * t, 128 * t + 128)
        dflat_ref[336:352, at] = (
            lanes_from(odd, 64, 128) + pltpu.roll(lanes_from(even, 64, 128), 64, 1) + norm_rows[:, at]
        ).astype(BF)
    dp = mm_nt(dz, g0_ref[...])
    dq_ref[:, 0:128] = (dq1 + dp * head).astype(BF)
    dhead_ref[...] = pltpu.roll(lanes_from(dp * q01, 32, 64), 96, 1)


def spectrum_back_kernel(
    plan, place, spec_ref, dq_ref, dhead_ref, taps_ref, forward_hbm, back_hbm, tapmap_hbm, tapback_hbm, *rest
):
    da_ref, kernel_out, forward, back, tapmap, tapback, dtaps_ref, sems = rest[-8:]
    mode = plan[0, 0]
    tables = []
    for n, (src, dst) in enumerate(
        ((forward_hbm, forward), (back_hbm, back), (tapmap_hbm, tapmap), (tapback_hbm, tapback))
    ):
        tables.append(pltpu.make_async_copy(src.at[mode], dst, sems.at[n]))
        tables[-1].start()
    for copy in tables:
        copy.wait()
    dtaps_ref[:, 1024:] = jnp.zeros((64, 128), F32)

    def channels(j, carry):
        at = pl.ds(pl.multiple_of(j * 256, 256), 256)
        kernel = mm(tapmap[...], taps_ref[:, at])
        grad = mm(forward[...], dq_ref[:, at])
        spec = spec_ref[:, at].astype(F32)
        kr, ki = kernel[:HALF], kernel[HALF:]
        dc, ds = grad[:HALF], grad[HALF:]
        xc, xs = spec[:HALF], spec[HALF:]
        dspec = jnp.concatenate([dc * kr - ds * ki, dc * ki + ds * kr], axis=0).astype(BF)
        da_ref[:, at] = mm(back[...], dspec).astype(BF)
        dkernel = jnp.concatenate([dc * xc + ds * xs, dc * xs - ds * xc], axis=0).astype(BF)
        dtaps_ref[:, at] = mm(tapback[...], dkernel)
        return carry

    lax.fori_loop(0, 4, channels, 0)
    da_ref[:, 0:128] = (da_ref[:, 0:128].astype(F32) + dhead_ref[...]).astype(BF)
    count = (1024 - 32) // 4
    for shard in range(4):
        low = 32 + count * shard
        rel = shard ^ place[2]
        kernel_out[(rel & 1) * 2 + (rel >> 1)] = dtaps_ref[:, low : low + 256].astype(BF)


def mix_back_kernel(per, place, dm1_ref, x_ref, norm_ref, da_ref, dflat_ref, dout_ref, w_ref, *rest):
    dx_ref, keep_out, send_out, rows_ref = rest[-4:]
    emit_rows(dout_ref[...], rows_ref, keep_out, send_out, 32, place)
    normal, rstd = norm_stats(x_ref[...].astype(F32))
    gain = norm_ref[0:1]
    u = (normal * gain + norm_ref[2:3]).astype(BF)
    du = jnp.zeros(dm1_ref.shape, F32)
    for half in range(2):
        da = da_ref[:, SIDE * half : SIDE * half + SIDE]
        emit_rows(mm_tn(u, da), rows_ref, keep_out, send_out, 16 * half, place)
        du = du + mm_nt(da, matrix(w_ref, 16 * half))
    dgain = jnp.sum(du * normal, axis=0, keepdims=True)
    dbias = jnp.sum(du, axis=0, keepdims=True)
    low = dflat_ref[336:352, :].astype(F32)
    row = iota2(low.shape, 0)
    low = jnp.where(row == 8, dgain, jnp.where(row == 10, dbias, low))
    dflat = jnp.concatenate([dflat_ref[0:336, :], low.astype(BF)], axis=0)
    emit_rows(mm_tn(window_map(32, per), dflat), rows_ref, keep_out, send_out, 48, place)
    dx_ref[...] = dm1_ref[...] + norm_back(du, normal, rstd, gain)


def place_lanes(row, lanes, shift):
    pad = jnp.zeros((row.shape[0], lanes - row.shape[1]), F32)
    return pltpu.roll(jnp.concatenate([row.astype(F32), pad], axis=1), shift, 1)


def pack_mix_kernel(layer, place, in_hbm, out_hbm, gated_hbm, gain_hbm, bias_hbm, scale_hbm, taps_hbm, *rest):
    out, gated_ref, gain_ref, bias_ref, scale_ref, taps_ref, sems = rest[-7:]
    pack_ref = out.at[0]
    plans = (
        (gated_hbm, gated_ref),
        (gain_hbm, gain_ref),
        (bias_hbm, bias_ref),
        (scale_hbm, scale_ref),
        (taps_hbm.at[layer], taps_ref),
        (in_hbm.at[layer, :, pl.ds(0, SIDE)], pack_ref.at[pl.ds(0, 16)]),
        (in_hbm.at[layer, :, pl.ds(SIDE, SIDE)], pack_ref.at[pl.ds(16, 16)]),
        (out_hbm.at[layer], pack_ref.at[pl.ds(32, 16)]),
    )
    copies = [pltpu.make_async_copy(src, dst, sems.at[n]) for n, (src, dst) in enumerate(plans)]
    for copy in copies:
        copy.start()
    for copy in copies:
        copy.wait()
    gated = place_lanes(gated_ref[layer : layer + 1, :], WIN * SIDE, place[4])
    rows = [gated[:, SIDE * r : SIDE * r + SIDE] for r in range(WIN)]
    for ref in (gain_ref, bias_ref, scale_ref):
        rows.append(place_lanes(ref[layer : layer + 1, :], SIDE, place[5]))
    rows.append(jnp.zeros((1, SIDE), F32))
    pack_ref[48:64, :] = jnp.concatenate(rows, axis=0).astype(BF)
    pack_ref[64:96, 0:256] = taps_ref[0:32, :]
    pack_ref[64:96, 256:512] = taps_ref[32:64, :]


def pack_feed_kernel(layer, up_hbm, down_hbm, *rest):
    out, sems = rest[-2:]
    pack_ref = out.at[0]
    copies = [
        pltpu.make_async_copy(
            up_hbm.at[layer, :, pl.ds(SIDE * b, SIDE)], pack_ref.at[pl.ds(16 * b, 16)], sems.at[b]
        )
        for b in range(4)
    ]
    copies.append(pltpu.make_async_copy(down_hbm.at[layer], pack_ref.at[pl.ds(64, 64)], sems.at[4]))
    for copy in copies:
        copy.start()
    for copy in copies:
        copy.wait()


def join_kernel(mine, got, *rest):
    out = rest[-1]
    count = mine.shape[0]
    out[:count] = mine[...]
    out[count:] = got[...]


def place_kernel(place, mine, got, *rest):
    out = rest[-1]
    for number, piece in enumerate((mine, got)):
        source = place[1] ^ number
        first = jnp.where(source == 0, 1, 2)
        for at in range(16):
            spot = place[0] ^ (((at >> 2) & 1) * first) ^ ((at >> 3) * (3 - first))
            out[spot, source, place[2] ^ Z_ORDER[at & 3]] = piece[at]


def join_taps_kernel(place, mine, got, *rest):
    out, taps, split, wide = rest[-4:]
    for at, zrel in enumerate(Z_ORDER):
        piece = mine[at] if at < 2 else got[at - 2]
        out[at] = piece[0:64, :]
        split[place[2] ^ zrel] = piece[64:96, :].astype(F32)
    wide[:, 0:128] = jnp.zeros((64, 128), F32)
    count = (1024 - 32) // 4
    for shard in range(4):
        low = 32 + count * shard
        wide[0:32, low : low + count] = split[shard, :, 0:count]
        wide[32:64, low : low + count] = split[shard, :, 256 : 256 + count]
    taps[...] = wide[...].astype(BF)


def step_kernel(kept, got, *rest):
    stay, out = rest[-2:]
    count = out.shape[0]

    def one(n, carry):
        stay[n] = kept[n].astype(F32) + got[n].astype(F32)
        out[n] = (kept[count + n].astype(F32) + got[count + n].astype(F32)).astype(BF)
        return carry

    lax.fori_loop(0, count, one, 0)


def settle_kernel(kept, got, *rest):
    rest[-1][...] = kept[0] + got[0].astype(F32)


def tap_pack_kernel(*refs):
    stay, out = refs[-2:]
    for block in range(stay.shape[1]):
        stay[:, block] = refs[block][0:2]
        out[:, block] = refs[block][2:4]


def tap_halve_kernel(mine, got, *rest):
    stay, out = rest[-2:]
    stay[...] = (mine[0].astype(F32) + got[0].astype(F32)).astype(BF)
    out[...] = (mine[1].astype(F32) + got[1].astype(F32)).astype(BF)


def tap_sum_kernel(mine, got, *rest):
    out = rest[-1]
    out[...] = (mine[...].astype(F32) + got[...].astype(F32)).astype(out.dtype)


def unpack_kernel(layers, place, *rest):
    gain_ref, bias_ref, scale_ref, in_ref, gated_ref, out_ref, up_ref, down_ref = rest[-8:]
    per = gated_ref.shape[1]
    for layer in range(layers):
        mix, feed = rest[2 * layer : 2 * layer + 2]
        in_ref[layer, :, :SIDE] = mix[0:16]
        in_ref[layer, :, SIDE:] = mix[16:32]
        out_ref[layer] = mix[32:48]
        flat = jnp.concatenate([mix[48 + r : 49 + r] for r in range(WIN)], axis=1)
        flat = pltpu.roll(flat, WIN * SIDE - place[4], 1)
        gated_ref[layer : layer + 1, :] = flat[:, :per]
        for n, ref in enumerate((gain_ref, bias_ref, scale_ref)):
            row = pltpu.roll(mix[48 + WIN + n : 49 + WIN + n], SIDE - place[5], 1)
            ref[layer : layer + 1, :] = row[:, : ref.shape[1]]
        for b in range(4):
            up_ref[layer, :, SIDE * b : SIDE * b + SIDE] = feed[16 * b : 16 * b + 16]
        down_ref[layer] = feed[64:128]


def whole(shape, dtype):
    return jax.ShapeDtypeStruct(shape, dtype)


VM = pl.BlockSpec(memory_space=pltpu.VMEM)
SM = pl.BlockSpec(memory_space=pltpu.SMEM)
HB = pl.BlockSpec(memory_space=pltpu.HBM)
ANY = pl.BlockSpec(memory_space=pl.ANY)


SCALE = 1.0
MICROS = {
    "mix_forward": 7.5,
    "feed_forward": 4.5,
    "feed_back": 8.0,
    "chain_back": 3.3,
    "spectrum_back": 5.8,
    "mix_back": 3.0,
}


class Order:
    def __init__(self):
        self.last = ()

    def hold(self, values):
        values = pl.pallas_call(
            lambda *refs: None,
            out_shape=whole(values.shape, values.dtype),
            in_specs=[ANY] * 2,
            out_specs=ANY,
            input_output_aliases={0: 0},
            compiler_params=pltpu.CompilerParams(vmem_limit_bytes=1024 * 1024),
            name="hold",
        )(values, *self.last)
        self.last = (values,)
        return values

    def __call__(self, kernel, ins, in_specs, outs, scratch, name, limit=VMEM_BYTES):
        many = isinstance(outs, tuple)
        results = pl.pallas_call(
            kernel,
            out_shape=outs,
            in_specs=list(in_specs) + [ANY] * len(self.last),
            out_specs=jax.tree.map(lambda unused: VM, outs),
            scratch_shapes=scratch,
            compiler_params=pltpu.CompilerParams(vmem_limit_bytes=limit),
            cost_estimate=pl.CostEstimate(
                flops=int(MICROS.get(name, 0.02) * SCALE * 1e9), bytes_accessed=10_000, transcendentals=0
            ),
            name=name,
        )(*ins, *self.last)
        self.last = (min(results, key=lambda result: result.size * result.dtype.itemsize) if many else results,)
        return results


CORE = [(i, i ^ 1) for i in range(8)]
FIRST = [(i, i ^ (4 if i & 1 else 2)) for i in range(8)]
SECOND = [(i, i ^ (2 if i & 1 else 4)) for i in range(8)]
AXIS_X = [(i, i ^ 2) for i in range(8)]
AXIS_Y = [(i, i ^ 4) for i in range(8)]


def along(values, perm):
    return lax.ppermute(values, "dp", perm)


def along_z(values, k):
    return lax.ppermute(values, "fsdp", [(i, i ^ k) for i in range(4)])


class Gather:
    def __init__(self, order, pack):
        self.order = order
        self.have = pack
        self.come = along_z(pack, 2)

    def join(self):
        shape = (2 * self.have.shape[0], *self.have.shape[1:])
        self.have = self.order(join_kernel, (self.have, self.come), [VM, VM], whole(shape, BF), [], "join")

    def second(self):
        self.join()
        self.come = along_z(self.have, 1)

    def third(self, place=None):
        if place is None:
            self.join()
        else:
            self.have, self.taps = self.order(
                join_taps_kernel,
                (place, self.have, self.come),
                [SM, VM, VM],
                (whole((4, 64, SIDE), BF), whole((64, 1024), BF)),
                [pltpu.VMEM((4, 32, SIDE), F32), pltpu.VMEM((64, 1024), F32)],
                "join_taps",
            )
        self.come = along(self.have, FIRST)

    def fourth(self):
        self.join()
        self.come = along(self.have, SECOND)

    def last(self):
        self.join()
        self.come = along(self.have, CORE)

    def finish(self, place):
        shape = (4, 2, 4, *self.have.shape[1:])
        self.whole = self.order(
            place_kernel, (place, self.have, self.come), [SM, VM, VM], whole(shape, BF), [], "place"
        )


class Scatter:
    def __init__(self, order, keep, send):
        self.order = order
        self.keep = keep
        self.send = send
        self.moves = [
            lambda out: along(out, FIRST),
            lambda out: along(out, SECOND),
            lambda out: along_z(out, 1),
            lambda out: along_z(out, 2),
        ]

    def step(self):
        shape = (self.keep.shape[0] // 2, *self.keep.shape[1:])
        self.keep, out = self.order(
            step_kernel, (self.keep, self.come), [VM, VM], (whole(shape, F32), whole(shape, BF)), [], "step"
        )
        self.come = self.moves.pop(0)(out)

    def start(self):
        self.come = along(self.order.hold(self.send), CORE)

    def settle(self):
        shape = self.keep.shape[1:]
        self.total = self.order(settle_kernel, (self.keep, self.come), [VM, VM], whole(shape, F32), [], "settle")


class TapSum:
    def __init__(self, order, dtaps):
        self.order = order
        shape = whole((2, len(dtaps), *dtaps[0].shape[1:]), BF)
        self.stay, self.out = order(tap_pack_kernel, dtaps, [VM] * len(dtaps), (shape, shape), [], "tap_pack")
        self.come = along_z(self.out, 1)
        self.moves = [
            lambda out: along_z(out, 2),
            lambda out: along(out, CORE),
            lambda out: along(out, AXIS_X),
            lambda out: along(out, AXIS_Y),
        ]

    def step(self):
        halve = len(self.moves) == 4
        shape = whole(self.stay.shape[1:] if halve else self.stay.shape, BF)
        kernel = tap_halve_kernel if halve else tap_sum_kernel
        results = self.order(
            kernel, (self.stay, self.come), [VM, VM], (shape, shape) if halve else shape, [], "tap_sum"
        )
        self.stay, out = results if halve else (results, results)
        self.come = self.moves.pop(0)(out)

    def final(self):
        return self.stay.astype(F32) + self.come.astype(F32)


def fast_device(
    pixels,
    cotangent,
    image_plan,
    keep_mask,
    norm_gains,
    norm_biases,
    layer_scales,
    in_proj,
    depth_kernel,
    gated_weights,
    out_proj,
    up_proj,
    down_proj,
):
    pix, width = pixels.shape
    edge = math.isqrt(pix)
    per = gated_weights.shape[1]
    dp = lax.axis_index("dp")
    z = lax.axis_index("fsdp")
    me = dp * 4 + z
    phase = 64 * ((me * (per // 64)) % 8)
    place = jnp.stack([dp >> 1, dp & 1, z, me, phase, 32 * (me % 16)]).astype(jnp.int32)
    forward, back, tapmap, tapback = [jnp.asarray(t, BF) for t in fourier_tables(edge)]
    count = depth_kernel.shape[1]
    tap_shard = jnp.pad(jnp.swapaxes(depth_kernel, 1, 2), ((0, 0), (0, 15), (0, 256 - count)))
    order = Order()

    def pack_mix(l, limit=VMEM_BYTES):
        pack = order(
            partial(pack_mix_kernel, l),
            (place, in_proj, out_proj, gated_weights, norm_gains, norm_biases, layer_scales, tap_shard),
            [SM] + [HB] * 7,
            whole((1, 96, SIDE), BF),
            [
                pltpu.VMEM(gated_weights.shape, BF),
                pltpu.VMEM(norm_gains.shape, BF),
                pltpu.VMEM(norm_gains.shape, BF),
                pltpu.VMEM(norm_gains.shape, BF),
                pltpu.VMEM((64, 256), BF),
                pltpu.SemaphoreType.DMA((8,)),
            ],
            "pack_mix",
            limit,
        )
        return Gather(order, pack)

    def pack_feed(l):
        pack = order(
            partial(pack_feed_kernel, l),
            (up_proj, down_proj),
            [HB] * 2,
            whole((1, 128, SIDE), BF),
            [pltpu.SemaphoreType.DMA((5,))],
            "pack_feed",
        )
        return Gather(order, pack)

    def mix_forward(l, x, mix):
        return order(
            partial(mix_forward_kernel, l, edge, per),
            (place, image_plan, keep_mask, x, mix.taps, mix.whole, forward, back, tapmap),
            [SM, SM, SM, VM, VM, VM, HB, HB, HB],
            (
                whole((pix, width), F32),
                whole((pix, 128), F32),
                whole((pix, 1024), F32),
                whole((pix, 1024), F32),
                whole((pix, width), F32),
                whole((2 * HALF, 1024), BF),
                whole((HALF, SIDE), BF),
                whole((128, 128), BF),
                whole((128, 128), BF),
                whole((128, 256), BF),
                whole((8, SIDE), F32),
            ),
            [
                pltpu.VMEM((2 * HALF, pix), BF),
                pltpu.VMEM((pix, 2 * HALF), BF),
                pltpu.VMEM((2 * HALF, 64), BF),
                pltpu.VMEM((pix, 1024), BF),
                pltpu.SemaphoreType.DMA((3,)),
            ],
            "mix_forward",
        )

    def feed_forward(l, mixed, feed, last):
        return order(
            partial(feed_forward_kernel, l, edge, last),
            (place, image_plan, keep_mask, mixed[0], mixed[10], feed.whole),
            [SM, SM, SM, VM, VM, VM],
            (
                whole((pix, width), BF if last else F32),
                whole((pix, 4 * SIDE), F32),
                whole((pix, width), F32),
            ),
            [],
            "feed_forward",
        )

    def feed_back(l, dx, mixed, h, f, feed):
        return order(
            partial(feed_back_kernel, l, edge),
            (place, image_plan, keep_mask, dx, mixed[0], h, f, mixed[10], feed.whole),
            [SM, SM, SM, VM, VM, VM, VM, VM, VM],
            (
                whole((pix, width), F32),
                whole((16, 128, SIDE), BF),
                whole((16, 128, SIDE), BF),
                whole((8, SIDE), F32),
            ),
            [pltpu.VMEM((pix, width), F32), pltpu.VMEM((32, 16, SIDE), BF)],
            "feed_back",
        )

    def chain_back(l, dm1, mixed, small, mix):
        m1, a0, q, zs, y, spec, flat, g0, g1, g2, norms = mixed
        return order(
            partial(chain_back_kernel, l, edge),
            (place, image_plan, keep_mask, dm1, a0, q, zs, y, flat, g0, g1, g2, norms, small, mix.whole),
            [SM] * 3 + [VM] * 12,
            (
                whole((pix, 1024), BF),
                whole((pix, 128), F32),
                whole((HALF, SIDE), BF),
                whole((SIDE, SIDE), BF),
            ),
            [],
            "chain_back",
        )

    def spectrum_back(mixed, dq, dhead, mix):
        return order(
            spectrum_back_kernel,
            (image_plan, place, mixed[5], dq, dhead, mix.taps, forward, back, tapmap, tapback),
            [SM] * 2 + [VM] * 4 + [HB] * 4,
            (whole((pix, 1024), BF), whole((4, 64, 256), BF)),
            [
                pltpu.VMEM((2 * HALF, pix), BF),
                pltpu.VMEM((pix, 2 * HALF), BF),
                pltpu.VMEM((2 * HALF, 64), BF),
                pltpu.VMEM((64, 2 * HALF), BF),
                pltpu.VMEM((64, 1024 + 128), F32),
                pltpu.SemaphoreType.DMA((4,)),
            ],
            "spectrum_back",
        )

    def mix_back(dm1, x, mixed, da, dflat, dout, mix):
        return order(
            partial(mix_back_kernel, per),
            (place, dm1, x, mixed[10], da, dflat, dout, mix.whole),
            [SM] + [VM] * 7,
            (whole((pix, width), F32), whole((16, 64, SIDE), BF), whole((16, 64, SIDE), BF)),
            [pltpu.VMEM((32, 16, SIDE), BF)],
            "mix_back",
        )

    mix0 = pack_mix(0, 60 * 1024 * 1024)
    mix0.second()
    feed0 = pack_feed(0)
    mix0.third(place)
    feed0.second()
    mix0.fourth()
    mix1 = pack_mix(1)
    feed0.third()
    mix1.second()
    mix0.last()
    feed1 = pack_feed(1)
    mix0.finish(place)
    mixed0 = mix_forward(0, pixels, mix0)
    feed0.fourth()
    mix1.third(place)
    feed1.second()
    mix1.fourth()
    feed1.third()
    feed0.last()
    feed0.finish(place)
    x1, h0, f0 = feed_forward(0, mixed0, feed0, False)
    mix1.last()
    feed1.fourth()
    mix1.finish(place)
    mixed1 = mix_forward(1, x1, mix1)
    feed1.last()
    feed1.finish(place)
    result, h1, f1 = feed_forward(1, mixed1, feed1, True)

    dm1, keep, send, small = feed_back(1, cotangent, mixed1, h1, f1, feed1)
    sum_feed1 = Scatter(order, keep, send)
    sum_feed1.start()
    dq, dhead, dflat, dout = chain_back(1, dm1, mixed1, small, mix1)
    sum_feed1.step()
    da, dtaps1 = spectrum_back(mixed1, dq, dhead, mix1)
    dx, keep, send = mix_back(dm1, x1, mixed1, da, dflat, dout, mix1)
    sum_mix1 = Scatter(order, keep, send)
    sum_feed1.step()
    sum_mix1.start()
    sum_mix1.step()
    dm1, keep, send, small = feed_back(0, dx, mixed0, h0, f0, feed0)
    sum_feed0 = Scatter(order, keep, send)
    sum_feed1.step()
    sum_mix1.step()
    sum_feed0.start()
    dq, dhead, dflat, dout = chain_back(0, dm1, mixed0, small, mix0)
    sum_feed0.step()
    sum_feed1.step()
    sum_mix1.step()
    da, dtaps0 = spectrum_back(mixed0, dq, dhead, mix0)
    sum_mix1.step()
    sum_feed1.settle()
    taps_sum = TapSum(order, (dtaps0, dtaps1))
    dx, keep, send = mix_back(dm1, pixels, mixed0, da, dflat, dout, mix0)
    sum_mix0 = Scatter(order, keep, send)
    sum_feed0.step()
    sum_mix0.start()
    sum_mix1.settle()
    taps_sum.step()
    sum_mix0.step()
    taps_sum.step()
    sum_feed0.step()
    taps_sum.step()
    sum_mix0.step()
    sum_feed0.step()
    taps_sum.step()
    sum_mix0.step()
    sum_feed0.settle()
    sum_mix0.step()
    sum_mix0.settle()
    terms = [sum_mix0.total, sum_feed0.total, sum_mix1.total, sum_feed1.total]
    gain, bias, scale, in_grad, gated, out_grad, up, down = order(
        partial(unpack_kernel, 2),
        (place, *terms),
        [SM] + [VM] * len(terms),
        tuple(
            whole(ref.shape, F32)
            for ref in (
                norm_gains,
                norm_biases,
                layer_scales,
                in_proj,
                gated_weights,
                out_proj,
                up_proj,
                down_proj,
            )
        ),
        [],
        "unpack",
    )
    taps_grad = jnp.swapaxes(taps_sum.final()[:, :49, :count], 1, 2)
    return (result, dx, gain, bias, scale, in_grad, taps_grad, gated, out_grad, up, down)


def fits(mesh):
    return dict(mesh.shape) == {"dp": 8, "fsdp": 4}


def layer_norm(values, gain_vec, bias_vec):
    center = values - jnp.mean(values, axis=-1, keepdims=True)
    spread = jnp.mean(center * center, axis=-1, keepdims=True)
    return center * lax.rsqrt(spread + 1e-06) * gain_vec + bias_vec


def branch_factors(layout_plan, keep_row, edge_cells, tile_edge):
    row_ids = jnp.arange(edge_cells, dtype=jnp.int32)[:, None]
    col_ids = jnp.arange(edge_cells, dtype=jnp.int32)[None, :]
    quarter = row_ids // tile_edge * 2 + col_ids // tile_edge
    image_ids = jnp.where(layout_plan[0] == 1, jnp.zeros_like(quarter), quarter)
    occupied = jnp.where(
        layout_plan[0] == 1, jnp.ones_like(quarter), (quarter < layout_plan[1]).astype(jnp.int32)
    )
    onehot = (image_ids.reshape(-1, 1) == jnp.arange(4, dtype=jnp.int32)[None, :]).astype(
        jnp.float32
    )
    keep_table = keep_row.reshape(4, -1).astype(jnp.float32)
    chosen = jnp.dot(onehot, keep_table, precision=lax.Precision.HIGHEST)
    return (image_ids, chosen * occupied.astype(jnp.float32).reshape(-1, 1) * 1.25)


def depthwise(values_in, kernel, image_ids):
    edge_cells = image_ids.shape[0]
    spatial = values_in.reshape(edge_cells, edge_cells, -1)
    padded = jnp.pad(spatial, ((3, 3), (3, 3), (0, 0)))
    padded_ids = jnp.pad(image_ids, 3, constant_values=-1)
    summed = jnp.zeros_like(spatial)
    for offset in range(49):
        row_off = offset // 7
        col_off = offset % 7
        nearby = padded[row_off : row_off + edge_cells, col_off : col_off + edge_cells]
        matched = (
            padded_ids[row_off : row_off + edge_cells, col_off : col_off + edge_cells] == image_ids
        ).astype(jnp.float32)
        summed = summed + nearby * matched[:, :, None] * kernel[:, offset]
    return summed.reshape(values_in.shape) / 3.0


def gated_widths(model_width):
    return [model_width // 16, model_width // 8, model_width // 4, model_width // 2, model_width]


def split_gated(flat_weights, model_width):
    widths = gated_widths(model_width)
    matrices = []
    cursor = 0
    for section_idx in range(4):
        amount = widths[section_idx] * widths[section_idx + 1]
        matrices.append(
            flat_weights[cursor : cursor + amount].reshape(
                widths[section_idx], widths[section_idx + 1]
            )
        )
        cursor = cursor + amount
    return matrices


def outer_sum(left_op, right_op):
    return lax.dot_general(
        left_op, right_op, (((0,), (0,)), ((), ())), preferred_element_type=jnp.float32
    )


def times_transpose(left_op, right_op):
    return lax.dot_general(
        left_op, right_op, (((1,), (1,)), ((), ())), preferred_element_type=jnp.float32
    )


def forward_block(residual, weights, kernel, image_ids, factors):
    in_weight, out_weight, up_weight, down_weight, gated_flat, gain_vec, bias_vec, scale_vec = (
        weights
    )
    model_width = residual.shape[1]
    widths = gated_widths(model_width)
    gain_full = gain_vec.astype(jnp.float32)
    bias_full = bias_vec.astype(jnp.float32)
    scale_full = scale_vec.astype(jnp.float32)
    normed = layer_norm(residual, gain_full[:model_width], bias_full[:model_width]).astype(
        jnp.bfloat16
    )
    mixed_all = jnp.dot(normed, in_weight, preferred_element_type=jnp.float32)
    scaled = depthwise(mixed_all[:, widths[0] :], kernel.astype(jnp.float32), image_ids)
    product = mixed_all[:, : widths[0]] * scaled[:, : widths[0]]
    lowered = []
    inners = []
    cursor = widths[0]
    for section_idx, matrix in enumerate(split_gated(gated_flat, model_width)):
        product_low = product.astype(jnp.bfloat16)
        inner_out = jnp.dot(product_low, matrix, preferred_element_type=jnp.float32)
        lowered.append(product_low)
        inners.append(inner_out)
        product = inner_out * scaled[:, cursor : cursor + widths[section_idx + 1]]
        cursor = cursor + widths[section_idx + 1]
    lowered.append(product.astype(jnp.bfloat16))
    branch = jnp.dot(lowered[4], out_weight, preferred_element_type=jnp.float32)
    middle = residual + factors[:, 0:1] * scale_full[:model_width] * branch
    normed_two = layer_norm(middle, gain_full[model_width:], bias_full[model_width:]).astype(
        jnp.bfloat16
    )
    hidden = jnp.dot(normed_two, up_weight, preferred_element_type=jnp.float32)
    activated = jax.nn.gelu(hidden).astype(jnp.bfloat16)
    expanded = jnp.dot(activated, down_weight, preferred_element_type=jnp.float32)
    output = middle + factors[:, 1:2] * scale_full[model_width:] * expanded
    retained = (
        residual,
        normed,
        mixed_all,
        scaled,
        lowered,
        inners,
        branch,
        middle,
        normed_two,
        hidden,
        activated,
        expanded,
    )
    return (output, retained)


def backward_block(grad_out, retained, weights, kernel, image_ids, factors):
    (
        residual,
        normed,
        mixed_all,
        scaled,
        lowered,
        inners,
        branch,
        middle,
        normed_two,
        hidden,
        activated,
        expanded,
    ) = retained
    in_weight, out_weight, up_weight, down_weight, gated_flat, gain_vec, bias_vec, scale_vec = (
        weights
    )
    model_width = residual.shape[1]
    widths = gated_widths(model_width)
    gain_full = gain_vec.astype(jnp.float32)
    bias_full = bias_vec.astype(jnp.float32)
    scale_full = scale_vec.astype(jnp.float32)
    first_factor = factors[:, 0:1]
    second_factor = factors[:, 1:2]
    scale_two_grad = jnp.sum(grad_out * second_factor * expanded, axis=0)
    expanded_grad = (grad_out * second_factor * scale_full[model_width:]).astype(jnp.bfloat16)
    down_weight_grad = outer_sum(activated, expanded_grad)
    activated_grad = times_transpose(expanded_grad, down_weight)
    unused_gelu, gelu_pull = jax.vjp(jax.nn.gelu, hidden)
    hidden_grad = gelu_pull(activated_grad)[0].astype(jnp.bfloat16)
    up_weight_grad = outer_sum(normed_two, hidden_grad)
    normed_two_grad = times_transpose(hidden_grad, up_weight)
    unused_two, second_pull = jax.vjp(
        layer_norm, middle, gain_full[model_width:], bias_full[model_width:]
    )
    middle_extra, gain_two_grad, bias_two_grad = second_pull(normed_two_grad)
    middle_grad = grad_out + middle_extra
    scale_one_grad = jnp.sum(middle_grad * first_factor * branch, axis=0)
    branch_grad = (middle_grad * first_factor * scale_full[:model_width]).astype(jnp.bfloat16)
    out_weight_grad = outer_sum(lowered[4], branch_grad)
    product_grad = times_transpose(branch_grad, out_weight)
    matrices = split_gated(gated_flat, model_width)
    starts = [0]
    for width_here in widths:
        starts.append(starts[-1] + width_here)
    gated_parts = [None, None, None, None]
    scaled_parts = [None, None, None, None, None]
    for section_idx in reversed(range(4)):
        scaled_part = scaled[:, starts[section_idx + 1] : starts[section_idx + 2]]
        inner_grad = (product_grad * scaled_part).astype(jnp.bfloat16)
        scaled_parts[section_idx + 1] = product_grad * inners[section_idx]
        gated_parts[section_idx] = outer_sum(lowered[section_idx], inner_grad)
        product_grad = times_transpose(inner_grad, matrices[section_idx])
    head_grad = product_grad * scaled[:, : widths[0]]
    scaled_parts[0] = product_grad * mixed_all[:, : widths[0]]
    scaled_grad = jnp.concatenate(scaled_parts, axis=1)
    unused_conv, conv_pull = jax.vjp(
        partial(depthwise, image_ids=image_ids),
        mixed_all[:, widths[0] :],
        kernel.astype(jnp.float32),
    )
    rest_grad, kernel_weight_grad = conv_pull(scaled_grad)
    mixed_grad = jnp.concatenate([head_grad, rest_grad], axis=1).astype(jnp.bfloat16)
    in_weight_grad = outer_sum(normed, mixed_grad)
    normed_grad = times_transpose(mixed_grad, in_weight)
    unused_one, first_pull = jax.vjp(
        layer_norm, residual, gain_full[:model_width], bias_full[:model_width]
    )
    residual_extra, gain_one_grad, bias_one_grad = first_pull(normed_grad)
    input_grad = middle_grad + residual_extra
    gated_grad = jnp.concatenate([matrix_grad.reshape(-1) for matrix_grad in gated_parts])
    weight_grads = (
        in_weight_grad,
        out_weight_grad,
        up_weight_grad,
        down_weight_grad,
        gated_grad,
        jnp.concatenate([gain_one_grad, gain_two_grad]),
        jnp.concatenate([bias_one_grad, bias_two_grad]),
        jnp.concatenate([scale_one_grad, scale_two_grad]),
    )
    return (input_grad, weight_grads, kernel_weight_grad)


def per_device(
    pixels,
    cotangent,
    image_plan,
    keep_mask,
    norm_gains,
    norm_biases,
    layer_scales,
    in_proj,
    depth_kernel,
    gated_weights,
    out_proj,
    up_proj,
    down_proj,
):
    tokens_here = pixels.shape[0]
    edge_cells = math.isqrt(tokens_here)
    tile_edge = edge_cells // 2
    layer_count = in_proj.shape[0]
    image_ids, factors = branch_factors(image_plan[0], keep_mask[0], edge_cells, tile_edge)
    residual = pixels.astype(jnp.float32)
    retained_all = []
    for layer_idx in range(layer_count):
        weights = (
            lax.all_gather(in_proj[layer_idx], ("dp", "fsdp"), axis=0, tiled=True),
            lax.all_gather(out_proj[layer_idx], ("dp", "fsdp"), axis=0, tiled=True),
            lax.all_gather(up_proj[layer_idx], ("dp", "fsdp"), axis=0, tiled=True),
            lax.all_gather(down_proj[layer_idx], ("dp", "fsdp"), axis=0, tiled=True),
            lax.all_gather(gated_weights[layer_idx], ("dp", "fsdp"), axis=0, tiled=True),
            lax.all_gather(norm_gains[layer_idx], ("dp", "fsdp"), axis=0, tiled=True),
            lax.all_gather(norm_biases[layer_idx], ("dp", "fsdp"), axis=0, tiled=True),
            lax.all_gather(layer_scales[layer_idx], ("dp", "fsdp"), axis=0, tiled=True),
        )
        kernel = lax.all_gather(depth_kernel[layer_idx], "fsdp", axis=0, tiled=True)
        residual, retained = forward_block(
            residual, weights, kernel, image_ids, factors[:, 2 * layer_idx : 2 * layer_idx + 2]
        )
        retained_all.append(retained)
    result = residual.astype(jnp.bfloat16)
    grad_now = cotangent.astype(jnp.float32)
    layer_grads = [None] * layer_count
    kernel_grads = [None] * layer_count
    for layer_idx in reversed(range(layer_count)):
        weights = (
            lax.all_gather(in_proj[layer_idx], ("dp", "fsdp"), axis=0, tiled=True),
            lax.all_gather(out_proj[layer_idx], ("dp", "fsdp"), axis=0, tiled=True),
            lax.all_gather(up_proj[layer_idx], ("dp", "fsdp"), axis=0, tiled=True),
            lax.all_gather(down_proj[layer_idx], ("dp", "fsdp"), axis=0, tiled=True),
            lax.all_gather(gated_weights[layer_idx], ("dp", "fsdp"), axis=0, tiled=True),
            lax.all_gather(norm_gains[layer_idx], ("dp", "fsdp"), axis=0, tiled=True),
            lax.all_gather(norm_biases[layer_idx], ("dp", "fsdp"), axis=0, tiled=True),
            lax.all_gather(layer_scales[layer_idx], ("dp", "fsdp"), axis=0, tiled=True),
        )
        kernel = lax.all_gather(depth_kernel[layer_idx], "fsdp", axis=0, tiled=True)
        grad_now, weight_grads, kernel_weight_grad = backward_block(
            grad_now,
            retained_all[layer_idx],
            weights,
            kernel,
            image_ids,
            factors[:, 2 * layer_idx : 2 * layer_idx + 2],
        )
        kernel_grads[layer_idx] = kernel_weight_grad
        layer_grads[layer_idx] = (
            lax.psum_scatter(weight_grads[0], ("dp", "fsdp"), scatter_dimension=0, tiled=True),
            lax.psum_scatter(weight_grads[1], ("dp", "fsdp"), scatter_dimension=0, tiled=True),
            lax.psum_scatter(weight_grads[2], ("dp", "fsdp"), scatter_dimension=0, tiled=True),
            lax.psum_scatter(weight_grads[3], ("dp", "fsdp"), scatter_dimension=0, tiled=True),
            lax.psum_scatter(weight_grads[4], ("dp", "fsdp"), scatter_dimension=0, tiled=True),
            lax.psum_scatter(weight_grads[5], ("dp", "fsdp"), scatter_dimension=0, tiled=True),
            lax.psum_scatter(weight_grads[6], ("dp", "fsdp"), scatter_dimension=0, tiled=True),
            lax.psum_scatter(weight_grads[7], ("dp", "fsdp"), scatter_dimension=0, tiled=True),
        )
    stacked = tuple(
        (
            jnp.stack([layer_grads[layer_idx][member] for layer_idx in range(layer_count)])
            for member in range(8)
        )
    )
    kernel_stack = jnp.stack(kernel_grads)
    kernel_share = lax.psum_scatter(
        kernel_stack.astype(jnp.bfloat16), "fsdp", scatter_dimension=1, tiled=True
    ).astype(jnp.float32)
    kernel_summed = lax.psum(kernel_share, "dp")
    return (
        result,
        grad_now,
        stacked[5],
        stacked[6],
        stacked[7],
        stacked[0],
        kernel_summed,
        stacked[4],
        stacked[1],
        stacked[2],
        stacked[3],
    )


def solution(mesh):
    in_specs = (
        P(("dp", "fsdp"), None),
        P(("dp", "fsdp"), None),
        P(("dp", "fsdp"), None),
        P(("dp", "fsdp"), None),
        P(None, ("dp", "fsdp")),
        P(None, ("dp", "fsdp")),
        P(None, ("dp", "fsdp")),
        P(None, ("dp", "fsdp"), None),
        P(None, "fsdp", None),
        P(None, ("dp", "fsdp")),
        P(None, ("dp", "fsdp"), None),
        P(None, ("dp", "fsdp"), None),
        P(None, ("dp", "fsdp"), None),
    )
    out_specs = (
        P(("dp", "fsdp"), None),
        P(("dp", "fsdp"), None),
        P(None, ("dp", "fsdp")),
        P(None, ("dp", "fsdp")),
        P(None, ("dp", "fsdp")),
        P(None, ("dp", "fsdp"), None),
        P(None, "fsdp", None),
        P(None, ("dp", "fsdp")),
        P(None, ("dp", "fsdp"), None),
        P(None, ("dp", "fsdp"), None),
        P(None, ("dp", "fsdp"), None),
    )
    return jax.shard_map(
        fast_device if fits(mesh) else per_device, mesh=mesh, in_specs=in_specs, out_specs=out_specs, check_vma=False
    )
```

```python
from functools import partial
import math

import jax
import jax.numpy as jnp
import numpy as np
from jax import lax
from jax.experimental import pallas as pl
from jax.experimental.pallas import tpu as pltpu
from jax.sharding import PartitionSpec as P

BF = jnp.bfloat16
F32 = jnp.float32
HALF = 352
SIDE = 512
Z_ORDER = (0, 2, 1, 3)
WIN = 12
VMEM_BYTES = 24 * 1024 * 1024


def half_spectrum(size):
    seen = set()
    kept = []
    for row in range(size):
        for col in range(size):
            if ((-row) % size, (-col) % size) in seen:
                continue
            seen.add((row, col))
            kept.append((row, col))
    return kept


def fourier_tables(edge):
    tile = edge // 2
    plans = [
        [(0, 0, tile), (0, tile, tile), (tile, 0, tile), (tile, tile, tile)],
        [(0, 0, edge)],
    ]
    forward = np.zeros((2, 2 * HALF, edge * edge), np.float32)
    taps = np.zeros((2, 2 * HALF, 64), np.float32)
    for which, tiles in enumerate(plans):
        at = 0
        for top, left, extent in tiles:
            size = extent + 3
            rows, cols = np.meshgrid(np.arange(extent), np.arange(extent), indexing="ij")
            slots = ((rows + top) * edge + cols + left).reshape(-1)
            tap_rows, tap_cols = np.meshgrid(np.arange(7) - 3, np.arange(7) - 3, indexing="ij")
            for fr, fc in half_spectrum(size):
                angle = 2 * np.pi * ((fr * rows + fc * cols) % size) / size
                forward[which, at, slots] = np.cos(angle).reshape(-1)
                forward[which, HALF + at, slots] = np.sin(angle).reshape(-1)
                weight = (1.0 if (fr, fc) == (0, 0) else 2.0) / (3.0 * size * size)
                angle = 2 * np.pi * ((fr * tap_rows + fc * tap_cols) % size) / size
                taps[which, at, :49] = weight * np.cos(angle).reshape(-1)
                taps[which, HALF + at, :49] = weight * np.sin(angle).reshape(-1)
                at += 1
        assert at <= HALF
    return (
        forward,
        np.ascontiguousarray(forward.transpose(0, 2, 1)),
        taps,
        np.ascontiguousarray(taps.transpose(0, 2, 1)),
    )


def mm(left, right):
    return lax.dot_general(left, right, (((1,), (0,)), ((), ())), preferred_element_type=F32)


def mm_nt(left, right):
    return lax.dot_general(left, right, (((1,), (1,)), ((), ())), preferred_element_type=F32)


def mm_tn(left, right):
    return lax.dot_general(left, right, (((0,), (0,)), ((), ())), preferred_element_type=F32)


def iota2(shape, dim):
    return lax.broadcasted_iota(jnp.int32, shape, dim)


def pixel_factor(plan_ref, keep_ref, column, edge, tile):
    slot = iota2((edge * edge, 1), 0)
    row = jnp.floor((slot.astype(F32) + 0.5) * (1.0 / edge)).astype(jnp.int32)
    col = slot - row * edge
    quarter = jnp.where(row >= tile, 2, 0) + jnp.where(col >= tile, 1, 0)
    large = plan_ref[0, 0]
    count = plan_ref[0, 1]
    width = keep_ref.shape[1] // 4
    total = jnp.zeros((edge * edge, 1), F32)
    for t in range(4):
        kept = keep_ref[0, t * width + column].astype(F32) * 1.25
        first = keep_ref[0, column].astype(F32) * 1.25
        here = jnp.where(t < count, kept, 0.0)
        here = jnp.where(large == 1, first, here)
        total = jnp.where(quarter == t, here, total)
    return total


def norm_stats(values):
    center = values - jnp.mean(values, axis=-1, keepdims=True)
    rstd = lax.rsqrt(jnp.mean(center * center, axis=-1, keepdims=True) + 1e-06)
    return center * rstd, rstd


def norm_back(grad, normal, rstd, gain):
    inner = grad * gain
    return rstd * (
        inner
        - jnp.mean(inner, axis=-1, keepdims=True)
        - normal * jnp.mean(inner * normal, axis=-1, keepdims=True)
    )


def window_map(shards, per):
    shape = (HALF, shards * 16)
    r = iota2(shape, 0)
    c = iota2(shape, 1)
    shard = lax.shift_right_logical(c, 4)
    t = c & 15
    flat_row = jnp.where(
        r < 256, r + 84, jnp.where(r < 320, r - 236, jnp.where(r < 336, r - 316, r - 336))
    )
    start = lax.shift_right_logical(shard * (per // 64), 3)
    gated = (t < WIN) & (r < 340) & (flat_row == start + t)
    norm = r - 344
    second = jnp.where(shard >= shards // 2, 1, 0)
    vec = (norm >= 0) & (norm < 6) & (t == WIN + lax.shift_right_arithmetic(norm, 1)) & ((norm & 1) == second)
    return jnp.where(gated | vec, 1.0, 0.0).astype(BF)


def spread(rows, cols, stride, offset, shift, count=None):
    r = iota2((rows, cols), 0) - shift
    c = iota2((rows, cols), 1)
    hit = r == stride * c + offset
    if count is not None:
        hit = hit & (c < count)
    return jnp.where(hit, 1.0, 0.0).astype(BF)


def lanes_from(values, low, high):
    lane = iota2(values.shape, 1)
    return jnp.where((lane >= low) & (lane < high), values, jnp.zeros_like(values))


def gated_matrices(flat):
    g2 = mm(spread(128, 64, 2, 0, 0), flat[256:320, 0:256]) + mm(
        spread(128, 64, 2, 1, 0), flat[256:320, 256:512]
    )
    g1 = jnp.zeros((128, 128), F32)
    for h in range(4):
        g1 = g1 + mm(spread(128, 16, 4, h, 64), flat[320:336, 128 * h : 128 * h + 128])
    g0 = jnp.zeros((128, 128), F32)
    for t in range(4):
        part = flat[336:352, 128 * t : 128 * t + 128].astype(F32)
        part = jnp.where(iota2(part.shape, 0) < 4, part, 0.0)
        odd = lanes_from(part, 64, 128).astype(BF)
        even = lanes_from(pltpu.roll(part, 64, 1), 64, 128).astype(BF)
        g0 = g0 + mm(spread(128, 16, 8, 2 * t, 32), even) + mm(spread(128, 16, 8, 2 * t + 1, 32), odd)
    return g0.astype(BF), g1.astype(BF), g2.astype(BF)


def matrix(w_ref, row):
    return w_ref[:, :, :, pl.ds(row, 16), :].reshape(SIDE, SIDE)


def down_rows(w_ref, j):
    return w_ref[j, :, :, 64:128, :].reshape(SIDE, SIDE)


def gelu_parts(hidden):
    root = math.sqrt(2.0 / math.pi)
    square = hidden * hidden
    bent = jnp.tanh(root * hidden * (1.0 + 0.044715 * square))
    half = 0.5 * (1.0 + bent)
    value = hidden * half
    slope = half + 0.5 * hidden * (1.0 - bent * bent) * (root * (1.0 + 0.134145 * square))
    return value, slope


def emit_block(read, outs, rows, place):
    yx = place[0]
    z = place[2]
    for sel in range(2):
        dest = place[1] ^ sel
        first = jnp.where(dest == 0, 1, 2)
        for r1 in range(2):
            for r2 in range(2):
                spot = yx ^ (r1 * first) ^ (r2 * (3 - first))
                for at, zrel in enumerate(Z_ORDER):
                    values = read(spot, dest, z ^ zrel)
                    outs[sel][r1 * 8 + r2 * 4 + at, rows, :] = values


def emit_rows(value, rows_ref, outs, row, place):
    rows_ref[...] = value.astype(BF).reshape(rows_ref.shape)
    emit_block(lambda spot, core, z: rows_ref[spot * 8 + core * 4 + z], outs, pl.ds(row, 16), place)


def tables_kernel(plan, *rest):
    mode = plan[0, 0]
    sources, targets, sems = rest[:4], rest[-5:-1], rest[-1]
    copies = [
        pltpu.make_async_copy(src.at[mode], dst, sems.at[n]) for n, (src, dst) in enumerate(zip(sources, targets))
    ]
    for copy in copies:
        copy.start()
    for copy in copies:
        copy.wait()


def mix_forward_kernel(
    layer, edge, per, plan, keep, x_ref, taps_ref, w_ref, forward, back, tapmap, *rest
):
    m1_ref, a0_ref, q_ref, z_ref, p_ref, y_ref, spec_ref, kern_ref, flat_ref, g0_ref, g1_ref, g2_ref, norm_ref = rest[
        -14:-1
    ]
    a_low = rest[-1]
    shards = 32
    factor = pixel_factor(plan, keep, 2 * layer, edge, edge // 2)
    picks = window_map(shards, per)
    flat = mm(picks, matrix(w_ref, 48))
    norm_ref[...] = flat[344:352]
    flat_low = flat.astype(BF)
    flat_ref[...] = flat_low
    g0, g1, g2 = gated_matrices(flat_low)
    g0_ref[...] = g0
    g1_ref[...] = g1
    g2_ref[...] = g2
    x = x_ref[...].astype(F32)
    normal, unused = norm_stats(x)
    u = (normal * flat[344:345] + flat[346:347]).astype(BF)
    for half in range(2):
        a = mm(u, matrix(w_ref, 16 * half))
        a_low[:, SIDE * half : SIDE * half + SIDE] = a.astype(BF)
        if half == 0:
            a0_ref[...] = a[:, :128]

    def channels(j):
        at = slice(j * SIDE, j * SIDE + SIDE)
        kernel = mm(tapmap[...], taps_ref[:, at])
        kern_ref[:, at] = kernel.astype(BF)
        spec = mm(forward[...], a_low[:, at])
        spec_ref[:, at] = spec.astype(BF)
        kr, ki = kernel[:HALF], kernel[HALF:]
        xc, xs = spec[:HALF], spec[HALF:]
        product = jnp.concatenate([xc * kr + xs * ki, xs * kr - xc * ki], axis=0).astype(BF)
        q_ref[:, at] = mm(back[...], product).astype(BF)

    for j in range(2):
        channels(j)
    q0 = q_ref[:, 0:128].astype(F32)
    p0 = lanes_from(pltpu.roll(a0_ref[...], 32, 1) * q0, 32, 64)
    z = mm(p0.astype(BF), g0)
    z_ref[:, 0:128] = z.astype(BF)
    p = z * q0
    p_ref[:, 0:128] = (p0 + p).astype(BF)
    z = mm(p.astype(BF), g1)
    z_ref[:, 128:256] = z.astype(BF)
    p = (z * q_ref[:, 128:256].astype(F32)).astype(BF)
    p_ref[:, 128:256] = p
    z = mm(p, g2)
    z_ref[:, 256:512] = z.astype(BF)
    p = (z * q_ref[:, 256:512].astype(F32)).astype(BF)
    p_ref[:, 256:512] = p
    z = mm(p, flat_ref[0:256, :])
    z_ref[:, 512:1024] = z.astype(BF)
    p = (z * q_ref[:, 512:1024].astype(F32)).astype(BF)
    p_ref[:, 512:1024] = p
    y = mm(p, matrix(w_ref, 32))
    y_ref[...] = y.astype(BF)
    m1_ref[...] = x + factor * flat[348:349] * y


def feed_forward_kernel(layer, edge, last, plan, keep, m1_ref, norm_ref, w_ref, *rest):
    x_ref, e_ref, slope_ref, f_ref, total = rest[-5:]
    factor = pixel_factor(plan, keep, 2 * layer + 1, edge, edge // 2)
    m1 = m1_ref[...]
    normal, unused = norm_stats(m1)
    v = (normal * norm_ref[1:2] + norm_ref[3:4]).astype(BF)
    total[...] = jnp.zeros_like(total)

    def hidden(j):
        at = slice(j * SIDE, j * SIDE + SIDE)
        value, slope = gelu_parts(mm(v, matrix(w_ref, j * 16)))
        e = value.astype(BF)
        e_ref[:, at] = e
        slope_ref[:, at] = slope.astype(BF)
        total[...] += mm(e, down_rows(w_ref, j))

    for j in range(4):
        hidden(j)
    f_ref[...] = total[...].astype(BF)
    x_ref[...] = (m1 + factor * norm_ref[5:6] * total[...]).astype(x_ref.dtype)


def feed_back_kernel(
    layer, edge, place, plan, keep, dx_ref, m1_ref, e_ref, slope_ref, f_ref, norm_ref, w_ref, *rest
):
    dm1_ref, *outs, small_ref, dv_ref, rows_ref, down_ref = rest[-7:]
    factor = pixel_factor(plan, keep, 2 * layer + 1, edge, edge // 2)
    dx = dx_ref[...].astype(F32)
    scaled = dx * factor
    small_ref[...] = jnp.zeros_like(small_ref)
    small_ref[5:6] = jnp.sum(scaled * f_ref[...].astype(F32), axis=0, keepdims=True)
    df = (scaled * norm_ref[5:6]).astype(BF)
    normal, rstd = norm_stats(m1_ref[...])
    v = (normal * norm_ref[1:2] + norm_ref[3:4]).astype(BF)
    dv_ref[...] = jnp.zeros_like(dv_ref)

    def hidden(j):
        at = slice(j * SIDE, j * SIDE + SIDE)
        e = e_ref[:, at]
        dh = (slope_ref[:, at].astype(F32) * mm_nt(df, down_rows(w_ref, j))).astype(BF)
        dv_ref[...] += mm_nt(dh, matrix(w_ref, j * 16))
        emit_rows(mm_tn(v, dh), rows_ref, outs, j * 16, place)
        down_ref[j] = mm_tn(e, df).astype(BF).reshape(down_ref.shape[1:])

    for j in range(4):
        hidden(j)
    emit_block(lambda spot, core, z: down_ref[spot, core, z], outs, slice(64, 128), place)
    dv = dv_ref[...]
    small_ref[1:2] = jnp.sum(dv * normal, axis=0, keepdims=True)
    small_ref[3:4] = jnp.sum(dv, axis=0, keepdims=True)
    dm1_ref[...] = dx + norm_back(dv, normal, rstd, norm_ref[1:2])


def chain_back_kernel(
    layer,
    edge,
    plan,
    keep,
    dm1_ref,
    a0_ref,
    q_ref,
    z_ref,
    p_ref,
    y_ref,
    flat_ref,
    g0_ref,
    g1_ref,
    g2_ref,
    norm_ref,
    small_ref,
    w_ref,
    *rest,
):
    dq_ref, dhead_ref, dflat_ref, dout_ref = rest[-4:]
    factor = pixel_factor(plan, keep, 2 * layer, edge, edge // 2)
    scaled = dm1_ref[...] * factor
    dscale = jnp.sum(scaled * y_ref[...].astype(F32), axis=0, keepdims=True)
    dy = (scaled * norm_ref[4:5]).astype(BF)
    dout_ref[...] = mm_tn(p_ref[:, 512:1024], dy).astype(BF)

    def link(dp, low, high):
        dz = (dp * q_ref[:, low:high].astype(F32)).astype(BF)
        return dz, dp * z_ref[:, low:high].astype(F32)

    dp = mm_nt(dy, matrix(w_ref, 32))
    dz, dq = link(dp, 512, 1024)
    dq_ref[:, 512:1024] = dq.astype(BF)
    dflat_ref[0:256, :] = mm_tn(p_ref[:, 256:512], dz).astype(BF)
    dp = mm_nt(dz, flat_ref[0:256, :])
    dz, dq = link(dp, 256, 512)
    dq_ref[:, 256:512] = dq.astype(BF)
    dg2 = mm_tn(p_ref[:, 128:256], dz).astype(BF)
    for h in range(2):
        dflat_ref[256:320, 256 * h : 256 * h + 256] = mm_tn(spread(128, 64, 2, h, 0), dg2).astype(BF)
    dp = mm_nt(dz, g2_ref[...])
    dz, dq = link(dp, 128, 256)
    dq_ref[:, 128:256] = dq.astype(BF)
    p01 = p_ref[:, 0:128]
    dg1 = mm_tn(p01, dz).astype(BF)
    for h in range(4):
        dflat_ref[320:336, 128 * h : 128 * h + 128] = mm_tn(spread(128, 16, 4, h, 64), dg1).astype(BF)
    dp = mm_nt(dz, g1_ref[...])
    dz, dq1 = link(dp, 0, 128)
    dg0 = mm_tn(p01, dz).astype(BF)
    norm_rows = jnp.concatenate(
        [jnp.zeros((8, SIDE), F32), small_ref[0:4], dscale, small_ref[5:8]], axis=0
    )
    for t in range(4):
        even = mm_tn(spread(128, 16, 8, 2 * t, 32, 4), dg0)
        odd = mm_tn(spread(128, 16, 8, 2 * t + 1, 32, 4), dg0)
        at = slice(128 * t, 128 * t + 128)
        dflat_ref[336:352, at] = (
            lanes_from(odd, 64, 128) + pltpu.roll(lanes_from(even, 64, 128), 64, 1) + norm_rows[:, at]
        ).astype(BF)
    dp = mm_nt(dz, g0_ref[...])
    head = lanes_from(pltpu.roll(a0_ref[...], 32, 1), 32, 64)
    dq_ref[:, 0:128] = (dq1 + dp * head).astype(BF)
    dhead_ref[...] = pltpu.roll(lanes_from(dp * q_ref[:, 0:128].astype(F32), 32, 64), 96, 1)


def spectrum_back_kernel(place, spec_ref, kern_ref, dq_ref, dhead_ref, forward, back, tapback, *rest):
    da_ref, kernel_out, dtaps_ref = rest[-3:]
    dtaps_ref[:, 1024:] = jnp.zeros((64, 128), F32)

    def channels(j):
        at = slice(j * SIDE, j * SIDE + SIDE)
        kernel = kern_ref[:, at].astype(F32)
        grad = mm(forward[...], dq_ref[:, at])
        spec = spec_ref[:, at].astype(F32)
        kr, ki = kernel[:HALF], kernel[HALF:]
        dc, ds = grad[:HALF], grad[HALF:]
        xc, xs = spec[:HALF], spec[HALF:]
        dspec = jnp.concatenate([dc * kr - ds * ki, dc * ki + ds * kr], axis=0).astype(BF)
        da_ref[:, at] = mm(back[...], dspec).astype(BF)
        dkernel = jnp.concatenate([dc * xc + ds * xs, dc * xs - ds * xc], axis=0).astype(BF)
        dtaps_ref[:, at] = mm(tapback[...], dkernel)

    for j in range(2):
        channels(j)
    da_ref[:, 0:128] = (da_ref[:, 0:128].astype(F32) + dhead_ref[...]).astype(BF)
    count = (1024 - 32) // 4
    for shard in range(4):
        low = 32 + count * shard
        rel = shard ^ place[2]
        at = (rel & 1) * 2 + (rel >> 1)
        kernel_out[at, :, 0:256] = dtaps_ref[0:32, low : low + 256].astype(BF)
        kernel_out[at, :, 256:512] = dtaps_ref[32:64, low : low + 256].astype(BF)


def mix_back_kernel(per, place, dm1_ref, x_ref, norm_ref, da_ref, dflat_ref, dout_ref, w_ref, *rest):
    dx_ref, *outs, rows_ref = rest[-4:]
    emit_rows(dout_ref[...], rows_ref, outs, 32, place)
    normal, rstd = norm_stats(x_ref[...].astype(F32))
    gain = norm_ref[0:1]
    u = (normal * gain + norm_ref[2:3]).astype(BF)
    du = jnp.zeros(dm1_ref.shape, F32)
    for half in range(2):
        da = da_ref[:, SIDE * half : SIDE * half + SIDE]
        emit_rows(mm_tn(u, da), rows_ref, outs, 16 * half, place)
        du = du + mm_nt(da, matrix(w_ref, 16 * half))
    dgain = jnp.sum(du * normal, axis=0, keepdims=True)
    dbias = jnp.sum(du, axis=0, keepdims=True)
    low = dflat_ref[336:352, :].astype(F32)
    row = iota2(low.shape, 0)
    low = jnp.where(row == 8, dgain, jnp.where(row == 10, dbias, low))
    dflat = jnp.concatenate([dflat_ref[0:336, :], low.astype(BF)], axis=0)
    emit_rows(mm_tn(window_map(32, per), dflat), rows_ref, outs, 48, place)
    dx_ref[...] = dm1_ref[...] + norm_back(du, normal, rstd, gain)


def place_lanes(row, lanes, shift):
    pad = jnp.zeros((row.shape[0], lanes - row.shape[1]), F32)
    return pltpu.roll(jnp.concatenate([row.astype(F32), pad], axis=1), shift, 1)


def pack_mix_kernel(layer, place, in_hbm, out_hbm, gated_hbm, gain_hbm, bias_hbm, scale_hbm, taps_hbm, *rest):
    out, gated_ref, gain_ref, bias_ref, scale_ref, taps_ref, sems = rest[-7:]
    pack_ref = out.at[0]
    plans = (
        (gated_hbm, gated_ref),
        (gain_hbm, gain_ref),
        (bias_hbm, bias_ref),
        (scale_hbm, scale_ref),
        (taps_hbm.at[layer], taps_ref),
        (in_hbm.at[layer, :, pl.ds(0, SIDE)], pack_ref.at[pl.ds(0, 16)]),
        (in_hbm.at[layer, :, pl.ds(SIDE, SIDE)], pack_ref.at[pl.ds(16, 16)]),
        (out_hbm.at[layer], pack_ref.at[pl.ds(32, 16)]),
    )
    copies = [pltpu.make_async_copy(src, dst, sems.at[n]) for n, (src, dst) in enumerate(plans)]
    for copy in copies:
        copy.start()
    for copy in copies:
        copy.wait()
    gated = place_lanes(gated_ref[layer : layer + 1, :], WIN * SIDE, place[4])
    rows = [gated[:, SIDE * r : SIDE * r + SIDE] for r in range(WIN)]
    for ref in (gain_ref, bias_ref, scale_ref):
        rows.append(place_lanes(ref[layer : layer + 1, :], SIDE, place[5]))
    rows.append(jnp.zeros((1, SIDE), F32))
    pack_ref[48:64, :] = jnp.concatenate(rows, axis=0).astype(BF)
    pack_ref[64:96, 0:256] = taps_ref[0:32, :]
    pack_ref[64:96, 256:512] = taps_ref[32:64, :]


def pack_feed_copies(layer, up_hbm, down_hbm, pack_ref, row, sems):
    copies = [
        pltpu.make_async_copy(
            up_hbm.at[layer, :, pl.ds(SIDE * b, SIDE)], pack_ref.at[pl.ds(row + 16 * b, 16)], sems.at[b]
        )
        for b in range(4)
    ]
    copies.append(pltpu.make_async_copy(down_hbm.at[layer], pack_ref.at[pl.ds(row + 64, 64)], sems.at[4]))
    return copies


def pack_feed_kernel(layer, up_hbm, down_hbm, *rest):
    out, sems = rest[-2:]
    copies = pack_feed_copies(layer, up_hbm, down_hbm, out.at[0], 0, sems)
    for copy in copies:
        copy.start()
    for copy in copies:
        copy.wait()


def pack_both_kernel(
    layer, place, in_hbm, out_hbm, gated_hbm, gain_hbm, bias_hbm, scale_hbm, taps_hbm, up_hbm, down_hbm, *rest
):
    out, sems = rest[-8], rest[-1]
    copies = pack_feed_copies(layer, up_hbm, down_hbm, out.at[0], 96, sems)
    for copy in copies:
        copy.start()
    pack_mix_kernel(
        layer, place, in_hbm, out_hbm, gated_hbm, gain_hbm, bias_hbm, scale_hbm, taps_hbm, *rest[-8:-1]
    )
    for copy in copies:
        copy.wait()


def join_wide(split, wide, taps):
    wide[:, 0:128] = jnp.zeros((64, 128), F32)
    count = (1024 - 32) // 4
    for shard in range(4):
        low = 32 + count * shard
        wide[0:32, low : low + count] = split[shard, :, 0:count]
        wide[32:64, low : low + count] = split[shard, :, 256 : 256 + count]
    taps[...] = wide[...].astype(BF)


def split_kernel(place, mine, got, *rest):
    mix, feed, taps, split, wide = rest[-5:]
    for at, zrel in enumerate(Z_ORDER):
        piece = mine[at] if at < 2 else got[at - 2]
        mix[at] = piece[0:64, :]
        split[place[2] ^ zrel] = piece[64:96, :].astype(F32)
        feed[at] = piece[96:224, :]
    join_wide(split, wide, taps)


def join_kernel(mine, got, *rest):
    out = rest[-1]
    count = mine.shape[0]
    out[:count] = mine[...]
    out[count:] = got[...]


def place_kernel(place, mine, got, other_a, other_b, other_c, *rest):
    out = rest[-1]
    for number, pieces in enumerate(((mine, got), (other_a, other_b, other_c))):
        source = place[1] ^ number
        first = jnp.where(source == 0, 1, 2)
        at = 0
        for piece in pieces:
            for n in range(piece.shape[0]):
                spot = place[0] ^ (((at >> 2) & 1) * first) ^ ((at >> 3) * (3 - first))
                out[spot, source, place[2] ^ Z_ORDER[at & 3]] = piece[n]
                at += 1


def join_taps_kernel(place, mine, got, *rest):
    out, taps, split, wide = rest[-4:]
    for at, zrel in enumerate(Z_ORDER):
        piece = mine[at] if at < 2 else got[at - 2]
        out[at] = piece[0:64, :]
        split[place[2] ^ zrel] = piece[64:96, :].astype(F32)
    join_wide(split, wide, taps)


def step_kernel(kept, got, *rest):
    stay, out = rest[-2:]
    count = out.shape[0]

    def one(n, carry):
        stay[n] = kept[n].astype(F32) + got[n].astype(F32)
        out[n] = (kept[count + n].astype(F32) + got[count + n].astype(F32)).astype(BF)
        return carry

    lax.fori_loop(0, count, one, 0)


def settle_kernel(kept, got, *rest):
    rest[-1][...] = kept[0] + got[0].astype(F32)


def tap_pack_kernel(*refs):
    stay, out = refs[-2:]
    for block in range(stay.shape[1]):
        stay[:, block] = refs[block][0:2]
        out[:, block] = refs[block][2:4]


def tap_halve_kernel(mine, got, *rest):
    stay, out = rest[-2:]
    stay[...] = (mine[0].astype(F32) + got[0].astype(F32)).astype(BF)
    out[...] = (mine[1].astype(F32) + got[1].astype(F32)).astype(BF)


def tap_sum_kernel(mine, got, *rest):
    out = rest[-1]
    out[...] = (mine[...].astype(F32) + got[...].astype(F32)).astype(out.dtype)


def unpack_kernel(layers, place, *rest):
    gain_ref, bias_ref, scale_ref, in_ref, gated_ref, out_ref, up_ref, down_ref = rest[-8:]
    per = gated_ref.shape[1]
    for layer in range(layers):
        mix, feed = rest[2 * layer : 2 * layer + 2]
        in_ref[layer, :, :SIDE] = mix[0:16]
        in_ref[layer, :, SIDE:] = mix[16:32]
        out_ref[layer] = mix[32:48]
        flat = jnp.concatenate([mix[48 + r : 49 + r] for r in range(WIN)], axis=1)
        flat = pltpu.roll(flat, WIN * SIDE - place[4], 1)
        gated_ref[layer : layer + 1, :] = flat[:, :per]
        for n, ref in enumerate((gain_ref, bias_ref, scale_ref)):
            row = pltpu.roll(mix[48 + WIN + n : 49 + WIN + n], SIDE - place[5], 1)
            ref[layer : layer + 1, :] = row[:, : ref.shape[1]]
        for b in range(4):
            up_ref[layer, :, SIDE * b : SIDE * b + SIDE] = feed[16 * b : 16 * b + 16]
        down_ref[layer] = feed[64:128]


def whole(shape, dtype):
    return jax.ShapeDtypeStruct(shape, dtype)


VM = pl.BlockSpec(memory_space=pltpu.VMEM)
SM = pl.BlockSpec(memory_space=pltpu.SMEM)
HB = pl.BlockSpec(memory_space=pltpu.HBM)
ANY = pl.BlockSpec(memory_space=pl.ANY)


FORWARD_ORDER = (
    "a01", "a02", "b01", "a03", "b02", "a04", "c11", "b03", "T", "c12", "b04", "mf0",
    "c13", "a14", "ff0", "b14", "mf1", "ff1",
)
BACKWARD_ORDER = (
    "fb1", "B10", "cb1", "B11", "sb1", "mb1", "A10", "fb0", "B12", "A11", "B00", "cb0",
    "B01", "sb0", "B13", "A12", "mb0", "A00", "B14", "t0", "A13", "B02", "A01", "t1",
    "A14", "B03", "A02", "t2", "B04", "A03", "t3", "B15", "A15", "A04", "t4", "B05",
    "A05",
)
SCALE = 1.0
SMALL = 20.0
MICROS = {
    "mix_forward": 7.5,
    "feed_forward": 4.5,
    "feed_back": 8.0,
    "chain_back": 3.3,
    "spectrum_back": 5.8,
    "mix_back": 3.0,
}


EVENT_MICROS = {}


class Order:
    def __init__(self):
        self.last = ()
        self.event = None

    def cost(self, name):
        micros = EVENT_MICROS.get(self.event, MICROS.get(name, SMALL) * SCALE)
        return pl.CostEstimate(flops=int(micros * 1e9), bytes_accessed=10_000, transcendentals=0)

    def hold(self, values):
        values = pl.pallas_call(
            lambda *refs: None,
            out_shape=tuple(whole(value.shape, value.dtype) for value in values),
            in_specs=[ANY] * (len(values) + 1),
            out_specs=(ANY,) * len(values),
            input_output_aliases={n: n for n in range(len(values))},
            compiler_params=pltpu.CompilerParams(vmem_limit_bytes=1024 * 1024),
            cost_estimate=self.cost("hold"),
            name="hold",
        )(*values, *self.last)
        self.last = (values[0],)
        return values

    def __call__(self, kernel, ins, in_specs, outs, scratch, name, limit=VMEM_BYTES):
        many = isinstance(outs, tuple)
        results = pl.pallas_call(
            kernel,
            out_shape=outs,
            in_specs=list(in_specs) + [ANY] * len(self.last),
            out_specs=jax.tree.map(lambda unused: VM, outs),
            scratch_shapes=scratch,
            compiler_params=pltpu.CompilerParams(vmem_limit_bytes=limit),
            cost_estimate=self.cost(name),
            name=name,
        )(*ins, *self.last)
        self.last = (min(results, key=lambda result: result.size * result.dtype.itemsize) if many else results,)
        return results


CORE = [(i, i ^ 1) for i in range(8)]
FIRST = [(i, i ^ (4 if i & 1 else 2)) for i in range(8)]
SECOND = [(i, i ^ (2 if i & 1 else 4)) for i in range(8)]
AXIS_X = [(i, i ^ 2) for i in range(8)]
AXIS_Y = [(i, i ^ 4) for i in range(8)]


def along(values, perm):
    return lax.ppermute(values, "dp", perm)


def along_z(values, k):
    return lax.ppermute(values, "fsdp", [(i, i ^ k) for i in range(4)])


class Gather:
    def __init__(self, order, pack):
        self.order = order
        self.have = pack
        self.come = None if pack is None else along_z(pack, 2)

    def join(self):
        shape = (2 * self.have.shape[0], *self.have.shape[1:])
        self.have = self.order(join_kernel, (self.have, self.come), [VM, VM], whole(shape, BF), [], "join")

    def second(self):
        self.join()
        self.come = along_z(self.have, 1)

    def third(self, place=None):
        if place is None:
            self.join()
        else:
            self.have, self.taps = self.order(
                join_taps_kernel,
                (place, self.have, self.come),
                [SM, VM, VM],
                (whole((4, 64, SIDE), BF), whole((64, 1024), BF)),
                [pltpu.VMEM((4, 32, SIDE), F32), pltpu.VMEM((64, 1024), F32)],
                "join_taps",
            )
        self.first_axis()

    def first_axis(self):
        self.come = along(self.have, FIRST)
        self.other = [along(self.have, CORE)]

    def fourth(self):
        self.other.append(along(self.come, CORE))
        self.join()
        self.come = along(self.have, SECOND)
        self.other.append(along(self.come, CORE))

    def finish(self, place):
        shape = (4, 2, 4, *self.have.shape[1:])
        self.whole = self.order(
            place_kernel, (place, self.have, self.come, *self.other), [SM] + [VM] * 5, whole(shape, BF), [], "place"
        )


def split(order, place, both):
    mix, feed = Gather(order, None), Gather(order, None)
    mix.have, feed.have, mix.taps = order(
        split_kernel,
        (place, both.have, both.come),
        [SM, VM, VM],
        (whole((4, 64, SIDE), BF), whole((4, 128, SIDE), BF), whole((64, 1024), BF)),
        [pltpu.VMEM((4, 32, SIDE), F32), pltpu.VMEM((64, 1024), F32)],
        "split",
    )
    mix.first_axis()
    feed.first_axis()
    return mix, feed


class Scatter:
    def __init__(self, order, keep, send):
        self.order = order
        self.keep = keep
        self.send = send
        self.moves = [
            lambda out: along(out, FIRST),
            lambda out: along(out, SECOND),
            lambda out: along_z(out, 1),
            lambda out: along_z(out, 2),
        ]

    def step(self):
        shape = (self.keep.shape[0] // 2, *self.keep.shape[1:])
        self.keep, out = self.order(
            step_kernel,
            (self.keep, self.come),
            [VM] * 2,
            (whole(shape, F32), whole(shape, BF)),
            [],
            "step",
        )
        self.come = self.moves.pop(0)(out)

    def start(self):
        (self.come,) = [along(part, CORE) for part in self.order.hold(self.send)]

    def settle(self):
        shape = self.keep.shape[1:]
        self.total = self.order(settle_kernel, (self.keep, self.come), [VM, VM], whole(shape, F32), [], "settle")


class TapSum:
    def __init__(self, order, dtaps):
        self.order = order
        shape = whole((2, len(dtaps), *dtaps[0].shape[1:]), BF)
        self.stay, self.out = order(tap_pack_kernel, dtaps, [VM] * len(dtaps), (shape, shape), [], "tap_pack")
        self.come = along_z(self.out, 1)
        self.moves = [
            lambda out: along_z(out, 2),
            lambda out: along(out, CORE),
            lambda out: along(out, AXIS_X),
            lambda out: along(out, AXIS_Y),
        ]

    def step(self):
        halve = len(self.moves) == 4
        shape = whole(self.stay.shape[1:] if halve else self.stay.shape, BF)
        kernel = tap_halve_kernel if halve else tap_sum_kernel
        results = self.order(
            kernel, (self.stay, self.come), [VM, VM], (shape, shape) if halve else shape, [], "tap_sum"
        )
        self.stay, out = results if halve else (results, results)
        self.come = self.moves.pop(0)(out)

    def final(self):
        return self.stay.astype(F32) + self.come.astype(F32)


def fast_device(
    pixels,
    cotangent,
    image_plan,
    keep_mask,
    norm_gains,
    norm_biases,
    layer_scales,
    in_proj,
    depth_kernel,
    gated_weights,
    out_proj,
    up_proj,
    down_proj,
):
    pix, width = pixels.shape
    edge = math.isqrt(pix)
    per = gated_weights.shape[1]
    dp = lax.axis_index("dp")
    z = lax.axis_index("fsdp")
    me = dp * 4 + z
    phase = 64 * ((me * (per // 64)) % 8)
    place = jnp.stack([dp >> 1, dp & 1, z, me, phase, 32 * (me % 16)]).astype(jnp.int32)
    tables = [jnp.asarray(t, BF) for t in fourier_tables(edge)]
    count = depth_kernel.shape[1]
    tap_shard = jnp.pad(jnp.swapaxes(depth_kernel, 1, 2), ((0, 0), (0, 15), (0, 256 - count)))
    order = Order()

    def pack_mix(l, limit=VMEM_BYTES):
        pack = order(
            partial(pack_mix_kernel, l),
            (place, in_proj, out_proj, gated_weights, norm_gains, norm_biases, layer_scales, tap_shard),
            [SM] + [HB] * 7,
            whole((1, 96, SIDE), BF),
            [
                pltpu.VMEM(gated_weights.shape, BF),
                pltpu.VMEM(norm_gains.shape, BF),
                pltpu.VMEM(norm_gains.shape, BF),
                pltpu.VMEM(norm_gains.shape, BF),
                pltpu.VMEM((64, 256), BF),
                pltpu.SemaphoreType.DMA((8,)),
            ],
            "pack_mix",
            limit,
        )
        return Gather(order, pack)

    def pack_both(l):
        pack = order(
            partial(pack_both_kernel, l),
            (
                place,
                in_proj,
                out_proj,
                gated_weights,
                norm_gains,
                norm_biases,
                layer_scales,
                tap_shard,
                up_proj,
                down_proj,
            ),
            [SM] + [HB] * 9,
            whole((1, 224, SIDE), BF),
            [
                pltpu.VMEM(gated_weights.shape, BF),
                pltpu.VMEM(norm_gains.shape, BF),
                pltpu.VMEM(norm_gains.shape, BF),
                pltpu.VMEM(norm_gains.shape, BF),
                pltpu.VMEM((64, 256), BF),
                pltpu.SemaphoreType.DMA((8,)),
                pltpu.SemaphoreType.DMA((5,)),
            ],
            "pack_both",
        )
        return Gather(order, pack)

    def pack_feed(l):
        pack = order(
            partial(pack_feed_kernel, l),
            (up_proj, down_proj),
            [HB] * 2,
            whole((1, 128, SIDE), BF),
            [pltpu.SemaphoreType.DMA((5,))],
            "pack_feed",
        )
        return Gather(order, pack)

    def mix_forward(l, x, mix):
        return order(
            partial(mix_forward_kernel, l, edge, per),
            (image_plan, keep_mask, x, mix.taps, mix.whole, *state["tables"][:3]),
            [SM, SM] + [VM] * 6,
            (
                whole((pix, width), F32),
                whole((pix, 128), F32),
                whole((pix, 1024), BF),
                whole((pix, 1024), BF),
                whole((pix, 1024), BF),
                whole((pix, width), BF),
                whole((2 * HALF, 1024), BF),
                whole((2 * HALF, 1024), BF),
                whole((HALF, SIDE), BF),
                whole((128, 128), BF),
                whole((128, 128), BF),
                whole((128, 256), BF),
                whole((8, SIDE), F32),
            ),
            [pltpu.VMEM((pix, 1024), BF)],
            "mix_forward",
        )

    def feed_forward(l, mixed, feed, last):
        return order(
            partial(feed_forward_kernel, l, edge, last),
            (image_plan, keep_mask, mixed[0], mixed[12], feed.whole),
            [SM, SM] + [VM] * 3,
            (
                whole((pix, width), BF if last else F32),
                whole((pix, 4 * SIDE), BF),
                whole((pix, 4 * SIDE), BF),
                whole((pix, width), BF),
            ),
            [pltpu.VMEM((pix, width), F32)],
            "feed_forward",
        )

    def feed_back(l, dx, mixed, fed, feed):
        return order(
            partial(feed_back_kernel, l, edge),
            (place, image_plan, keep_mask, dx, mixed[0], *fed[1:], mixed[12], feed.whole),
            [SM] * 3 + [VM] * 7,
            (
                whole((pix, width), F32),
                whole((16, 128, SIDE), BF),
                whole((16, 128, SIDE), BF),
                whole((8, SIDE), F32),
            ),
            [
                pltpu.VMEM((pix, width), F32),
                pltpu.VMEM((32, 16, SIDE), BF),
                pltpu.VMEM((4, 2, 4, 64, SIDE), BF),
            ],
            "feed_back",
        )

    def chain_back(l, dm1, mixed, small, mix):
        m1, a0, q, zs, ps, y, spec, kern, flat, g0, g1, g2, norms = mixed
        return order(
            partial(chain_back_kernel, l, edge),
            (image_plan, keep_mask, dm1, a0, q, zs, ps, y, flat, g0, g1, g2, norms, small, mix.whole),
            [SM] * 2 + [VM] * 13,
            (
                whole((pix, 1024), BF),
                whole((pix, 128), F32),
                whole((HALF, SIDE), BF),
                whole((SIDE, SIDE), BF),
            ),
            [],
            "chain_back",
        )

    def spectrum_back(mixed, dq, dhead):
        return order(
            spectrum_back_kernel,
            (place, mixed[6], mixed[7], dq, dhead, *state["tables"][:2], state["tables"][3]),
            [SM] + [VM] * 7,
            (whole((pix, 1024), BF), whole((4, 32, SIDE), BF)),
            [pltpu.VMEM((64, 1024 + 128), F32)],
            "spectrum_back",
        )

    def mix_back(dm1, x, mixed, da, dflat, dout, mix):
        return order(
            partial(mix_back_kernel, per),
            (place, dm1, x, mixed[12], da, dflat, dout, mix.whole),
            [SM] + [VM] * 7,
            (whole((pix, width), F32), whole((16, 64, SIDE), BF), whole((16, 64, SIDE), BF)),
            [pltpu.VMEM((32, 16, SIDE), BF)],
            "mix_back",
        )

    state = {"x0": pixels, "dx2": cotangent}

    def load_tables():
        state["tables"] = order(
            tables_kernel,
            (image_plan, *tables),
            [SM] + [HB] * 4,
            tuple(whole(table.shape[1:], BF) for table in tables),
            [pltpu.SemaphoreType.DMA((4,))],
            "tables",
        )

    def pack(name):
        state[name] = {
            "a0": partial(pack_mix, 0, 60 * 1024 * 1024),
            "b0": partial(pack_feed, 0),
            "c1": partial(pack_both, 1),
        }[name]()

    def gather(name, step):
        chain = state[name]
        if name == "c1" and step == 3:
            state["a1"], state["b1"] = split(order, place, chain)
        elif step == 3:
            chain.third(place if name == "a0" else None)
        else:
            (chain.second, None, chain.fourth)[step - 2]()

    def forward_mix(l):
        mix = state[f"a{l}"]
        mix.finish(place)
        state[f"mixed{l}"] = mix_forward(l, state[f"x{l}"], mix)

    def forward_feed(l):
        feed = state[f"b{l}"]
        feed.finish(place)
        state[f"fed{l}"] = feed_forward(l, state[f"mixed{l}"], feed, l == 1)
        state[f"x{l + 1}"] = state[f"fed{l}"][0]

    def backward_feed(l):
        state["dm"], keep, *send, state["small"] = feed_back(
            l, state[f"dx{l + 1}"], state[f"mixed{l}"], state[f"fed{l}"], state[f"b{l}"]
        )
        state[f"feedsum{l}"] = Scatter(order, keep, send)

    def backward_chain(l):
        state["chain"] = chain_back(l, state["dm"], state[f"mixed{l}"], state["small"], state[f"a{l}"])

    def backward_spectrum(l):
        dq, dhead, dflat, dout = state["chain"]
        state["da"], state[f"dtaps{l}"] = spectrum_back(state[f"mixed{l}"], dq, dhead)

    def backward_mix(l):
        dq, dhead, dflat, dout = state["chain"]
        state[f"dx{l}"], keep, *send = mix_back(
            state["dm"], state[f"x{l}"], state[f"mixed{l}"], state["da"], dflat, dout, state[f"a{l}"]
        )
        state[f"mixsum{l}"] = Scatter(order, keep, send)

    def scatter(l, mix, step):
        chain = state[f"mixsum{l}" if mix else f"feedsum{l}"]
        if step == 0:
            chain.start()
        elif step == 5:
            chain.settle()
        else:
            chain.step()

    def sum_taps(step):
        if step == 0:
            state["taps"] = TapSum(order, (state["dtaps0"], state["dtaps1"]))
        else:
            state["taps"].step()

    events = {"T": load_tables}
    for name in ("a0", "b0", "c1"):
        events[name + "1"] = partial(pack, name)
    for name in ("a0", "b0", "c1", "a1", "b1"):
        for step in range(2, 5):
            events[f"{name}{step}"] = partial(gather, name, step)
    for l in range(2):
        for step in range(6):
            events[f"A{l}{step}"] = partial(scatter, l, True, step)
            events[f"B{l}{step}"] = partial(scatter, l, False, step)
        events[f"mf{l}"] = partial(forward_mix, l)
        events[f"ff{l}"] = partial(forward_feed, l)
        events[f"fb{l}"] = partial(backward_feed, l)
        events[f"cb{l}"] = partial(backward_chain, l)
        events[f"sb{l}"] = partial(backward_spectrum, l)
        events[f"mb{l}"] = partial(backward_mix, l)
    for step in range(5):
        events[f"t{step}"] = partial(sum_taps, step)
    for name in FORWARD_ORDER + BACKWARD_ORDER:
        order.event = name
        events[name]()
    terms = [state[f"{name}sum{l}"].total for l in range(2) for name in ("mix", "feed")]
    result, dx = state["x2"], state["dx0"]
    gain, bias, scale, in_grad, gated, out_grad, up, down = order(
        partial(unpack_kernel, 2),
        (place, *terms),
        [SM] + [VM] * len(terms),
        tuple(
            whole(ref.shape, F32)
            for ref in (
                norm_gains,
                norm_biases,
                layer_scales,
                in_proj,
                gated_weights,
                out_proj,
                up_proj,
                down_proj,
            )
        ),
        [],
        "unpack",
    )
    taps_grad = state["taps"].final()
    taps_grad = jnp.concatenate([taps_grad[..., :count], taps_grad[..., 256 : 256 + count]], axis=1)
    taps_grad = jnp.swapaxes(taps_grad[:, :49], 1, 2)
    return (result, dx, gain, bias, scale, in_grad, taps_grad, gated, out_grad, up, down)


def fits(mesh):
    return dict(mesh.shape) == {"dp": 8, "fsdp": 4}


def layer_norm(values, gain_vec, bias_vec):
    center = values - jnp.mean(values, axis=-1, keepdims=True)
    spread = jnp.mean(center * center, axis=-1, keepdims=True)
    return center * lax.rsqrt(spread + 1e-06) * gain_vec + bias_vec


def branch_factors(layout_plan, keep_row, edge_cells, tile_edge):
    row_ids = jnp.arange(edge_cells, dtype=jnp.int32)[:, None]
    col_ids = jnp.arange(edge_cells, dtype=jnp.int32)[None, :]
    quarter = row_ids // tile_edge * 2 + col_ids // tile_edge
    image_ids = jnp.where(layout_plan[0] == 1, jnp.zeros_like(quarter), quarter)
    occupied = jnp.where(
        layout_plan[0] == 1, jnp.ones_like(quarter), (quarter < layout_plan[1]).astype(jnp.int32)
    )
    onehot = (image_ids.reshape(-1, 1) == jnp.arange(4, dtype=jnp.int32)[None, :]).astype(
        jnp.float32
    )
    keep_table = keep_row.reshape(4, -1).astype(jnp.float32)
    chosen = jnp.dot(onehot, keep_table, precision=lax.Precision.HIGHEST)
    return (image_ids, chosen * occupied.astype(jnp.float32).reshape(-1, 1) * 1.25)


def depthwise(values_in, kernel, image_ids):
    edge_cells = image_ids.shape[0]
    spatial = values_in.reshape(edge_cells, edge_cells, -1)
    padded = jnp.pad(spatial, ((3, 3), (3, 3), (0, 0)))
    padded_ids = jnp.pad(image_ids, 3, constant_values=-1)
    summed = jnp.zeros_like(spatial)
    for offset in range(49):
        row_off = offset // 7
        col_off = offset % 7
        nearby = padded[row_off : row_off + edge_cells, col_off : col_off + edge_cells]
        matched = (
            padded_ids[row_off : row_off + edge_cells, col_off : col_off + edge_cells] == image_ids
        ).astype(jnp.float32)
        summed = summed + nearby * matched[:, :, None] * kernel[:, offset]
    return summed.reshape(values_in.shape) / 3.0


def gated_widths(model_width):
    return [model_width // 16, model_width // 8, model_width // 4, model_width // 2, model_width]


def split_gated(flat_weights, model_width):
    widths = gated_widths(model_width)
    matrices = []
    cursor = 0
    for section_idx in range(4):
        amount = widths[section_idx] * widths[section_idx + 1]
        matrices.append(
            flat_weights[cursor : cursor + amount].reshape(
                widths[section_idx], widths[section_idx + 1]
            )
        )
        cursor = cursor + amount
    return matrices


def outer_sum(left_op, right_op):
    return lax.dot_general(
        left_op, right_op, (((0,), (0,)), ((), ())), preferred_element_type=jnp.float32
    )


def times_transpose(left_op, right_op):
    return lax.dot_general(
        left_op, right_op, (((1,), (1,)), ((), ())), preferred_element_type=jnp.float32
    )


def forward_block(residual, weights, kernel, image_ids, factors):
    in_weight, out_weight, up_weight, down_weight, gated_flat, gain_vec, bias_vec, scale_vec = (
        weights
    )
    model_width = residual.shape[1]
    widths = gated_widths(model_width)
    gain_full = gain_vec.astype(jnp.float32)
    bias_full = bias_vec.astype(jnp.float32)
    scale_full = scale_vec.astype(jnp.float32)
    normed = layer_norm(residual, gain_full[:model_width], bias_full[:model_width]).astype(
        jnp.bfloat16
    )
    mixed_all = jnp.dot(normed, in_weight, preferred_element_type=jnp.float32)
    scaled = depthwise(mixed_all[:, widths[0] :], kernel.astype(jnp.float32), image_ids)
    product = mixed_all[:, : widths[0]] * scaled[:, : widths[0]]
    lowered = []
    inners = []
    cursor = widths[0]
    for section_idx, matrix in enumerate(split_gated(gated_flat, model_width)):
        product_low = product.astype(jnp.bfloat16)
        inner_out = jnp.dot(product_low, matrix, preferred_element_type=jnp.float32)
        lowered.append(product_low)
        inners.append(inner_out)
        product = inner_out * scaled[:, cursor : cursor + widths[section_idx + 1]]
        cursor = cursor + widths[section_idx + 1]
    lowered.append(product.astype(jnp.bfloat16))
    branch = jnp.dot(lowered[4], out_weight, preferred_element_type=jnp.float32)
    middle = residual + factors[:, 0:1] * scale_full[:model_width] * branch
    normed_two = layer_norm(middle, gain_full[model_width:], bias_full[model_width:]).astype(
        jnp.bfloat16
    )
    hidden = jnp.dot(normed_two, up_weight, preferred_element_type=jnp.float32)
    activated = jax.nn.gelu(hidden).astype(jnp.bfloat16)
    expanded = jnp.dot(activated, down_weight, preferred_element_type=jnp.float32)
    output = middle + factors[:, 1:2] * scale_full[model_width:] * expanded
    retained = (
        residual,
        normed,
        mixed_all,
        scaled,
        lowered,
        inners,
        branch,
        middle,
        normed_two,
        hidden,
        activated,
        expanded,
    )
    return (output, retained)


def backward_block(grad_out, retained, weights, kernel, image_ids, factors):
    (
        residual,
        normed,
        mixed_all,
        scaled,
        lowered,
        inners,
        branch,
        middle,
        normed_two,
        hidden,
        activated,
        expanded,
    ) = retained
    in_weight, out_weight, up_weight, down_weight, gated_flat, gain_vec, bias_vec, scale_vec = (
        weights
    )
    model_width = residual.shape[1]
    widths = gated_widths(model_width)
    gain_full = gain_vec.astype(jnp.float32)
    bias_full = bias_vec.astype(jnp.float32)
    scale_full = scale_vec.astype(jnp.float32)
    first_factor = factors[:, 0:1]
    second_factor = factors[:, 1:2]
    scale_two_grad = jnp.sum(grad_out * second_factor * expanded, axis=0)
    expanded_grad = (grad_out * second_factor * scale_full[model_width:]).astype(jnp.bfloat16)
    down_weight_grad = outer_sum(activated, expanded_grad)
    activated_grad = times_transpose(expanded_grad, down_weight)
    unused_gelu, gelu_pull = jax.vjp(jax.nn.gelu, hidden)
    hidden_grad = gelu_pull(activated_grad)[0].astype(jnp.bfloat16)
    up_weight_grad = outer_sum(normed_two, hidden_grad)
    normed_two_grad = times_transpose(hidden_grad, up_weight)
    unused_two, second_pull = jax.vjp(
        layer_norm, middle, gain_full[model_width:], bias_full[model_width:]
    )
    middle_extra, gain_two_grad, bias_two_grad = second_pull(normed_two_grad)
    middle_grad = grad_out + middle_extra
    scale_one_grad = jnp.sum(middle_grad * first_factor * branch, axis=0)
    branch_grad = (middle_grad * first_factor * scale_full[:model_width]).astype(jnp.bfloat16)
    out_weight_grad = outer_sum(lowered[4], branch_grad)
    product_grad = times_transpose(branch_grad, out_weight)
    matrices = split_gated(gated_flat, model_width)
    starts = [0]
    for width_here in widths:
        starts.append(starts[-1] + width_here)
    gated_parts = [None, None, None, None]
    scaled_parts = [None, None, None, None, None]
    for section_idx in reversed(range(4)):
        scaled_part = scaled[:, starts[section_idx + 1] : starts[section_idx + 2]]
        inner_grad = (product_grad * scaled_part).astype(jnp.bfloat16)
        scaled_parts[section_idx + 1] = product_grad * inners[section_idx]
        gated_parts[section_idx] = outer_sum(lowered[section_idx], inner_grad)
        product_grad = times_transpose(inner_grad, matrices[section_idx])
    head_grad = product_grad * scaled[:, : widths[0]]
    scaled_parts[0] = product_grad * mixed_all[:, : widths[0]]
    scaled_grad = jnp.concatenate(scaled_parts, axis=1)
    unused_conv, conv_pull = jax.vjp(
        partial(depthwise, image_ids=image_ids),
        mixed_all[:, widths[0] :],
        kernel.astype(jnp.float32),
    )
    rest_grad, kernel_weight_grad = conv_pull(scaled_grad)
    mixed_grad = jnp.concatenate([head_grad, rest_grad], axis=1).astype(jnp.bfloat16)
    in_weight_grad = outer_sum(normed, mixed_grad)
    normed_grad = times_transpose(mixed_grad, in_weight)
    unused_one, first_pull = jax.vjp(
        layer_norm, residual, gain_full[:model_width], bias_full[:model_width]
    )
    residual_extra, gain_one_grad, bias_one_grad = first_pull(normed_grad)
    input_grad = middle_grad + residual_extra
    gated_grad = jnp.concatenate([matrix_grad.reshape(-1) for matrix_grad in gated_parts])
    weight_grads = (
        in_weight_grad,
        out_weight_grad,
        up_weight_grad,
        down_weight_grad,
        gated_grad,
        jnp.concatenate([gain_one_grad, gain_two_grad]),
        jnp.concatenate([bias_one_grad, bias_two_grad]),
        jnp.concatenate([scale_one_grad, scale_two_grad]),
    )
    return (input_grad, weight_grads, kernel_weight_grad)


def per_device(
    pixels,
    cotangent,
    image_plan,
    keep_mask,
    norm_gains,
    norm_biases,
    layer_scales,
    in_proj,
    depth_kernel,
    gated_weights,
    out_proj,
    up_proj,
    down_proj,
):
    tokens_here = pixels.shape[0]
    edge_cells = math.isqrt(tokens_here)
    tile_edge = edge_cells // 2
    layer_count = in_proj.shape[0]
    image_ids, factors = branch_factors(image_plan[0], keep_mask[0], edge_cells, tile_edge)
    residual = pixels.astype(jnp.float32)
    retained_all = []
    for layer_idx in range(layer_count):
        weights = (
            lax.all_gather(in_proj[layer_idx], ("dp", "fsdp"), axis=0, tiled=True),
            lax.all_gather(out_proj[layer_idx], ("dp", "fsdp"), axis=0, tiled=True),
            lax.all_gather(up_proj[layer_idx], ("dp", "fsdp"), axis=0, tiled=True),
            lax.all_gather(down_proj[layer_idx], ("dp", "fsdp"), axis=0, tiled=True),
            lax.all_gather(gated_weights[layer_idx], ("dp", "fsdp"), axis=0, tiled=True),
            lax.all_gather(norm_gains[layer_idx], ("dp", "fsdp"), axis=0, tiled=True),
            lax.all_gather(norm_biases[layer_idx], ("dp", "fsdp"), axis=0, tiled=True),
            lax.all_gather(layer_scales[layer_idx], ("dp", "fsdp"), axis=0, tiled=True),
        )
        kernel = lax.all_gather(depth_kernel[layer_idx], "fsdp", axis=0, tiled=True)
        residual, retained = forward_block(
            residual, weights, kernel, image_ids, factors[:, 2 * layer_idx : 2 * layer_idx + 2]
        )
        retained_all.append(retained)
    result = residual.astype(jnp.bfloat16)
    grad_now = cotangent.astype(jnp.float32)
    layer_grads = [None] * layer_count
    kernel_grads = [None] * layer_count
    for layer_idx in reversed(range(layer_count)):
        weights = (
            lax.all_gather(in_proj[layer_idx], ("dp", "fsdp"), axis=0, tiled=True),
            lax.all_gather(out_proj[layer_idx], ("dp", "fsdp"), axis=0, tiled=True),
            lax.all_gather(up_proj[layer_idx], ("dp", "fsdp"), axis=0, tiled=True),
            lax.all_gather(down_proj[layer_idx], ("dp", "fsdp"), axis=0, tiled=True),
            lax.all_gather(gated_weights[layer_idx], ("dp", "fsdp"), axis=0, tiled=True),
            lax.all_gather(norm_gains[layer_idx], ("dp", "fsdp"), axis=0, tiled=True),
            lax.all_gather(norm_biases[layer_idx], ("dp", "fsdp"), axis=0, tiled=True),
            lax.all_gather(layer_scales[layer_idx], ("dp", "fsdp"), axis=0, tiled=True),
        )
        kernel = lax.all_gather(depth_kernel[layer_idx], "fsdp", axis=0, tiled=True)
        grad_now, weight_grads, kernel_weight_grad = backward_block(
            grad_now,
            retained_all[layer_idx],
            weights,
            kernel,
            image_ids,
            factors[:, 2 * layer_idx : 2 * layer_idx + 2],
        )
        kernel_grads[layer_idx] = kernel_weight_grad
        layer_grads[layer_idx] = (
            lax.psum_scatter(weight_grads[0], ("dp", "fsdp"), scatter_dimension=0, tiled=True),
            lax.psum_scatter(weight_grads[1], ("dp", "fsdp"), scatter_dimension=0, tiled=True),
            lax.psum_scatter(weight_grads[2], ("dp", "fsdp"), scatter_dimension=0, tiled=True),
            lax.psum_scatter(weight_grads[3], ("dp", "fsdp"), scatter_dimension=0, tiled=True),
            lax.psum_scatter(weight_grads[4], ("dp", "fsdp"), scatter_dimension=0, tiled=True),
            lax.psum_scatter(weight_grads[5], ("dp", "fsdp"), scatter_dimension=0, tiled=True),
            lax.psum_scatter(weight_grads[6], ("dp", "fsdp"), scatter_dimension=0, tiled=True),
            lax.psum_scatter(weight_grads[7], ("dp", "fsdp"), scatter_dimension=0, tiled=True),
        )
    stacked = tuple(
        (
            jnp.stack([layer_grads[layer_idx][member] for layer_idx in range(layer_count)])
            for member in range(8)
        )
    )
    kernel_stack = jnp.stack(kernel_grads)
    kernel_share = lax.psum_scatter(
        kernel_stack.astype(jnp.bfloat16), "fsdp", scatter_dimension=1, tiled=True
    ).astype(jnp.float32)
    kernel_summed = lax.psum(kernel_share, "dp")
    return (
        result,
        grad_now,
        stacked[5],
        stacked[6],
        stacked[7],
        stacked[0],
        kernel_summed,
        stacked[4],
        stacked[1],
        stacked[2],
        stacked[3],
    )


def solution(mesh):
    in_specs = (
        P(("dp", "fsdp"), None),
        P(("dp", "fsdp"), None),
        P(("dp", "fsdp"), None),
        P(("dp", "fsdp"), None),
        P(None, ("dp", "fsdp")),
        P(None, ("dp", "fsdp")),
        P(None, ("dp", "fsdp")),
        P(None, ("dp", "fsdp"), None),
        P(None, "fsdp", None),
        P(None, ("dp", "fsdp")),
        P(None, ("dp", "fsdp"), None),
        P(None, ("dp", "fsdp"), None),
        P(None, ("dp", "fsdp"), None),
    )
    out_specs = (
        P(("dp", "fsdp"), None),
        P(("dp", "fsdp"), None),
        P(None, ("dp", "fsdp")),
        P(None, ("dp", "fsdp")),
        P(None, ("dp", "fsdp")),
        P(None, ("dp", "fsdp"), None),
        P(None, "fsdp", None),
        P(None, ("dp", "fsdp")),
        P(None, ("dp", "fsdp"), None),
        P(None, ("dp", "fsdp"), None),
        P(None, ("dp", "fsdp"), None),
    )
    return jax.shard_map(
        fast_device if fits(mesh) else per_device, mesh=mesh, in_specs=in_specs, out_specs=out_specs, check_vma=False
    )
```

```python
from functools import partial
import math

import jax
import jax.numpy as jnp
import numpy as np
from jax import lax
from jax.experimental import pallas as pl
from jax.experimental.pallas import tpu as pltpu
from jax.sharding import PartitionSpec as P

BF = jnp.bfloat16
F32 = jnp.float32
HALF = 352
SIDE = 512
Z_ORDER = (0, 2, 1, 3)
WIN = 12
VMEM_BYTES = 24 * 1024 * 1024


def half_spectrum(size):
    seen = set()
    kept = []
    for row in range(size):
        for col in range(size):
            if ((-row) % size, (-col) % size) in seen:
                continue
            seen.add((row, col))
            kept.append((row, col))
    return kept


def fourier_tables(edge):
    tile = edge // 2
    plans = [
        [(0, 0, tile), (0, tile, tile), (tile, 0, tile), (tile, tile, tile)],
        [(0, 0, edge)],
    ]
    forward = np.zeros((2, 2 * HALF, edge * edge), np.float32)
    taps = np.zeros((2, 2 * HALF, 64), np.float32)
    for which, tiles in enumerate(plans):
        at = 0
        for top, left, extent in tiles:
            size = extent + 3
            rows, cols = np.meshgrid(np.arange(extent), np.arange(extent), indexing="ij")
            slots = ((rows + top) * edge + cols + left).reshape(-1)
            tap_rows, tap_cols = np.meshgrid(np.arange(7) - 3, np.arange(7) - 3, indexing="ij")
            for fr, fc in half_spectrum(size):
                angle = 2 * np.pi * ((fr * rows + fc * cols) % size) / size
                forward[which, at, slots] = np.cos(angle).reshape(-1)
                forward[which, HALF + at, slots] = np.sin(angle).reshape(-1)
                weight = (1.0 if (fr, fc) == (0, 0) else 2.0) / (3.0 * size * size)
                angle = 2 * np.pi * ((fr * tap_rows + fc * tap_cols) % size) / size
                taps[which, at, :49] = weight * np.cos(angle).reshape(-1)
                taps[which, HALF + at, :49] = weight * np.sin(angle).reshape(-1)
                at += 1
        assert at <= HALF
    return (
        forward,
        np.ascontiguousarray(forward.transpose(0, 2, 1)),
        taps,
        np.ascontiguousarray(taps.transpose(0, 2, 1)),
    )


def mm(left, right):
    return lax.dot_general(left, right, (((1,), (0,)), ((), ())), preferred_element_type=F32)


def mm_nt(left, right):
    return lax.dot_general(left, right, (((1,), (1,)), ((), ())), preferred_element_type=F32)


def mm_tn(left, right):
    return lax.dot_general(left, right, (((0,), (0,)), ((), ())), preferred_element_type=F32)


def iota2(shape, dim):
    return lax.broadcasted_iota(jnp.int32, shape, dim)


def pixel_factor(plan_ref, keep_ref, column, edge, tile):
    slot = iota2((edge * edge, 1), 0)
    row = jnp.floor((slot.astype(F32) + 0.5) * (1.0 / edge)).astype(jnp.int32)
    col = slot - row * edge
    quarter = jnp.where(row >= tile, 2, 0) + jnp.where(col >= tile, 1, 0)
    large = plan_ref[0, 0]
    count = plan_ref[0, 1]
    width = keep_ref.shape[1] // 4
    total = jnp.zeros((edge * edge, 1), F32)
    for t in range(4):
        kept = keep_ref[0, t * width + column].astype(F32) * 1.25
        first = keep_ref[0, column].astype(F32) * 1.25
        here = jnp.where(t < count, kept, 0.0)
        here = jnp.where(large == 1, first, here)
        total = jnp.where(quarter == t, here, total)
    return total


def norm_stats(values):
    center = values - jnp.mean(values, axis=-1, keepdims=True)
    rstd = lax.rsqrt(jnp.mean(center * center, axis=-1, keepdims=True) + 1e-06)
    return center * rstd, rstd


def norm_back(grad, normal, rstd, gain):
    inner = grad * gain
    return rstd * (
        inner
        - jnp.mean(inner, axis=-1, keepdims=True)
        - normal * jnp.mean(inner * normal, axis=-1, keepdims=True)
    )


def window_map(shards, per):
    shape = (HALF, shards * 16)
    r = iota2(shape, 0)
    c = iota2(shape, 1)
    shard = lax.shift_right_logical(c, 4)
    t = c & 15
    flat_row = jnp.where(
        r < 256, r + 84, jnp.where(r < 320, r - 236, jnp.where(r < 336, r - 316, r - 336))
    )
    start = lax.shift_right_logical(shard * (per // 64), 3)
    gated = (t < WIN) & (r < 340) & (flat_row == start + t)
    norm = r - 344
    second = jnp.where(shard >= shards // 2, 1, 0)
    vec = (norm >= 0) & (norm < 6) & (t == WIN + lax.shift_right_arithmetic(norm, 1)) & ((norm & 1) == second)
    return jnp.where(gated | vec, 1.0, 0.0).astype(BF)


def spread(rows, cols, stride, offset, shift, count=None):
    r = iota2((rows, cols), 0) - shift
    c = iota2((rows, cols), 1)
    hit = r == stride * c + offset
    if count is not None:
        hit = hit & (c < count)
    return jnp.where(hit, 1.0, 0.0).astype(BF)


def lanes_from(values, low, high):
    lane = iota2(values.shape, 1)
    return jnp.where((lane >= low) & (lane < high), values, jnp.zeros_like(values))


def gated_matrices(flat):
    g2 = mm(spread(128, 64, 2, 0, 0), flat[256:320, 0:256]) + mm(
        spread(128, 64, 2, 1, 0), flat[256:320, 256:512]
    )
    g1 = jnp.zeros((128, 128), F32)
    for h in range(4):
        g1 = g1 + mm(spread(128, 16, 4, h, 64), flat[320:336, 128 * h : 128 * h + 128])
    g0 = jnp.zeros((128, 128), F32)
    for t in range(4):
        part = flat[336:352, 128 * t : 128 * t + 128].astype(F32)
        part = jnp.where(iota2(part.shape, 0) < 4, part, 0.0)
        odd = lanes_from(part, 64, 128).astype(BF)
        even = lanes_from(pltpu.roll(part, 64, 1), 64, 128).astype(BF)
        g0 = g0 + mm(spread(128, 16, 8, 2 * t, 32), even) + mm(spread(128, 16, 8, 2 * t + 1, 32), odd)
    return g0.astype(BF), g1.astype(BF), g2.astype(BF)


def matrix(w_ref, row):
    return w_ref[:, :, :, pl.ds(row, 16), :].reshape(SIDE, SIDE)


def down_rows(w_ref, j):
    return w_ref[j, :, :, 64:128, :].reshape(SIDE, SIDE)


def gelu_parts(hidden):
    root = math.sqrt(2.0 / math.pi)
    square = hidden * hidden
    bent = jnp.tanh(root * hidden * (1.0 + 0.044715 * square))
    half = 0.5 * (1.0 + bent)
    value = hidden * half
    slope = half + 0.5 * hidden * (1.0 - bent * bent) * (root * (1.0 + 0.134145 * square))
    return value, slope


def emit_block(read, outs, rows, place):
    yx = place[0]
    z = place[2]
    for sel in range(2):
        dest = place[1] ^ sel
        first = jnp.where(dest == 0, 1, 2)
        for r1 in range(2):
            for r2 in range(2):
                spot = yx ^ (r1 * first) ^ (r2 * (3 - first))
                for at, zrel in enumerate(Z_ORDER):
                    values = read(spot, dest, z ^ zrel)
                    outs[sel][r1 * 8 + r2 * 4 + at, rows, :] = values


def emit_rows(value, rows_ref, outs, row, place):
    rows_ref[...] = value.astype(BF).reshape(rows_ref.shape)
    emit_block(lambda spot, core, z: rows_ref[spot * 8 + core * 4 + z], outs, pl.ds(row, 16), place)


def tables_kernel(plan, *rest):
    mode = plan[0, 0]
    sources, targets, sems = rest[:4], rest[-5:-1], rest[-1]
    copies = [
        pltpu.make_async_copy(src.at[mode], dst, sems.at[n]) for n, (src, dst) in enumerate(zip(sources, targets))
    ]
    for copy in copies:
        copy.start()
    for copy in copies:
        copy.wait()


def mix_forward_kernel(
    layer, edge, per, plan, keep, x_ref, taps_ref, w_ref, forward, back, tapmap, *rest
):
    m1_ref, a0_ref, q_ref, z_ref, p_ref, y_ref, spec_ref, kern_ref, flat_ref, g0_ref, g1_ref, g2_ref, norm_ref = rest[
        -14:-1
    ]
    a_low = rest[-1]
    shards = 32
    factor = pixel_factor(plan, keep, 2 * layer, edge, edge // 2)
    picks = window_map(shards, per)
    flat = mm(picks, matrix(w_ref, 48))
    norm_ref[...] = flat[344:352]
    flat_low = flat.astype(BF)
    flat_ref[...] = flat_low
    g0, g1, g2 = gated_matrices(flat_low)
    g0_ref[...] = g0
    g1_ref[...] = g1
    g2_ref[...] = g2
    x = x_ref[...].astype(F32)
    normal, unused = norm_stats(x)
    u = (normal * flat[344:345] + flat[346:347]).astype(BF)
    for half in range(2):
        a = mm(u, matrix(w_ref, 16 * half))
        a_low[:, SIDE * half : SIDE * half + SIDE] = a.astype(BF)
        if half == 0:
            a0_ref[...] = a[:, :128]

    def channels(j):
        at = slice(j * SIDE, j * SIDE + SIDE)
        kernel = mm(tapmap[...], taps_ref[:, at])
        kern_ref[:, at] = kernel.astype(BF)
        spec = mm(forward[...], a_low[:, at])
        spec_ref[:, at] = spec.astype(BF)
        kr, ki = kernel[:HALF], kernel[HALF:]
        xc, xs = spec[:HALF], spec[HALF:]
        product = jnp.concatenate([xc * kr + xs * ki, xs * kr - xc * ki], axis=0).astype(BF)
        q_ref[:, at] = mm(back[...], product).astype(BF)

    for j in range(2):
        channels(j)
    q0 = q_ref[:, 0:128].astype(F32)
    p0 = lanes_from(pltpu.roll(a0_ref[...], 32, 1) * q0, 32, 64)
    z = mm(p0.astype(BF), g0)
    z_ref[:, 0:128] = z.astype(BF)
    p = z * q0
    p_ref[:, 0:128] = (p0 + p).astype(BF)
    z = mm(p.astype(BF), g1)
    z_ref[:, 128:256] = z.astype(BF)
    p = (z * q_ref[:, 128:256].astype(F32)).astype(BF)
    p_ref[:, 128:256] = p
    z = mm(p, g2)
    z_ref[:, 256:512] = z.astype(BF)
    p = (z * q_ref[:, 256:512].astype(F32)).astype(BF)
    p_ref[:, 256:512] = p
    z = mm(p, flat_ref[0:256, :])
    z_ref[:, 512:1024] = z.astype(BF)
    p = (z * q_ref[:, 512:1024].astype(F32)).astype(BF)
    p_ref[:, 512:1024] = p
    y = mm(p, matrix(w_ref, 32))
    y_ref[...] = y.astype(BF)
    m1_ref[...] = x + factor * flat[348:349] * y


def feed_forward_kernel(layer, edge, last, plan, keep, m1_ref, norm_ref, w_ref, *rest):
    x_ref, e_ref, slope_ref, f_ref, total = rest[-5:]
    factor = pixel_factor(plan, keep, 2 * layer + 1, edge, edge // 2)
    m1 = m1_ref[...]
    normal, unused = norm_stats(m1)
    v = (normal * norm_ref[1:2] + norm_ref[3:4]).astype(BF)
    total[...] = jnp.zeros_like(total)

    def hidden(j):
        at = slice(j * SIDE, j * SIDE + SIDE)
        value, slope = gelu_parts(mm(v, matrix(w_ref, j * 16)))
        e = value.astype(BF)
        e_ref[:, at] = e
        slope_ref[:, at] = slope.astype(BF)
        total[...] += mm(e, down_rows(w_ref, j))

    for j in range(4):
        hidden(j)
    f_ref[...] = total[...].astype(BF)
    x_ref[...] = (m1 + factor * norm_ref[5:6] * total[...]).astype(x_ref.dtype)


def feed_back_kernel(
    layer, edge, place, plan, keep, dx_ref, m1_ref, e_ref, slope_ref, f_ref, norm_ref, w_ref, *rest
):
    dm1_ref, *outs, small_ref, dv_ref, rows_ref, down_ref = rest[-7:]
    factor = pixel_factor(plan, keep, 2 * layer + 1, edge, edge // 2)
    dx = dx_ref[...].astype(F32)
    scaled = dx * factor
    small_ref[...] = jnp.zeros_like(small_ref)
    small_ref[5:6] = jnp.sum(scaled * f_ref[...].astype(F32), axis=0, keepdims=True)
    df = (scaled * norm_ref[5:6]).astype(BF)
    normal, rstd = norm_stats(m1_ref[...])
    v = (normal * norm_ref[1:2] + norm_ref[3:4]).astype(BF)
    dv_ref[...] = jnp.zeros_like(dv_ref)

    def hidden(j):
        at = slice(j * SIDE, j * SIDE + SIDE)
        e = e_ref[:, at]
        dh = (slope_ref[:, at].astype(F32) * mm_nt(df, down_rows(w_ref, j))).astype(BF)
        dv_ref[...] += mm_nt(dh, matrix(w_ref, j * 16))
        emit_rows(mm_tn(v, dh), rows_ref, outs, j * 16, place)
        down_ref[j] = mm_tn(e, df).astype(BF).reshape(down_ref.shape[1:])

    for j in range(4):
        hidden(j)
    emit_block(lambda spot, core, z: down_ref[spot, core, z], outs, slice(64, 128), place)
    dv = dv_ref[...]
    small_ref[1:2] = jnp.sum(dv * normal, axis=0, keepdims=True)
    small_ref[3:4] = jnp.sum(dv, axis=0, keepdims=True)
    dm1_ref[...] = dx + norm_back(dv, normal, rstd, norm_ref[1:2])


def chain_back_kernel(
    layer,
    edge,
    plan,
    keep,
    dm1_ref,
    a0_ref,
    q_ref,
    z_ref,
    p_ref,
    y_ref,
    flat_ref,
    g0_ref,
    g1_ref,
    g2_ref,
    norm_ref,
    small_ref,
    w_ref,
    *rest,
):
    dq_ref, dhead_ref, dflat_ref, dout_ref = rest[-4:]
    factor = pixel_factor(plan, keep, 2 * layer, edge, edge // 2)
    scaled = dm1_ref[...] * factor
    dscale = jnp.sum(scaled * y_ref[...].astype(F32), axis=0, keepdims=True)
    dy = (scaled * norm_ref[4:5]).astype(BF)
    dout_ref[...] = mm_tn(p_ref[:, 512:1024], dy).astype(BF)

    def link(dp, low, high):
        dz = (dp * q_ref[:, low:high].astype(F32)).astype(BF)
        return dz, dp * z_ref[:, low:high].astype(F32)

    dp = mm_nt(dy, matrix(w_ref, 32))
    dz, dq = link(dp, 512, 1024)
    dq_ref[:, 512:1024] = dq.astype(BF)
    dflat_ref[0:256, :] = mm_tn(p_ref[:, 256:512], dz).astype(BF)
    dp = mm_nt(dz, flat_ref[0:256, :])
    dz, dq = link(dp, 256, 512)
    dq_ref[:, 256:512] = dq.astype(BF)
    dg2 = mm_tn(p_ref[:, 128:256], dz).astype(BF)
    for h in range(2):
        dflat_ref[256:320, 256 * h : 256 * h + 256] = mm_tn(spread(128, 64, 2, h, 0), dg2).astype(BF)
    dp = mm_nt(dz, g2_ref[...])
    dz, dq = link(dp, 128, 256)
    dq_ref[:, 128:256] = dq.astype(BF)
    p01 = p_ref[:, 0:128]
    dg1 = mm_tn(p01, dz).astype(BF)
    for h in range(4):
        dflat_ref[320:336, 128 * h : 128 * h + 128] = mm_tn(spread(128, 16, 4, h, 64), dg1).astype(BF)
    dp = mm_nt(dz, g1_ref[...])
    dz, dq1 = link(dp, 0, 128)
    dg0 = mm_tn(p01, dz).astype(BF)
    norm_rows = jnp.concatenate(
        [jnp.zeros((8, SIDE), F32), small_ref[0:4], dscale, small_ref[5:8]], axis=0
    )
    for t in range(4):
        even = mm_tn(spread(128, 16, 8, 2 * t, 32, 4), dg0)
        odd = mm_tn(spread(128, 16, 8, 2 * t + 1, 32, 4), dg0)
        at = slice(128 * t, 128 * t + 128)
        dflat_ref[336:352, at] = (
            lanes_from(odd, 64, 128) + pltpu.roll(lanes_from(even, 64, 128), 64, 1) + norm_rows[:, at]
        ).astype(BF)
    dp = mm_nt(dz, g0_ref[...])
    head = lanes_from(pltpu.roll(a0_ref[...], 32, 1), 32, 64)
    dq_ref[:, 0:128] = (dq1 + dp * head).astype(BF)
    dhead_ref[...] = pltpu.roll(lanes_from(dp * q_ref[:, 0:128].astype(F32), 32, 64), 96, 1)


def spectrum_back_kernel(place, spec_ref, kern_ref, dq_ref, dhead_ref, forward, back, tapback, *rest):
    da_ref, kernel_out, dtaps_ref = rest[-3:]
    dtaps_ref[:, 1024:] = jnp.zeros((64, 128), F32)

    def channels(j):
        at = slice(j * SIDE, j * SIDE + SIDE)
        kernel = kern_ref[:, at].astype(F32)
        grad = mm(forward[...], dq_ref[:, at])
        spec = spec_ref[:, at].astype(F32)
        kr, ki = kernel[:HALF], kernel[HALF:]
        dc, ds = grad[:HALF], grad[HALF:]
        xc, xs = spec[:HALF], spec[HALF:]
        dspec = jnp.concatenate([dc * kr - ds * ki, dc * ki + ds * kr], axis=0).astype(BF)
        da_ref[:, at] = mm(back[...], dspec).astype(BF)
        dkernel = jnp.concatenate([dc * xc + ds * xs, dc * xs - ds * xc], axis=0).astype(BF)
        dtaps_ref[:, at] = mm(tapback[...], dkernel)

    for j in range(2):
        channels(j)
    da_ref[:, 0:128] = (da_ref[:, 0:128].astype(F32) + dhead_ref[...]).astype(BF)
    count = (1024 - 32) // 4
    for shard in range(4):
        low = 32 + count * shard
        rel = shard ^ place[2]
        at = (rel & 1) * 2 + (rel >> 1)
        kernel_out[at, :, 0:256] = dtaps_ref[0:32, low : low + 256].astype(BF)
        kernel_out[at, :, 256:512] = dtaps_ref[32:64, low : low + 256].astype(BF)


def mix_back_kernel(per, place, dm1_ref, x_ref, norm_ref, da_ref, dflat_ref, dout_ref, w_ref, *rest):
    dx_ref, *outs, rows_ref = rest[-4:]
    emit_rows(dout_ref[...], rows_ref, outs, 32, place)
    normal, rstd = norm_stats(x_ref[...].astype(F32))
    gain = norm_ref[0:1]
    u = (normal * gain + norm_ref[2:3]).astype(BF)
    du = jnp.zeros(dm1_ref.shape, F32)
    for half in range(2):
        da = da_ref[:, SIDE * half : SIDE * half + SIDE]
        emit_rows(mm_tn(u, da), rows_ref, outs, 16 * half, place)
        du = du + mm_nt(da, matrix(w_ref, 16 * half))
    dgain = jnp.sum(du * normal, axis=0, keepdims=True)
    dbias = jnp.sum(du, axis=0, keepdims=True)
    low = dflat_ref[336:352, :].astype(F32)
    row = iota2(low.shape, 0)
    low = jnp.where(row == 8, dgain, jnp.where(row == 10, dbias, low))
    dflat = jnp.concatenate([dflat_ref[0:336, :], low.astype(BF)], axis=0)
    emit_rows(mm_tn(window_map(32, per), dflat), rows_ref, outs, 48, place)
    dx_ref[...] = dm1_ref[...] + norm_back(du, normal, rstd, gain)


def place_lanes(row, lanes, shift):
    pad = jnp.zeros((row.shape[0], lanes - row.shape[1]), F32)
    return pltpu.roll(jnp.concatenate([row.astype(F32), pad], axis=1), shift, 1)


def start_all(plans, sems, row=0):
    copies = [pltpu.make_async_copy(src, dst, sems.at[row + n]) for n, (src, dst) in enumerate(plans)]
    for copy in copies:
        copy.start()
    return copies


def mix_plans(layer, in_hbm, out_hbm, gated_hbm, gain_hbm, bias_hbm, scale_hbm, pack_ref, parts):
    gated_ref, gain_ref, bias_ref, scale_ref = parts
    return [
        (gated_hbm, gated_ref),
        (gain_hbm, gain_ref),
        (bias_hbm, bias_ref),
        (scale_hbm, scale_ref),
        (in_hbm.at[layer, :, pl.ds(0, SIDE)], pack_ref.at[pl.ds(0, 16)]),
        (in_hbm.at[layer, :, pl.ds(SIDE, SIDE)], pack_ref.at[pl.ds(16, 16)]),
        (out_hbm.at[layer], pack_ref.at[pl.ds(32, 16)]),
    ]


def feed_plans(layer, up_hbm, down_hbm, pack_ref, row):
    plans = [
        (up_hbm.at[layer, :, pl.ds(SIDE * b, SIDE)], pack_ref.at[pl.ds(row + 16 * b, 16)]) for b in range(4)
    ]
    return plans + [(down_hbm.at[layer], pack_ref.at[pl.ds(row + 64, 64)])]


def window_rows(layer, place, pack_ref, parts):
    gated_ref, *vectors = parts
    gated = place_lanes(gated_ref[layer : layer + 1, :], WIN * SIDE, place[4])
    rows = [gated[:, SIDE * r : SIDE * r + SIDE] for r in range(WIN)]
    for ref in vectors:
        rows.append(place_lanes(ref[layer : layer + 1, :], SIDE, place[5]))
    rows.append(jnp.zeros((1, SIDE), F32))
    pack_ref[48:64, :] = jnp.concatenate(rows, axis=0).astype(BF)


def tap_rows(taps_ref, wide, pack_ref, row):
    wide[...] = jnp.zeros_like(wide)
    wide[: taps_ref.shape[0], : taps_ref.shape[1]] = taps_ref[...].astype(F32)
    turned = wide[...].T.astype(BF)
    pack_ref[row : row + 32, 0:256] = turned[0:32]
    pack_ref[row : row + 32, 256:512] = turned[32:64]


def pack_mix_kernel(layer, place, in_hbm, out_hbm, gated_hbm, gain_hbm, bias_hbm, scale_hbm, *rest):
    out, *parts, sems = rest[-6:]
    pack_ref = out.at[0]
    plans = mix_plans(layer, in_hbm, out_hbm, gated_hbm, gain_hbm, bias_hbm, scale_hbm, pack_ref, parts)
    for copy in start_all(plans, sems):
        copy.wait()
    window_rows(layer, place, pack_ref, parts)


def pack_feed_kernel(layer, up_hbm, down_hbm, taps_hbm, *rest):
    out, taps_ref, wide, sems = rest[-4:]
    pack_ref = out.at[0]
    plans = feed_plans(layer, up_hbm, down_hbm, pack_ref, 0) + [(taps_hbm.at[layer], taps_ref)]
    for copy in start_all(plans, sems):
        copy.wait()
    tap_rows(taps_ref, wide, pack_ref, 128)


def pack_both_kernel(
    layer, place, in_hbm, out_hbm, gated_hbm, gain_hbm, bias_hbm, scale_hbm, up_hbm, down_hbm, taps_hbm, *rest
):
    out, *parts, taps_ref, wide, sems = rest[-8:]
    pack_ref = out.at[0]
    plans = mix_plans(layer, in_hbm, out_hbm, gated_hbm, gain_hbm, bias_hbm, scale_hbm, pack_ref, parts)
    plans += feed_plans(layer, up_hbm, down_hbm, pack_ref, 64) + [(taps_hbm.at[layer], taps_ref)]
    for copy in start_all(plans, sems):
        copy.wait()
    window_rows(layer, place, pack_ref, parts)
    tap_rows(taps_ref, wide, pack_ref, 192)


def join_wide(split, wide, taps):
    wide[:, 0:128] = jnp.zeros((64, 128), F32)
    count = (1024 - 32) // 4
    for shard in range(4):
        low = 32 + count * shard
        wide[0:32, low : low + count] = split[shard, :, 0:count]
        wide[32:64, low : low + count] = split[shard, :, 256 : 256 + count]
    taps[...] = wide[...].astype(BF)


def split_kernel(place, mine, got, *rest):
    *parts, taps, split, wide = rest[-4:] if mine.shape[1] == 160 else rest[-5:]
    parts = parts[-1:] if mine.shape[1] == 160 else parts
    for at, zrel in enumerate(Z_ORDER):
        piece = mine[at] if at < 2 else got[at - 2]
        row = 0
        for part in parts:
            part[at] = piece[row : row + part.shape[1], :]
            row += part.shape[1]
        split[place[2] ^ zrel] = piece[row : row + 32, :].astype(F32)
    join_wide(split, wide, taps)


def four_kernel(mine, got2, got1, got3, *rest):
    for at, piece in enumerate((mine, got2, got1, got3)):
        rest[-1][at] = piece[0]


def join_kernel(mine, got, *rest):
    out = rest[-1]
    count = mine.shape[0]
    out[:count] = mine[...]
    out[count:] = got[...]


def place_kernel(place, mine, got, other_a, other_b, other_c, *rest):
    out = rest[-1]
    for number, pieces in enumerate(((mine, got), (other_a, other_b, other_c))):
        source = place[1] ^ number
        first = jnp.where(source == 0, 1, 2)
        at = 0
        for piece in pieces:
            for n in range(piece.shape[0]):
                spot = place[0] ^ (((at >> 2) & 1) * first) ^ ((at >> 3) * (3 - first))
                out[spot, source, place[2] ^ Z_ORDER[at & 3]] = piece[n]
                at += 1


def step_kernel(kept, got, *rest):
    stay, out = rest[-2:]
    count = out.shape[0]

    def one(n, carry):
        stay[n] = kept[n].astype(F32) + got[n].astype(F32)
        out[n] = (kept[count + n].astype(F32) + got[count + n].astype(F32)).astype(BF)
        return carry

    lax.fori_loop(0, count, one, 0)


def settle_kernel(kept, got, *rest):
    rest[-1][...] = kept[0] + got[0].astype(F32)


def merge_taps_kernel(kept, got, taps0, taps1, *rest):
    stay, out = rest[-2:]
    total = kept[...] + got[...].astype(F32)
    stay[:, 0:64] = total[0:2]
    out[:, 0:64] = total[2:4].astype(BF)
    for n, taps in enumerate((taps0, taps1)):
        row = 64 + 32 * n
        stay[:, row : row + 32] = taps[0:2].astype(F32)
        out[:, row : row + 32] = taps[2:4]


def settle_taps_kernel(kept, got, *rest):
    total, low = rest[-2:]
    total[...] = kept[0, 0:64] + got[0, 0:64].astype(F32)
    low[...] = (kept[0, 64:128] + got[0, 64:128].astype(F32)).astype(BF)


def tap_sum_kernel(mine, got, *rest):
    out = rest[-1]
    out[...] = (mine[...].astype(F32) + got[...].astype(F32)).astype(out.dtype)


def unpack_kernel(layers, place, *rest):
    gain_ref, bias_ref, scale_ref, in_ref, gated_ref, out_ref, up_ref, down_ref = rest[-8:]
    per = gated_ref.shape[1]
    for layer in range(layers):
        if layer == 0:
            mix = rest[0][0] + rest[1][0].astype(F32)
            feed = rest[2][0] + rest[3][0].astype(F32)
        else:
            mix, feed = rest[4], rest[5]
        in_ref[layer, :, :SIDE] = mix[0:16]
        in_ref[layer, :, SIDE:] = mix[16:32]
        out_ref[layer] = mix[32:48]
        flat = jnp.concatenate([mix[48 + r : 49 + r] for r in range(WIN)], axis=1)
        flat = pltpu.roll(flat, WIN * SIDE - place[4], 1)
        gated_ref[layer : layer + 1, :] = flat[:, :per]
        for n, ref in enumerate((gain_ref, bias_ref, scale_ref)):
            row = pltpu.roll(mix[48 + WIN + n : 49 + WIN + n], SIDE - place[5], 1)
            ref[layer : layer + 1, :] = row[:, : ref.shape[1]]
        for b in range(4):
            up_ref[layer, :, SIDE * b : SIDE * b + SIDE] = feed[16 * b : 16 * b + 16]
        down_ref[layer] = feed[64:128]


def whole(shape, dtype):
    return jax.ShapeDtypeStruct(shape, dtype)


VM = pl.BlockSpec(memory_space=pltpu.VMEM)
SM = pl.BlockSpec(memory_space=pltpu.SMEM)
HB = pl.BlockSpec(memory_space=pltpu.HBM)
ANY = pl.BlockSpec(memory_space=pl.ANY)


FORWARD_ORDER = (
    "a01", "b01", "a03", "b02", "a04", "b03", "c11", "a05", "T", "a06", "mf0", "b04",
    "c12", "c13", "b05", "a14", "b06", "ff0", "b14", "a15", "a16", "mf1", "b15", "b16",
    "ff1",
)
BACKWARD_ORDER = (
    "fb1", "B10", "cb1", "B11", "sb1", "mb1", "A10", "fb0", "B12", "A11", "B00", "cb0",
    "B01", "sb0", "B13", "A12", "mb0", "A00", "B14", "A13", "B02", "A01", "A14", "B03",
    "A02", "A15", "B04", "t1", "A03", "t2", "B15", "A04", "t3",
)
SCALE = 1.0
SMALL = 20.0
SMALL_F = 20.0
MICROS = {
    "mix_forward": 7.5,
    "feed_forward": 4.5,
    "feed_back": 8.0,
    "chain_back": 3.3,
    "spectrum_back": 5.8,
    "mix_back": 3.0,
}


EVENT_MICROS = {
    **dict.fromkeys(("mf0", "ff0", "mf1", "b06"), 0.02),
    **dict.fromkeys(("a15", "a16", "b15", "b16", "sb0", "A11"), 5.0),
    **dict.fromkeys(("B00", "B02", "B03", "B04", "A02", "A03"), 40.0),
    **dict.fromkeys(("A04", "B14"), 10.0),
}


class Order:
    def __init__(self):
        self.last = ()
        self.event = None

    def cost(self, name):
        small = SMALL_F if self.event in FORWARD_ORDER else SMALL
        micros = EVENT_MICROS.get(self.event, MICROS.get(name, small) * SCALE)
        return pl.CostEstimate(flops=int(micros * 1e9), bytes_accessed=10_000, transcendentals=0)

    def hold(self, values):
        values = pl.pallas_call(
            lambda *refs: None,
            out_shape=tuple(whole(value.shape, value.dtype) for value in values),
            in_specs=[ANY] * (len(values) + 1),
            out_specs=(ANY,) * len(values),
            input_output_aliases={n: n for n in range(len(values))},
            compiler_params=pltpu.CompilerParams(vmem_limit_bytes=1024 * 1024),
            cost_estimate=self.cost("hold"),
            name="hold",
        )(*values, *self.last)
        self.last = (values[0],)
        return values

    def __call__(self, kernel, ins, in_specs, outs, scratch, name, limit=None):
        many = isinstance(outs, tuple)
        results = pl.pallas_call(
            kernel,
            out_shape=outs,
            in_specs=list(in_specs) + [ANY] * len(self.last),
            out_specs=jax.tree.map(lambda unused: VM, outs),
            scratch_shapes=scratch,
            compiler_params=pltpu.CompilerParams(vmem_limit_bytes=limit or VMEM_BYTES),
            cost_estimate=self.cost(name),
            name=name,
        )(*ins, *self.last)
        self.last = (min(results, key=lambda result: result.size * result.dtype.itemsize) if many else results,)
        return results


CORE = [(i, i ^ 1) for i in range(8)]
FIRST = [(i, i ^ (4 if i & 1 else 2)) for i in range(8)]
SECOND = [(i, i ^ (2 if i & 1 else 4)) for i in range(8)]
AXIS_X = [(i, i ^ 2) for i in range(8)]
AXIS_Y = [(i, i ^ 4) for i in range(8)]


def along(values, perm):
    return lax.ppermute(values, "dp", perm)


def along_z(values, k):
    return lax.ppermute(values, "fsdp", [(i, i ^ k) for i in range(4)])


class Gather:
    def __init__(self, order, pack):
        self.order = order
        self.have = pack
        self.come = None if pack is None else along_z(pack, 2)

    def join(self):
        shape = (2 * self.have.shape[0], *self.have.shape[1:])
        self.have = self.order(join_kernel, (self.have, self.come), [VM, VM], whole(shape, BF), [], "join")

    def second(self):
        self.join()
        self.come = along_z(self.have, 1)

    def third(self):
        self.join()
        self.first_axis()

    def first_axis(self):
        self.come = along(self.have, FIRST)
        self.other = [along(self.have, CORE)]

    def fourth(self):
        (self.come,) = self.order.hold([self.come])
        self.other.append(along(self.come, CORE))
        self.join()
        self.come = along(self.have, SECOND)

    def core(self):
        (self.come,) = self.order.hold([self.come])
        self.other.append(along(self.come, CORE))

    def finish(self, place):
        shape = (4, 2, 4, *self.have.shape[1:])
        self.whole = self.order(
            place_kernel, (place, self.have, self.come, *self.other), [SM] + [VM] * 5, whole(shape, BF), [], "place"
        )


class GatherDirect(Gather):
    def __init__(self, order, pack):
        self.order = order
        self.have = pack
        self.come = [along_z(pack, k) for k in Z_ORDER[1:]]

    def third(self):
        shape = (4, *self.have.shape[1:])
        self.have = self.order(four_kernel, (self.have, *self.come), [VM] * 4, whole(shape, BF), [], "four")
        self.first_axis()


def split(order, place, both, rows):
    *parts, taps = order(
        split_kernel,
        (place, both.have, both.come),
        [SM, VM, VM],
        (*[whole((4, count, SIDE), BF) for count in rows], whole((64, 1024), BF)),
        [pltpu.VMEM((4, 32, SIDE), F32), pltpu.VMEM((64, 1024), F32)],
        "split",
    )
    chains = []
    for part in parts:
        chains.append(Gather(order, None))
        chains[-1].have = part
        chains[-1].first_axis()
    return chains, taps


class Scatter:
    def __init__(self, order, keep, send):
        self.order = order
        self.keep = keep
        self.send = send
        self.moves = [
            lambda out: along(out, FIRST),
            lambda out: along(out, SECOND),
            lambda out: along_z(out, 1),
            lambda out: along_z(out, 2),
        ]

    def step(self):
        shape = (self.keep.shape[0] // 2, *self.keep.shape[1:])
        self.keep, out = self.order(
            step_kernel,
            (self.keep, self.come),
            [VM] * 2,
            (whole(shape, F32), whole(shape, BF)),
            [],
            "step",
        )
        self.come = self.moves.pop(0)(out)

    def start(self):
        (self.come,) = [along(part, CORE) for part in self.order.hold(self.send)]

    def settle(self):
        shape = self.keep.shape[1:]
        self.total = self.order(settle_kernel, (self.keep, self.come), [VM, VM], whole(shape, F32), [], "settle")


class TapSum(Scatter):
    def __init__(self, order, mix, taps):
        self.order = order
        self.moves = mix.moves[1:]
        self.keep, out = order(
            merge_taps_kernel,
            (mix.keep, mix.come, *taps),
            [VM] * 4,
            (whole((2, 128, SIDE), F32), whole((2, 128, SIDE), BF)),
            [],
            "merge_taps",
        )
        self.come = along_z(out, 1)

    def settle(self):
        self.total, self.low = self.order(
            settle_taps_kernel,
            (self.keep, self.come),
            [VM] * 2,
            (whole((64, SIDE), F32), whole((64, SIDE), BF)),
            [],
            "settle",
        )
        self.come = along(self.low, CORE)

    def taps(self, perm):
        self.low = self.order(
            tap_sum_kernel, (self.low, self.come), [VM] * 2, whole((64, SIDE), BF), [], "tap_sum"
        )
        self.come = along(self.low, perm)

    def final(self):
        total = self.order(tap_sum_kernel, (self.low, self.come), [VM] * 2, whole((64, SIDE), F32), [], "tap_sum")
        return total.reshape(2, 32, SIDE)


def fast_device(
    pixels,
    cotangent,
    image_plan,
    keep_mask,
    norm_gains,
    norm_biases,
    layer_scales,
    in_proj,
    depth_kernel,
    gated_weights,
    out_proj,
    up_proj,
    down_proj,
):
    pix, width = pixels.shape
    edge = math.isqrt(pix)
    per = gated_weights.shape[1]
    dp = lax.axis_index("dp")
    z = lax.axis_index("fsdp")
    me = dp * 4 + z
    phase = 64 * ((me * (per // 64)) % 8)
    place = jnp.stack([dp >> 1, dp & 1, z, me, phase, 32 * (me % 16)]).astype(jnp.int32)
    tables = [jnp.asarray(t, BF) for t in fourier_tables(edge)]
    count = depth_kernel.shape[1]
    order = Order()
    mix_ins = (place, in_proj, out_proj, gated_weights, norm_gains, norm_biases, layer_scales)
    mix_parts = [pltpu.VMEM(part.shape, BF) for part in mix_ins[3:]]
    tap_parts = [pltpu.VMEM(depth_kernel.shape[1:], BF), pltpu.VMEM((256, 128), F32)]

    def pack_mix(l):
        pack = order(
            partial(pack_mix_kernel, l),
            mix_ins,
            [SM] + [HB] * 6,
            whole((1, 64, SIDE), BF),
            mix_parts + [pltpu.SemaphoreType.DMA((7,))],
            "pack_mix",
            60 * 1024 * 1024,
        )
        return GatherDirect(order, pack)

    def pack_feed(l):
        pack = order(
            partial(pack_feed_kernel, l),
            (up_proj, down_proj, depth_kernel),
            [HB] * 3,
            whole((1, 160, SIDE), BF),
            tap_parts + [pltpu.SemaphoreType.DMA((6,))],
            "pack_feed",
        )
        return Gather(order, pack)

    def pack_both(l):
        pack = order(
            partial(pack_both_kernel, l),
            (*mix_ins, up_proj, down_proj, depth_kernel),
            [SM] + [HB] * 9,
            whole((1, 224, SIDE), BF),
            mix_parts + tap_parts + [pltpu.SemaphoreType.DMA((13,))],
            "pack_both",
        )
        return Gather(order, pack)

    def mix_forward(l, x, mix):
        return order(
            partial(mix_forward_kernel, l, edge, per),
            (image_plan, keep_mask, x, state[f"taps{l}"], mix.whole, *state["tables"][:3]),
            [SM, SM] + [VM] * 6,
            (
                whole((pix, width), F32),
                whole((pix, 128), F32),
                whole((pix, 1024), BF),
                whole((pix, 1024), BF),
                whole((pix, 1024), BF),
                whole((pix, width), BF),
                whole((2 * HALF, 1024), BF),
                whole((2 * HALF, 1024), BF),
                whole((HALF, SIDE), BF),
                whole((128, 128), BF),
                whole((128, 128), BF),
                whole((128, 256), BF),
                whole((8, SIDE), F32),
            ),
            [pltpu.VMEM((pix, 1024), BF)],
            "mix_forward",
        )

    def feed_forward(l, mixed, feed, last):
        return order(
            partial(feed_forward_kernel, l, edge, last),
            (image_plan, keep_mask, mixed[0], mixed[12], feed.whole),
            [SM, SM] + [VM] * 3,
            (
                whole((pix, width), BF if last else F32),
                whole((pix, 4 * SIDE), BF),
                whole((pix, 4 * SIDE), BF),
                whole((pix, width), BF),
            ),
            [pltpu.VMEM((pix, width), F32)],
            "feed_forward",
        )

    def feed_back(l, dx, mixed, fed, feed):
        return order(
            partial(feed_back_kernel, l, edge),
            (place, image_plan, keep_mask, dx, mixed[0], *fed[1:], mixed[12], feed.whole),
            [SM] * 3 + [VM] * 7,
            (
                whole((pix, width), F32),
                whole((16, 128, SIDE), BF),
                whole((16, 128, SIDE), BF),
                whole((8, SIDE), F32),
            ),
            [
                pltpu.VMEM((pix, width), F32),
                pltpu.VMEM((32, 16, SIDE), BF),
                pltpu.VMEM((4, 2, 4, 64, SIDE), BF),
            ],
            "feed_back",
        )

    def chain_back(l, dm1, mixed, small, mix):
        m1, a0, q, zs, ps, y, spec, kern, flat, g0, g1, g2, norms = mixed
        return order(
            partial(chain_back_kernel, l, edge),
            (image_plan, keep_mask, dm1, a0, q, zs, ps, y, flat, g0, g1, g2, norms, small, mix.whole),
            [SM] * 2 + [VM] * 13,
            (
                whole((pix, 1024), BF),
                whole((pix, 128), F32),
                whole((HALF, SIDE), BF),
                whole((SIDE, SIDE), BF),
            ),
            [],
            "chain_back",
        )

    def spectrum_back(mixed, dq, dhead):
        return order(
            spectrum_back_kernel,
            (place, mixed[6], mixed[7], dq, dhead, *state["tables"][:2], state["tables"][3]),
            [SM] + [VM] * 7,
            (whole((pix, 1024), BF), whole((4, 32, SIDE), BF)),
            [pltpu.VMEM((64, 1024 + 128), F32)],
            "spectrum_back",
        )

    def mix_back(dm1, x, mixed, da, dflat, dout, mix):
        return order(
            partial(mix_back_kernel, per),
            (place, dm1, x, mixed[12], da, dflat, dout, mix.whole),
            [SM] + [VM] * 7,
            (whole((pix, width), F32), whole((16, 64, SIDE), BF), whole((16, 64, SIDE), BF)),
            [pltpu.VMEM((32, 16, SIDE), BF)],
            "mix_back",
        )

    state = {"x0": pixels, "dx2": cotangent}

    def load_tables():
        state["tables"] = order(
            tables_kernel,
            (image_plan, *tables),
            [SM] + [HB] * 4,
            tuple(whole(table.shape[1:], BF) for table in tables),
            [pltpu.SemaphoreType.DMA((4,))],
            "tables",
        )

    def pack(name):
        state[name] = {"a0": partial(pack_mix, 0), "b0": partial(pack_feed, 0), "c1": partial(pack_both, 1)}[name]()

    def gather(name, step):
        chain = state[name]
        if name == "c1" and step == 3:
            (state["a1"], state["b1"]), state["taps1"] = split(order, place, chain, (64, 128))
        elif name == "b0" and step == 3:
            (state["b0"],), state["taps0"] = split(order, place, chain, (128,))
        else:
            (chain.second, chain.third, chain.fourth)[step - 2]()

    def finish(name, step):
        if step == 5:
            state[name].core()
        else:
            state[name].finish(place)

    def forward_mix(l):
        state[f"mixed{l}"] = mix_forward(l, state[f"x{l}"], state[f"a{l}"])

    def forward_feed(l):
        state[f"fed{l}"] = feed_forward(l, state[f"mixed{l}"], state[f"b{l}"], l == 1)
        state[f"x{l + 1}"] = state[f"fed{l}"][0]

    def backward_feed(l):
        state["dm"], keep, *send, state["small"] = feed_back(
            l, state[f"dx{l + 1}"], state[f"mixed{l}"], state[f"fed{l}"], state[f"b{l}"]
        )
        state[f"feedsum{l}"] = Scatter(order, keep, send)

    def backward_chain(l):
        state["chain"] = chain_back(l, state["dm"], state[f"mixed{l}"], state["small"], state[f"a{l}"])

    def backward_spectrum(l):
        dq, dhead, dflat, dout = state["chain"]
        state["da"], state[f"dtaps{l}"] = spectrum_back(state[f"mixed{l}"], dq, dhead)

    def backward_mix(l):
        dq, dhead, dflat, dout = state["chain"]
        state[f"dx{l}"], keep, *send = mix_back(
            state["dm"], state[f"x{l}"], state[f"mixed{l}"], state["da"], dflat, dout, state[f"a{l}"]
        )
        state[f"mixsum{l}"] = Scatter(order, keep, send)

    def scatter(l, mix, step):
        chain = state[f"mixsum{l}" if mix else f"feedsum{l}"]
        if step == 0:
            chain.start()
        elif mix and l == 1 and step == 3:
            state["mixsum1"] = TapSum(order, chain, (state["dtaps0"], state["dtaps1"]))
        elif step == 5:
            chain.settle()
        else:
            chain.step()

    def sum_taps(step):
        if step == 3:
            state["taps"] = state["mixsum1"].final()
        else:
            state["mixsum1"].taps(AXIS_X if step == 1 else AXIS_Y)

    events = {"T": load_tables}
    for name in ("a0", "b0", "c1"):
        events[name + "1"] = partial(pack, name)
    for name in ("a0", "b0", "c1", "a1", "b1"):
        for step in (5, 6):
            events[f"{name}{step}"] = partial(finish, name, step)
        for step in range(2, 5):
            events[f"{name}{step}"] = partial(gather, name, step)
    for l in range(2):
        for step in range(6):
            events[f"A{l}{step}"] = partial(scatter, l, True, step)
            events[f"B{l}{step}"] = partial(scatter, l, False, step)
        events[f"mf{l}"] = partial(forward_mix, l)
        events[f"ff{l}"] = partial(forward_feed, l)
        events[f"fb{l}"] = partial(backward_feed, l)
        events[f"cb{l}"] = partial(backward_chain, l)
        events[f"sb{l}"] = partial(backward_spectrum, l)
        events[f"mb{l}"] = partial(backward_mix, l)
    for step in (1, 2, 3):
        events[f"t{step}"] = partial(sum_taps, step)
    for name in FORWARD_ORDER + BACKWARD_ORDER:
        order.event = name
        events[name]()
    terms = [part for name in ("mix", "feed") for part in (state[f"{name}sum0"].keep, state[f"{name}sum0"].come)]
    terms += [state["mixsum1"].total, state["feedsum1"].total]
    result, dx = state["x2"], state["dx0"]
    gain, bias, scale, in_grad, gated, out_grad, up, down = order(
        partial(unpack_kernel, 2),
        (place, *terms),
        [SM] + [VM] * len(terms),
        tuple(
            whole(ref.shape, F32)
            for ref in (
                norm_gains,
                norm_biases,
                layer_scales,
                in_proj,
                gated_weights,
                out_proj,
                up_proj,
                down_proj,
            )
        ),
        [],
        "unpack",
    )
    taps_grad = state["taps"]
    taps_grad = jnp.concatenate([taps_grad[..., :count], taps_grad[..., 256 : 256 + count]], axis=1)
    taps_grad = jnp.swapaxes(taps_grad[:, :49], 1, 2)
    return (result, dx, gain, bias, scale, in_grad, taps_grad, gated, out_grad, up, down)


def fits(mesh):
    return dict(mesh.shape) == {"dp": 8, "fsdp": 4}


def layer_norm(values, gain_vec, bias_vec):
    center = values - jnp.mean(values, axis=-1, keepdims=True)
    spread = jnp.mean(center * center, axis=-1, keepdims=True)
    return center * lax.rsqrt(spread + 1e-06) * gain_vec + bias_vec


def branch_factors(layout_plan, keep_row, edge_cells, tile_edge):
    row_ids = jnp.arange(edge_cells, dtype=jnp.int32)[:, None]
    col_ids = jnp.arange(edge_cells, dtype=jnp.int32)[None, :]
    quarter = row_ids // tile_edge * 2 + col_ids // tile_edge
    image_ids = jnp.where(layout_plan[0] == 1, jnp.zeros_like(quarter), quarter)
    occupied = jnp.where(
        layout_plan[0] == 1, jnp.ones_like(quarter), (quarter < layout_plan[1]).astype(jnp.int32)
    )
    onehot = (image_ids.reshape(-1, 1) == jnp.arange(4, dtype=jnp.int32)[None, :]).astype(
        jnp.float32
    )
    keep_table = keep_row.reshape(4, -1).astype(jnp.float32)
    chosen = jnp.dot(onehot, keep_table, precision=lax.Precision.HIGHEST)
    return (image_ids, chosen * occupied.astype(jnp.float32).reshape(-1, 1) * 1.25)


def depthwise(values_in, kernel, image_ids):
    edge_cells = image_ids.shape[0]
    spatial = values_in.reshape(edge_cells, edge_cells, -1)
    padded = jnp.pad(spatial, ((3, 3), (3, 3), (0, 0)))
    padded_ids = jnp.pad(image_ids, 3, constant_values=-1)
    summed = jnp.zeros_like(spatial)
    for offset in range(49):
        row_off = offset // 7
        col_off = offset % 7
        nearby = padded[row_off : row_off + edge_cells, col_off : col_off + edge_cells]
        matched = (
            padded_ids[row_off : row_off + edge_cells, col_off : col_off + edge_cells] == image_ids
        ).astype(jnp.float32)
        summed = summed + nearby * matched[:, :, None] * kernel[:, offset]
    return summed.reshape(values_in.shape) / 3.0


def gated_widths(model_width):
    return [model_width // 16, model_width // 8, model_width // 4, model_width // 2, model_width]


def split_gated(flat_weights, model_width):
    widths = gated_widths(model_width)
    matrices = []
    cursor = 0
    for section_idx in range(4):
        amount = widths[section_idx] * widths[section_idx + 1]
        matrices.append(
            flat_weights[cursor : cursor + amount].reshape(
                widths[section_idx], widths[section_idx + 1]
            )
        )
        cursor = cursor + amount
    return matrices


def outer_sum(left_op, right_op):
    return lax.dot_general(
        left_op, right_op, (((0,), (0,)), ((), ())), preferred_element_type=jnp.float32
    )


def times_transpose(left_op, right_op):
    return lax.dot_general(
        left_op, right_op, (((1,), (1,)), ((), ())), preferred_element_type=jnp.float32
    )


def forward_block(residual, weights, kernel, image_ids, factors):
    in_weight, out_weight, up_weight, down_weight, gated_flat, gain_vec, bias_vec, scale_vec = (
        weights
    )
    model_width = residual.shape[1]
    widths = gated_widths(model_width)
    gain_full = gain_vec.astype(jnp.float32)
    bias_full = bias_vec.astype(jnp.float32)
    scale_full = scale_vec.astype(jnp.float32)
    normed = layer_norm(residual, gain_full[:model_width], bias_full[:model_width]).astype(
        jnp.bfloat16
    )
    mixed_all = jnp.dot(normed, in_weight, preferred_element_type=jnp.float32)
    scaled = depthwise(mixed_all[:, widths[0] :], kernel.astype(jnp.float32), image_ids)
    product = mixed_all[:, : widths[0]] * scaled[:, : widths[0]]
    lowered = []
    inners = []
    cursor = widths[0]
    for section_idx, matrix in enumerate(split_gated(gated_flat, model_width)):
        product_low = product.astype(jnp.bfloat16)
        inner_out = jnp.dot(product_low, matrix, preferred_element_type=jnp.float32)
        lowered.append(product_low)
        inners.append(inner_out)
        product = inner_out * scaled[:, cursor : cursor + widths[section_idx + 1]]
        cursor = cursor + widths[section_idx + 1]
    lowered.append(product.astype(jnp.bfloat16))
    branch = jnp.dot(lowered[4], out_weight, preferred_element_type=jnp.float32)
    middle = residual + factors[:, 0:1] * scale_full[:model_width] * branch
    normed_two = layer_norm(middle, gain_full[model_width:], bias_full[model_width:]).astype(
        jnp.bfloat16
    )
    hidden = jnp.dot(normed_two, up_weight, preferred_element_type=jnp.float32)
    activated = jax.nn.gelu(hidden).astype(jnp.bfloat16)
    expanded = jnp.dot(activated, down_weight, preferred_element_type=jnp.float32)
    output = middle + factors[:, 1:2] * scale_full[model_width:] * expanded
    retained = (
        residual,
        normed,
        mixed_all,
        scaled,
        lowered,
        inners,
        branch,
        middle,
        normed_two,
        hidden,
        activated,
        expanded,
    )
    return (output, retained)


def backward_block(grad_out, retained, weights, kernel, image_ids, factors):
    (
        residual,
        normed,
        mixed_all,
        scaled,
        lowered,
        inners,
        branch,
        middle,
        normed_two,
        hidden,
        activated,
        expanded,
    ) = retained
    in_weight, out_weight, up_weight, down_weight, gated_flat, gain_vec, bias_vec, scale_vec = (
        weights
    )
    model_width = residual.shape[1]
    widths = gated_widths(model_width)
    gain_full = gain_vec.astype(jnp.float32)
    bias_full = bias_vec.astype(jnp.float32)
    scale_full = scale_vec.astype(jnp.float32)
    first_factor = factors[:, 0:1]
    second_factor = factors[:, 1:2]
    scale_two_grad = jnp.sum(grad_out * second_factor * expanded, axis=0)
    expanded_grad = (grad_out * second_factor * scale_full[model_width:]).astype(jnp.bfloat16)
    down_weight_grad = outer_sum(activated, expanded_grad)
    activated_grad = times_transpose(expanded_grad, down_weight)
    unused_gelu, gelu_pull = jax.vjp(jax.nn.gelu, hidden)
    hidden_grad = gelu_pull(activated_grad)[0].astype(jnp.bfloat16)
    up_weight_grad = outer_sum(normed_two, hidden_grad)
    normed_two_grad = times_transpose(hidden_grad, up_weight)
    unused_two, second_pull = jax.vjp(
        layer_norm, middle, gain_full[model_width:], bias_full[model_width:]
    )
    middle_extra, gain_two_grad, bias_two_grad = second_pull(normed_two_grad)
    middle_grad = grad_out + middle_extra
    scale_one_grad = jnp.sum(middle_grad * first_factor * branch, axis=0)
    branch_grad = (middle_grad * first_factor * scale_full[:model_width]).astype(jnp.bfloat16)
    out_weight_grad = outer_sum(lowered[4], branch_grad)
    product_grad = times_transpose(branch_grad, out_weight)
    matrices = split_gated(gated_flat, model_width)
    starts = [0]
    for width_here in widths:
        starts.append(starts[-1] + width_here)
    gated_parts = [None, None, None, None]
    scaled_parts = [None, None, None, None, None]
    for section_idx in reversed(range(4)):
        scaled_part = scaled[:, starts[section_idx + 1] : starts[section_idx + 2]]
        inner_grad = (product_grad * scaled_part).astype(jnp.bfloat16)
        scaled_parts[section_idx + 1] = product_grad * inners[section_idx]
        gated_parts[section_idx] = outer_sum(lowered[section_idx], inner_grad)
        product_grad = times_transpose(inner_grad, matrices[section_idx])
    head_grad = product_grad * scaled[:, : widths[0]]
    scaled_parts[0] = product_grad * mixed_all[:, : widths[0]]
    scaled_grad = jnp.concatenate(scaled_parts, axis=1)
    unused_conv, conv_pull = jax.vjp(
        partial(depthwise, image_ids=image_ids),
        mixed_all[:, widths[0] :],
        kernel.astype(jnp.float32),
    )
    rest_grad, kernel_weight_grad = conv_pull(scaled_grad)
    mixed_grad = jnp.concatenate([head_grad, rest_grad], axis=1).astype(jnp.bfloat16)
    in_weight_grad = outer_sum(normed, mixed_grad)
    normed_grad = times_transpose(mixed_grad, in_weight)
    unused_one, first_pull = jax.vjp(
        layer_norm, residual, gain_full[:model_width], bias_full[:model_width]
    )
    residual_extra, gain_one_grad, bias_one_grad = first_pull(normed_grad)
    input_grad = middle_grad + residual_extra
    gated_grad = jnp.concatenate([matrix_grad.reshape(-1) for matrix_grad in gated_parts])
    weight_grads = (
        in_weight_grad,
        out_weight_grad,
        up_weight_grad,
        down_weight_grad,
        gated_grad,
        jnp.concatenate([gain_one_grad, gain_two_grad]),
        jnp.concatenate([bias_one_grad, bias_two_grad]),
        jnp.concatenate([scale_one_grad, scale_two_grad]),
    )
    return (input_grad, weight_grads, kernel_weight_grad)


def per_device(
    pixels,
    cotangent,
    image_plan,
    keep_mask,
    norm_gains,
    norm_biases,
    layer_scales,
    in_proj,
    depth_kernel,
    gated_weights,
    out_proj,
    up_proj,
    down_proj,
):
    tokens_here = pixels.shape[0]
    edge_cells = math.isqrt(tokens_here)
    tile_edge = edge_cells // 2
    layer_count = in_proj.shape[0]
    image_ids, factors = branch_factors(image_plan[0], keep_mask[0], edge_cells, tile_edge)
    residual = pixels.astype(jnp.float32)
    retained_all = []
    for layer_idx in range(layer_count):
        weights = (
            lax.all_gather(in_proj[layer_idx], ("dp", "fsdp"), axis=0, tiled=True),
            lax.all_gather(out_proj[layer_idx], ("dp", "fsdp"), axis=0, tiled=True),
            lax.all_gather(up_proj[layer_idx], ("dp", "fsdp"), axis=0, tiled=True),
            lax.all_gather(down_proj[layer_idx], ("dp", "fsdp"), axis=0, tiled=True),
            lax.all_gather(gated_weights[layer_idx], ("dp", "fsdp"), axis=0, tiled=True),
            lax.all_gather(norm_gains[layer_idx], ("dp", "fsdp"), axis=0, tiled=True),
            lax.all_gather(norm_biases[layer_idx], ("dp", "fsdp"), axis=0, tiled=True),
            lax.all_gather(layer_scales[layer_idx], ("dp", "fsdp"), axis=0, tiled=True),
        )
        kernel = lax.all_gather(depth_kernel[layer_idx], "fsdp", axis=0, tiled=True)
        residual, retained = forward_block(
            residual, weights, kernel, image_ids, factors[:, 2 * layer_idx : 2 * layer_idx + 2]
        )
        retained_all.append(retained)
    result = residual.astype(jnp.bfloat16)
    grad_now = cotangent.astype(jnp.float32)
    layer_grads = [None] * layer_count
    kernel_grads = [None] * layer_count
    for layer_idx in reversed(range(layer_count)):
        weights = (
            lax.all_gather(in_proj[layer_idx], ("dp", "fsdp"), axis=0, tiled=True),
            lax.all_gather(out_proj[layer_idx], ("dp", "fsdp"), axis=0, tiled=True),
            lax.all_gather(up_proj[layer_idx], ("dp", "fsdp"), axis=0, tiled=True),
            lax.all_gather(down_proj[layer_idx], ("dp", "fsdp"), axis=0, tiled=True),
            lax.all_gather(gated_weights[layer_idx], ("dp", "fsdp"), axis=0, tiled=True),
            lax.all_gather(norm_gains[layer_idx], ("dp", "fsdp"), axis=0, tiled=True),
            lax.all_gather(norm_biases[layer_idx], ("dp", "fsdp"), axis=0, tiled=True),
            lax.all_gather(layer_scales[layer_idx], ("dp", "fsdp"), axis=0, tiled=True),
        )
        kernel = lax.all_gather(depth_kernel[layer_idx], "fsdp", axis=0, tiled=True)
        grad_now, weight_grads, kernel_weight_grad = backward_block(
            grad_now,
            retained_all[layer_idx],
            weights,
            kernel,
            image_ids,
            factors[:, 2 * layer_idx : 2 * layer_idx + 2],
        )
        kernel_grads[layer_idx] = kernel_weight_grad
        layer_grads[layer_idx] = (
            lax.psum_scatter(weight_grads[0], ("dp", "fsdp"), scatter_dimension=0, tiled=True),
            lax.psum_scatter(weight_grads[1], ("dp", "fsdp"), scatter_dimension=0, tiled=True),
            lax.psum_scatter(weight_grads[2], ("dp", "fsdp"), scatter_dimension=0, tiled=True),
            lax.psum_scatter(weight_grads[3], ("dp", "fsdp"), scatter_dimension=0, tiled=True),
            lax.psum_scatter(weight_grads[4], ("dp", "fsdp"), scatter_dimension=0, tiled=True),
            lax.psum_scatter(weight_grads[5], ("dp", "fsdp"), scatter_dimension=0, tiled=True),
            lax.psum_scatter(weight_grads[6], ("dp", "fsdp"), scatter_dimension=0, tiled=True),
            lax.psum_scatter(weight_grads[7], ("dp", "fsdp"), scatter_dimension=0, tiled=True),
        )
    stacked = tuple(
        (
            jnp.stack([layer_grads[layer_idx][member] for layer_idx in range(layer_count)])
            for member in range(8)
        )
    )
    kernel_stack = jnp.stack(kernel_grads)
    kernel_share = lax.psum_scatter(
        kernel_stack.astype(jnp.bfloat16), "fsdp", scatter_dimension=1, tiled=True
    ).astype(jnp.float32)
    kernel_summed = lax.psum(kernel_share, "dp")
    return (
        result,
        grad_now,
        stacked[5],
        stacked[6],
        stacked[7],
        stacked[0],
        kernel_summed,
        stacked[4],
        stacked[1],
        stacked[2],
        stacked[3],
    )


def solution(mesh):
    in_specs = (
        P(("dp", "fsdp"), None),
        P(("dp", "fsdp"), None),
        P(("dp", "fsdp"), None),
        P(("dp", "fsdp"), None),
        P(None, ("dp", "fsdp")),
        P(None, ("dp", "fsdp")),
        P(None, ("dp", "fsdp")),
        P(None, ("dp", "fsdp"), None),
        P(None, "fsdp", None),
        P(None, ("dp", "fsdp")),
        P(None, ("dp", "fsdp"), None),
        P(None, ("dp", "fsdp"), None),
        P(None, ("dp", "fsdp"), None),
    )
    out_specs = (
        P(("dp", "fsdp"), None),
        P(("dp", "fsdp"), None),
        P(None, ("dp", "fsdp")),
        P(None, ("dp", "fsdp")),
        P(None, ("dp", "fsdp")),
        P(None, ("dp", "fsdp"), None),
        P(None, "fsdp", None),
        P(None, ("dp", "fsdp")),
        P(None, ("dp", "fsdp"), None),
        P(None, ("dp", "fsdp"), None),
        P(None, ("dp", "fsdp"), None),
    )
    return jax.shard_map(
        fast_device if fits(mesh) else per_device, mesh=mesh, in_specs=in_specs, out_specs=out_specs, check_vma=False
    )
```

```python
from functools import partial
import math

import jax
import jax.numpy as jnp
import numpy as np
from jax import lax
from jax.experimental import pallas as pl
from jax.experimental.pallas import tpu as pltpu
from jax.sharding import PartitionSpec as P

BF = jnp.bfloat16
F32 = jnp.float32
HALF = 352
SIDE = 512
Z_ORDER = (0, 2, 1, 3)
WIN = 12
VMEM_BYTES = 14 * 1024 * 1024


def half_spectrum(size):
    seen = set()
    kept = []
    for row in range(size):
        for col in range(size):
            if ((-row) % size, (-col) % size) in seen:
                continue
            seen.add((row, col))
            kept.append((row, col))
    return kept


def fourier_tables(edge):
    tile = edge // 2
    plans = [
        [(0, 0, tile), (0, tile, tile), (tile, 0, tile), (tile, tile, tile)],
        [(0, 0, edge)],
    ]
    forward = np.zeros((2, 2 * HALF, edge * edge), np.float32)
    taps = np.zeros((2, 2 * HALF, 64), np.float32)
    for which, tiles in enumerate(plans):
        at = 0
        for top, left, extent in tiles:
            size = extent + 3
            rows, cols = np.meshgrid(np.arange(extent), np.arange(extent), indexing="ij")
            slots = ((rows + top) * edge + cols + left).reshape(-1)
            tap_rows, tap_cols = np.meshgrid(np.arange(7) - 3, np.arange(7) - 3, indexing="ij")
            for fr, fc in half_spectrum(size):
                angle = 2 * np.pi * ((fr * rows + fc * cols) % size) / size
                forward[which, at, slots] = np.cos(angle).reshape(-1)
                forward[which, HALF + at, slots] = np.sin(angle).reshape(-1)
                weight = (1.0 if (fr, fc) == (0, 0) else 2.0) / (3.0 * size * size)
                angle = 2 * np.pi * ((fr * tap_rows + fc * tap_cols) % size) / size
                taps[which, at, :49] = weight * np.cos(angle).reshape(-1)
                taps[which, HALF + at, :49] = weight * np.sin(angle).reshape(-1)
                at += 1
        assert at <= HALF
    return (
        forward,
        np.ascontiguousarray(forward.transpose(0, 2, 1)),
        taps,
        np.ascontiguousarray(taps.transpose(0, 2, 1)),
    )


def mm(left, right):
    return lax.dot_general(left, right, (((1,), (0,)), ((), ())), preferred_element_type=F32)


def mm_nt(left, right):
    return lax.dot_general(left, right, (((1,), (1,)), ((), ())), preferred_element_type=F32)


def mm_tn(left, right):
    return lax.dot_general(left, right, (((0,), (0,)), ((), ())), preferred_element_type=F32)


def iota2(shape, dim):
    return lax.broadcasted_iota(jnp.int32, shape, dim)


def pixel_factor(plan_ref, keep_ref, column, edge, tile):
    slot = iota2((edge * edge, 1), 0)
    row = jnp.floor((slot.astype(F32) + 0.5) * (1.0 / edge)).astype(jnp.int32)
    col = slot - row * edge
    quarter = jnp.where(row >= tile, 2, 0) + jnp.where(col >= tile, 1, 0)
    large = plan_ref[0, 0]
    count = plan_ref[0, 1]
    width = keep_ref.shape[1] // 4
    total = jnp.zeros((edge * edge, 1), F32)
    for t in range(4):
        kept = keep_ref[0, t * width + column].astype(F32) * 1.25
        first = keep_ref[0, column].astype(F32) * 1.25
        here = jnp.where(t < count, kept, 0.0)
        here = jnp.where(large == 1, first, here)
        total = jnp.where(quarter == t, here, total)
    return total


def norm_stats(values):
    center = values - jnp.mean(values, axis=-1, keepdims=True)
    rstd = lax.rsqrt(jnp.mean(center * center, axis=-1, keepdims=True) + 1e-06)
    return center * rstd, rstd


def norm_back(grad, normal, rstd, gain):
    inner = grad * gain
    return rstd * (
        inner
        - jnp.mean(inner, axis=-1, keepdims=True)
        - normal * jnp.mean(inner * normal, axis=-1, keepdims=True)
    )


def window_map(shards, per):
    shape = (HALF, shards * 16)
    r = iota2(shape, 0)
    c = iota2(shape, 1)
    shard = lax.shift_right_logical(c, 4)
    t = c & 15
    flat_row = jnp.where(
        r < 256, r + 84, jnp.where(r < 320, r - 236, jnp.where(r < 336, r - 316, r - 336))
    )
    start = lax.shift_right_logical(shard * (per // 64), 3)
    gated = (t < WIN) & (r < 340) & (flat_row == start + t)
    norm = r - 344
    second = jnp.where(shard >= shards // 2, 1, 0)
    vec = (norm >= 0) & (norm < 6) & (t == WIN + lax.shift_right_arithmetic(norm, 1)) & ((norm & 1) == second)
    return jnp.where(gated | vec, 1.0, 0.0).astype(BF)


def spread(rows, cols, stride, offset, shift, count=None):
    r = iota2((rows, cols), 0) - shift
    c = iota2((rows, cols), 1)
    hit = r == stride * c + offset
    if count is not None:
        hit = hit & (c < count)
    return jnp.where(hit, 1.0, 0.0).astype(BF)


def lanes_from(values, low, high):
    lane = iota2(values.shape, 1)
    return jnp.where((lane >= low) & (lane < high), values, jnp.zeros_like(values))


def gated_matrices(flat):
    g2 = mm(spread(128, 64, 2, 0, 0), flat[256:320, 0:256]) + mm(
        spread(128, 64, 2, 1, 0), flat[256:320, 256:512]
    )
    g1 = jnp.zeros((128, 128), F32)
    for h in range(4):
        g1 = g1 + mm(spread(128, 16, 4, h, 64), flat[320:336, 128 * h : 128 * h + 128])
    g0 = jnp.zeros((128, 128), F32)
    for t in range(4):
        part = flat[336:352, 128 * t : 128 * t + 128].astype(F32)
        part = jnp.where(iota2(part.shape, 0) < 4, part, 0.0)
        odd = lanes_from(part, 64, 128).astype(BF)
        even = lanes_from(pltpu.roll(part, 64, 1), 64, 128).astype(BF)
        g0 = g0 + mm(spread(128, 16, 8, 2 * t, 32), even) + mm(spread(128, 16, 8, 2 * t + 1, 32), odd)
    return g0.astype(BF), g1.astype(BF), g2.astype(BF)


def matrix(w_ref, row):
    return w_ref[:, :, :, pl.ds(row, 16), :].reshape(SIDE, SIDE)


def down_rows(w_ref, j):
    return w_ref[j, :, :, 64:128, :].reshape(SIDE, SIDE)


def gelu_parts(hidden):
    root = math.sqrt(2.0 / math.pi)
    square = hidden * hidden
    bent = jnp.tanh(root * hidden * (1.0 + 0.044715 * square))
    half = 0.5 * (1.0 + bent)
    value = hidden * half
    slope = half + 0.5 * hidden * (1.0 - bent * bent) * (root * (1.0 + 0.134145 * square))
    return value, slope


def emit_block(read, outs, rows, place):
    yx = place[0]
    z = place[2]
    for sel in range(2):
        dest = place[1] ^ sel
        first = jnp.where(dest == 0, 1, 2)
        for r1 in range(2):
            for r2 in range(2):
                spot = yx ^ (r1 * first) ^ (r2 * (3 - first))
                for at, zrel in enumerate(Z_ORDER):
                    values = read(spot, dest, z ^ zrel)
                    outs[sel][r1 * 8 + r2 * 4 + at, rows, :] = values


def emit_rows(value, rows_ref, outs, row, place):
    rows_ref[...] = value.astype(BF).reshape(rows_ref.shape)
    emit_block(lambda spot, core, z: rows_ref[spot * 8 + core * 4 + z], outs, pl.ds(row, 16), place)


def tables_kernel(plan, *rest):
    mode = plan[0, 0]
    sources, targets, sems = rest[:4], rest[-5:-1], rest[-1]
    copies = [
        pltpu.make_async_copy(src.at[mode], dst, sems.at[n]) for n, (src, dst) in enumerate(zip(sources, targets))
    ]
    for copy in copies:
        copy.start()
    for copy in copies:
        copy.wait()


def mix_forward_kernel(
    layer, edge, per, plan, keep, x_ref, taps_ref, w_ref, forward, back, tapmap, *rest
):
    m1_ref, a0_ref, q_ref, z_ref, p_ref, y_ref, spec_ref, kern_ref, flat_ref, g0_ref, g1_ref, g2_ref, norm_ref = rest[
        -14:-1
    ]
    a_low = rest[-1]
    shards = 32
    factor = pixel_factor(plan, keep, 2 * layer, edge, edge // 2)
    picks = window_map(shards, per)
    flat = mm(picks, matrix(w_ref, 48))
    norm_ref[...] = flat[344:352]
    flat_low = flat.astype(BF)
    flat_ref[...] = flat_low
    g0, g1, g2 = gated_matrices(flat_low)
    g0_ref[...] = g0
    g1_ref[...] = g1
    g2_ref[...] = g2
    x = x_ref[...].astype(F32)
    normal, unused = norm_stats(x)
    u = (normal * flat[344:345] + flat[346:347]).astype(BF)
    for half in range(2):
        a = mm(u, matrix(w_ref, 16 * half))
        a_low[:, SIDE * half : SIDE * half + SIDE] = a.astype(BF)
        if half == 0:
            a0_ref[...] = a[:, :128]

    def channels(j):
        at = slice(j * SIDE, j * SIDE + SIDE)
        kernel = mm(tapmap[...], taps_ref[:, at])
        kern_ref[:, at] = kernel.astype(BF)
        spec = mm(forward[...], a_low[:, at])
        spec_ref[:, at] = spec.astype(BF)
        kr, ki = kernel[:HALF], kernel[HALF:]
        xc, xs = spec[:HALF], spec[HALF:]
        product = jnp.concatenate([xc * kr + xs * ki, xs * kr - xc * ki], axis=0).astype(BF)
        q_ref[:, at] = mm(back[...], product).astype(BF)

    for j in range(2):
        channels(j)
    q0 = q_ref[:, 0:128].astype(F32)
    p0 = lanes_from(pltpu.roll(a0_ref[...], 32, 1) * q0, 32, 64)
    z = mm(p0.astype(BF), g0)
    z_ref[:, 0:128] = z.astype(BF)
    p = z * q0
    p_ref[:, 0:128] = (p0 + p).astype(BF)
    z = mm(p.astype(BF), g1)
    z_ref[:, 128:256] = z.astype(BF)
    p = (z * q_ref[:, 128:256].astype(F32)).astype(BF)
    p_ref[:, 128:256] = p
    z = mm(p, g2)
    z_ref[:, 256:512] = z.astype(BF)
    p = (z * q_ref[:, 256:512].astype(F32)).astype(BF)
    p_ref[:, 256:512] = p
    z = mm(p, flat_ref[0:256, :])
    z_ref[:, 512:1024] = z.astype(BF)
    p = (z * q_ref[:, 512:1024].astype(F32)).astype(BF)
    p_ref[:, 512:1024] = p
    y = mm(p, matrix(w_ref, 32))
    y_ref[...] = y.astype(BF)
    m1_ref[...] = x + factor * flat[348:349] * y


def feed_forward_kernel(layer, edge, last, plan, keep, m1_ref, norm_ref, w_ref, *rest):
    x_ref, e_ref, slope_ref, f_ref, total = rest[-5:]
    factor = pixel_factor(plan, keep, 2 * layer + 1, edge, edge // 2)
    m1 = m1_ref[...]
    normal, unused = norm_stats(m1)
    v = (normal * norm_ref[1:2] + norm_ref[3:4]).astype(BF)
    total[...] = jnp.zeros_like(total)

    def hidden(j):
        at = slice(j * SIDE, j * SIDE + SIDE)
        value, slope = gelu_parts(mm(v, matrix(w_ref, j * 16)))
        e = value.astype(BF)
        e_ref[:, at] = e
        slope_ref[:, at] = slope.astype(BF)
        total[...] += mm(e, down_rows(w_ref, j))

    for j in range(4):
        hidden(j)
    f_ref[...] = total[...].astype(BF)
    x_ref[...] = (m1 + factor * norm_ref[5:6] * total[...]).astype(x_ref.dtype)


def feed_back_kernel(
    layer, edge, place, plan, keep, dx_ref, m1_ref, e_ref, slope_ref, f_ref, norm_ref, w_ref, *rest
):
    dm1_ref, *outs, small_ref, dv_ref, rows_ref, down_ref = rest[-7:]
    factor = pixel_factor(plan, keep, 2 * layer + 1, edge, edge // 2)
    dx = dx_ref[...].astype(F32)
    scaled = dx * factor
    small_ref[...] = jnp.zeros_like(small_ref)
    small_ref[5:6] = jnp.sum(scaled * f_ref[...].astype(F32), axis=0, keepdims=True)
    df = (scaled * norm_ref[5:6]).astype(BF)
    normal, rstd = norm_stats(m1_ref[...])
    v = (normal * norm_ref[1:2] + norm_ref[3:4]).astype(BF)
    dv_ref[...] = jnp.zeros_like(dv_ref)

    def hidden(j):
        at = slice(j * SIDE, j * SIDE + SIDE)
        e = e_ref[:, at]
        dh = (slope_ref[:, at].astype(F32) * mm_nt(df, down_rows(w_ref, j))).astype(BF)
        dv_ref[...] += mm_nt(dh, matrix(w_ref, j * 16))
        emit_rows(mm_tn(v, dh), rows_ref, outs, j * 16, place)
        down_ref[j] = mm_tn(e, df).astype(BF).reshape(down_ref.shape[1:])

    for j in range(4):
        hidden(j)
    emit_block(lambda spot, core, z: down_ref[spot, core, z], outs, slice(64, 128), place)
    dv = dv_ref[...]
    small_ref[1:2] = jnp.sum(dv * normal, axis=0, keepdims=True)
    small_ref[3:4] = jnp.sum(dv, axis=0, keepdims=True)
    dm1_ref[...] = dx + norm_back(dv, normal, rstd, norm_ref[1:2])


def chain_back_kernel(
    layer,
    edge,
    plan,
    keep,
    dm1_ref,
    a0_ref,
    q_ref,
    z_ref,
    p_ref,
    y_ref,
    flat_ref,
    g0_ref,
    g1_ref,
    g2_ref,
    norm_ref,
    small_ref,
    w_ref,
    *rest,
):
    dq_ref, dhead_ref, dflat_ref, dout_ref = rest[-4:]
    factor = pixel_factor(plan, keep, 2 * layer, edge, edge // 2)
    scaled = dm1_ref[...] * factor
    dscale = jnp.sum(scaled * y_ref[...].astype(F32), axis=0, keepdims=True)
    dy = (scaled * norm_ref[4:5]).astype(BF)
    dout_ref[...] = mm_tn(p_ref[:, 512:1024], dy).astype(BF)

    def link(dp, low, high):
        dz = (dp * q_ref[:, low:high].astype(F32)).astype(BF)
        return dz, dp * z_ref[:, low:high].astype(F32)

    dp = mm_nt(dy, matrix(w_ref, 32))
    dz, dq = link(dp, 512, 1024)
    dq_ref[:, 512:1024] = dq.astype(BF)
    dflat_ref[0:256, :] = mm_tn(p_ref[:, 256:512], dz).astype(BF)
    dp = mm_nt(dz, flat_ref[0:256, :])
    dz, dq = link(dp, 256, 512)
    dq_ref[:, 256:512] = dq.astype(BF)
    dg2 = mm_tn(p_ref[:, 128:256], dz).astype(BF)
    for h in range(2):
        dflat_ref[256:320, 256 * h : 256 * h + 256] = mm_tn(spread(128, 64, 2, h, 0), dg2).astype(BF)
    dp = mm_nt(dz, g2_ref[...])
    dz, dq = link(dp, 128, 256)
    dq_ref[:, 128:256] = dq.astype(BF)
    p01 = p_ref[:, 0:128]
    dg1 = mm_tn(p01, dz).astype(BF)
    for h in range(4):
        dflat_ref[320:336, 128 * h : 128 * h + 128] = mm_tn(spread(128, 16, 4, h, 64), dg1).astype(BF)
    dp = mm_nt(dz, g1_ref[...])
    dz, dq1 = link(dp, 0, 128)
    dg0 = mm_tn(p01, dz).astype(BF)
    norm_rows = jnp.concatenate(
        [jnp.zeros((8, SIDE), F32), small_ref[0:4], dscale, small_ref[5:8]], axis=0
    )
    for t in range(4):
        even = mm_tn(spread(128, 16, 8, 2 * t, 32, 4), dg0)
        odd = mm_tn(spread(128, 16, 8, 2 * t + 1, 32, 4), dg0)
        at = slice(128 * t, 128 * t + 128)
        dflat_ref[336:352, at] = (
            lanes_from(odd, 64, 128) + pltpu.roll(lanes_from(even, 64, 128), 64, 1) + norm_rows[:, at]
        ).astype(BF)
    dp = mm_nt(dz, g0_ref[...])
    head = lanes_from(pltpu.roll(a0_ref[...], 32, 1), 32, 64)
    dq_ref[:, 0:128] = (dq1 + dp * head).astype(BF)
    dhead_ref[...] = pltpu.roll(lanes_from(dp * q_ref[:, 0:128].astype(F32), 32, 64), 96, 1)


def spectrum_back_kernel(place, spec_ref, kern_ref, dq_ref, dhead_ref, forward, back, tapback, *rest):
    da_ref, kernel_out, dtaps_ref = rest[-3:]
    dtaps_ref[:, 1024:] = jnp.zeros((64, 128), F32)

    def channels(j):
        at = slice(j * SIDE, j * SIDE + SIDE)
        kernel = kern_ref[:, at].astype(F32)
        grad = mm(forward[...], dq_ref[:, at])
        spec = spec_ref[:, at].astype(F32)
        kr, ki = kernel[:HALF], kernel[HALF:]
        dc, ds = grad[:HALF], grad[HALF:]
        xc, xs = spec[:HALF], spec[HALF:]
        dspec = jnp.concatenate([dc * kr - ds * ki, dc * ki + ds * kr], axis=0).astype(BF)
        da_ref[:, at] = mm(back[...], dspec).astype(BF)
        dkernel = jnp.concatenate([dc * xc + ds * xs, dc * xs - ds * xc], axis=0).astype(BF)
        dtaps_ref[:, at] = mm(tapback[...], dkernel)

    for j in range(2):
        channels(j)
    da_ref[:, 0:128] = (da_ref[:, 0:128].astype(F32) + dhead_ref[...]).astype(BF)
    count = (1024 - 32) // 4
    for shard in range(4):
        low = 32 + count * shard
        rel = shard ^ place[2]
        at = (rel & 1) * 2 + (rel >> 1)
        kernel_out[at, :, 0:256] = dtaps_ref[0:32, low : low + 256].astype(BF)
        kernel_out[at, :, 256:512] = dtaps_ref[32:64, low : low + 256].astype(BF)


def mix_back_kernel(per, place, dm1_ref, x_ref, norm_ref, da_ref, dflat_ref, dout_ref, w_ref, *rest):
    dx_ref, *outs, rows_ref = rest[-4:]
    emit_rows(dout_ref[...], rows_ref, outs, 32, place)
    normal, rstd = norm_stats(x_ref[...].astype(F32))
    gain = norm_ref[0:1]
    u = (normal * gain + norm_ref[2:3]).astype(BF)
    du = jnp.zeros(dm1_ref.shape, F32)
    for half in range(2):
        da = da_ref[:, SIDE * half : SIDE * half + SIDE]
        emit_rows(mm_tn(u, da), rows_ref, outs, 16 * half, place)
        du = du + mm_nt(da, matrix(w_ref, 16 * half))
    dgain = jnp.sum(du * normal, axis=0, keepdims=True)
    dbias = jnp.sum(du, axis=0, keepdims=True)
    low = dflat_ref[336:352, :].astype(F32)
    row = iota2(low.shape, 0)
    low = jnp.where(row == 8, dgain, jnp.where(row == 10, dbias, low))
    dflat = jnp.concatenate([dflat_ref[0:336, :], low.astype(BF)], axis=0)
    emit_rows(mm_tn(window_map(32, per), dflat), rows_ref, outs, 48, place)
    dx_ref[...] = dm1_ref[...] + norm_back(du, normal, rstd, gain)


def place_lanes(row, lanes, shift):
    pad = jnp.zeros((row.shape[0], lanes - row.shape[1]), F32)
    return pltpu.roll(jnp.concatenate([row.astype(F32), pad], axis=1), shift, 1)


def start_all(plans, sems, row=0):
    copies = [pltpu.make_async_copy(src, dst, sems.at[row + n]) for n, (src, dst) in enumerate(plans)]
    for copy in copies:
        copy.start()
    return copies


def mix_plans(layer, in_hbm, out_hbm, gated_hbm, gain_hbm, bias_hbm, scale_hbm, pack_ref, parts):
    gated_ref, gain_ref, bias_ref, scale_ref = parts
    return [
        (gated_hbm, gated_ref),
        (gain_hbm, gain_ref),
        (bias_hbm, bias_ref),
        (scale_hbm, scale_ref),
        (in_hbm.at[layer, :, pl.ds(0, SIDE)], pack_ref.at[pl.ds(0, 16)]),
        (in_hbm.at[layer, :, pl.ds(SIDE, SIDE)], pack_ref.at[pl.ds(16, 16)]),
        (out_hbm.at[layer], pack_ref.at[pl.ds(32, 16)]),
    ]


def feed_plans(layer, up_hbm, down_hbm, pack_ref, row):
    plans = [
        (up_hbm.at[layer, :, pl.ds(SIDE * b, SIDE)], pack_ref.at[pl.ds(row + 16 * b, 16)]) for b in range(4)
    ]
    return plans + [(down_hbm.at[layer], pack_ref.at[pl.ds(row + 64, 64)])]


def window_rows(layer, place, pack_ref, parts):
    gated_ref, *vectors = parts
    gated = place_lanes(gated_ref[layer : layer + 1, :], WIN * SIDE, place[4])
    rows = [gated[:, SIDE * r : SIDE * r + SIDE] for r in range(WIN)]
    for ref in vectors:
        rows.append(place_lanes(ref[layer : layer + 1, :], SIDE, place[5]))
    rows.append(jnp.zeros((1, SIDE), F32))
    pack_ref[48:64, :] = jnp.concatenate(rows, axis=0).astype(BF)


def tap_rows(taps_ref, wide, pack_ref, row):
    wide[...] = jnp.zeros_like(wide)
    wide[: taps_ref.shape[0], : taps_ref.shape[1]] = taps_ref[...].astype(F32)
    turned = wide[...].T.astype(BF)
    pack_ref[row : row + 32, 0:256] = turned[0:32]
    pack_ref[row : row + 32, 256:512] = turned[32:64]


def pack_mix_kernel(layer, place, in_hbm, out_hbm, gated_hbm, gain_hbm, bias_hbm, scale_hbm, *rest):
    out, *parts, sems = rest[-6:]
    pack_ref = out.at[0]
    plans = mix_plans(layer, in_hbm, out_hbm, gated_hbm, gain_hbm, bias_hbm, scale_hbm, pack_ref, parts)
    for copy in start_all(plans, sems):
        copy.wait()
    window_rows(layer, place, pack_ref, parts)


def pack_feed_kernel(layer, up_hbm, down_hbm, taps_hbm, *rest):
    out, taps_ref, wide, sems = rest[-4:]
    pack_ref = out.at[0]
    plans = feed_plans(layer, up_hbm, down_hbm, pack_ref, 0) + [(taps_hbm.at[layer], taps_ref)]
    for copy in start_all(plans, sems):
        copy.wait()
    tap_rows(taps_ref, wide, pack_ref, 128)


def pack_both_kernel(
    layer, place, in_hbm, out_hbm, gated_hbm, gain_hbm, bias_hbm, scale_hbm, up_hbm, down_hbm, taps_hbm, *rest
):
    out, *parts, taps_ref, wide, sems = rest[-8:]
    pack_ref = out.at[0]
    plans = mix_plans(layer, in_hbm, out_hbm, gated_hbm, gain_hbm, bias_hbm, scale_hbm, pack_ref, parts)
    plans += feed_plans(layer, up_hbm, down_hbm, pack_ref, 64) + [(taps_hbm.at[layer], taps_ref)]
    for copy in start_all(plans, sems):
        copy.wait()
    window_rows(layer, place, pack_ref, parts)
    tap_rows(taps_ref, wide, pack_ref, 192)


def join_wide(split, wide, taps):
    wide[:, 0:128] = jnp.zeros((64, 128), F32)
    count = (1024 - 32) // 4
    for shard in range(4):
        low = 32 + count * shard
        wide[0:32, low : low + count] = split[shard, :, 0:count]
        wide[32:64, low : low + count] = split[shard, :, 256 : 256 + count]
    taps[...] = wide[...].astype(BF)


def split_kernel(place, mine, got, *rest):
    *parts, taps, split, wide = rest[-4:] if mine.shape[1] == 160 else rest[-5:]
    parts = parts[-1:] if mine.shape[1] == 160 else parts
    for at, zrel in enumerate(Z_ORDER):
        piece = mine[at] if at < 2 else got[at - 2]
        row = 0
        for part in parts:
            part[at] = piece[row : row + part.shape[1], :]
            row += part.shape[1]
        split[place[2] ^ zrel] = piece[row : row + 32, :].astype(F32)
    join_wide(split, wide, taps)


def four_kernel(mine, got2, got1, got3, *rest):
    for at, piece in enumerate((mine, got2, got1, got3)):
        rest[-1][at] = piece[0]


def join_kernel(mine, got, *rest):
    out = rest[-1]
    count = mine.shape[0]
    out[:count] = mine[...]
    out[count:] = got[...]


def place_kernel(place, mine, got, other_a, other_b, other_c, *rest):
    out = rest[-1]
    for number, pieces in enumerate(((mine, got), (other_a, other_b, other_c))):
        source = place[1] ^ number
        first = jnp.where(source == 0, 1, 2)
        at = 0
        for piece in pieces:
            for n in range(piece.shape[0]):
                spot = place[0] ^ (((at >> 2) & 1) * first) ^ ((at >> 3) * (3 - first))
                out[spot, source, place[2] ^ Z_ORDER[at & 3]] = piece[n]
                at += 1


def step_kernel(kept, got, *rest):
    stay, out = rest[-2:]
    count = out.shape[0]

    def one(n, carry):
        stay[n] = kept[n].astype(F32) + got[n].astype(F32)
        out[n] = (kept[count + n].astype(F32) + got[count + n].astype(F32)).astype(BF)
        return carry

    lax.fori_loop(0, count, one, 0)


def settle_kernel(kept, got, *rest):
    rest[-1][...] = kept[0] + got[0].astype(F32)


def merge_taps_kernel(kept, got, taps0, taps1, *rest):
    stay, out = rest[-2:]
    total = kept[...] + got[...].astype(F32)
    stay[:, 0:64] = total[0:2]
    out[:, 0:64] = total[2:4].astype(BF)
    for n, taps in enumerate((taps0, taps1)):
        row = 64 + 32 * n
        stay[:, row : row + 32] = taps[0:2].astype(F32)
        out[:, row : row + 32] = taps[2:4]


def settle_taps_kernel(kept, got, *rest):
    total, low = rest[-2:]
    total[...] = kept[0, 0:64] + got[0, 0:64].astype(F32)
    low[...] = (kept[0, 64:128] + got[0, 64:128].astype(F32)).astype(BF)


def tap_sum_kernel(mine, got, *rest):
    out = rest[-1]
    out[...] = (mine[...].astype(F32) + got[...].astype(F32)).astype(out.dtype)


def unpack_kernel(layers, place, *rest):
    gain_ref, bias_ref, scale_ref, in_ref, gated_ref, out_ref, up_ref, down_ref = rest[-8:]
    per = gated_ref.shape[1]
    for layer in range(layers):
        if layer == 0:
            mix = rest[0][0] + rest[1][0].astype(F32)
            feed = rest[2][0] + rest[3][0].astype(F32)
        else:
            mix, feed = rest[4], rest[5]
        in_ref[layer, :, :SIDE] = mix[0:16]
        in_ref[layer, :, SIDE:] = mix[16:32]
        out_ref[layer] = mix[32:48]
        flat = jnp.concatenate([mix[48 + r : 49 + r] for r in range(WIN)], axis=1)
        flat = pltpu.roll(flat, WIN * SIDE - place[4], 1)
        gated_ref[layer : layer + 1, :] = flat[:, :per]
        for n, ref in enumerate((gain_ref, bias_ref, scale_ref)):
            row = pltpu.roll(mix[48 + WIN + n : 49 + WIN + n], SIDE - place[5], 1)
            ref[layer : layer + 1, :] = row[:, : ref.shape[1]]
        for b in range(4):
            up_ref[layer, :, SIDE * b : SIDE * b + SIDE] = feed[16 * b : 16 * b + 16]
        down_ref[layer] = feed[64:128]


def copy_kernel(first, second, *rest):
    rest[-2][...] = first[...]
    rest[-1][...] = second[...]


def whole(shape, dtype):
    return jax.ShapeDtypeStruct(shape, dtype)


VM = pl.BlockSpec(memory_space=pltpu.VMEM)
SM = pl.BlockSpec(memory_space=pltpu.SMEM)
HB = pl.BlockSpec(memory_space=pltpu.HBM)
ANY = pl.BlockSpec(memory_space=pl.ANY)


FORWARD_ORDER = (
    "a01", "b01", "a03", "b02", "a04", "b03", "c11", "a05", "T", "a06", "mf0", "b04",
    "c12", "c13", "b05", "a14", "b06", "ff0", "b14", "a15", "a16", "mf1", "b15", "b16",
    "ff1",
)
BACKWARD_ORDER = (
    "fb1", "B10", "cb1", "B11", "sb1", "mb1", "A10", "fb0", "B12", "A11", "B00", "cb0",
    "B01", "sb0", "B13", "A12", "mb0", "A00", "B14", "A13", "B02", "A01", "o", "A14",
    "B03", "A02", "A15", "B04", "t1", "A03", "t2", "B15", "A04", "t3",
)
SCALE = 1.0
SMALL = 20.0
SMALL_F = 20.0
MICROS = {
    "mix_forward": 7.5,
    "feed_forward": 4.5,
    "feed_back": 8.0,
    "chain_back": 3.3,
    "spectrum_back": 5.8,
    "mix_back": 3.0,
}


EVENT_MICROS = {
    **dict.fromkeys(("mf0", "ff0", "mf1", "b06", "o"), 0.02),
    **dict.fromkeys(("a15", "a16", "b15", "b16", "sb0", "A11"), 5.0),
    **dict.fromkeys(("B00", "B02", "B03", "B04", "A02", "A03"), 40.0),
    **dict.fromkeys(("A04", "B14"), 10.0),
}


class Order:
    def __init__(self):
        self.last = ()
        self.event = None

    def cost(self, name):
        small = SMALL_F if self.event in FORWARD_ORDER else SMALL
        micros = EVENT_MICROS.get(self.event, MICROS.get(name, small) * SCALE)
        return pl.CostEstimate(flops=int(micros * 1e9), bytes_accessed=10_000, transcendentals=0)

    def hold(self, values):
        values = pl.pallas_call(
            lambda *refs: None,
            out_shape=tuple(whole(value.shape, value.dtype) for value in values),
            in_specs=[ANY] * (len(values) + 1),
            out_specs=(ANY,) * len(values),
            input_output_aliases={n: n for n in range(len(values))},
            compiler_params=pltpu.CompilerParams(vmem_limit_bytes=1024 * 1024),
            cost_estimate=self.cost("hold"),
            name="hold",
        )(*values, *self.last)
        self.last = (values[0],)
        return values

    def __call__(self, kernel, ins, in_specs, outs, scratch, name, limit=None):
        many = isinstance(outs, tuple)
        results = pl.pallas_call(
            kernel,
            out_shape=outs,
            in_specs=list(in_specs) + [ANY] * len(self.last),
            out_specs=jax.tree.map(lambda unused: VM, outs),
            scratch_shapes=scratch,
            compiler_params=pltpu.CompilerParams(vmem_limit_bytes=limit or VMEM_BYTES),
            cost_estimate=self.cost(name),
            name=name,
        )(*ins, *self.last)
        self.last = (min(results, key=lambda result: result.size * result.dtype.itemsize) if many else results,)
        return results


CORE = [(i, i ^ 1) for i in range(8)]
FIRST = [(i, i ^ (4 if i & 1 else 2)) for i in range(8)]
SECOND = [(i, i ^ (2 if i & 1 else 4)) for i in range(8)]
AXIS_X = [(i, i ^ 2) for i in range(8)]
AXIS_Y = [(i, i ^ 4) for i in range(8)]


def along(values, perm):
    return lax.ppermute(values, "dp", perm)


def along_z(values, k):
    return lax.ppermute(values, "fsdp", [(i, i ^ k) for i in range(4)])


class Gather:
    def __init__(self, order, pack):
        self.order = order
        self.have = pack
        self.come = None if pack is None else along_z(pack, 2)

    def join(self):
        shape = (2 * self.have.shape[0], *self.have.shape[1:])
        self.have = self.order(join_kernel, (self.have, self.come), [VM, VM], whole(shape, BF), [], "join")

    def second(self):
        self.join()
        self.come = along_z(self.have, 1)

    def third(self):
        self.join()
        self.first_axis()

    def first_axis(self):
        self.come = along(self.have, FIRST)
        self.other = [along(self.have, CORE)]

    def fourth(self):
        (self.come,) = self.order.hold([self.come])
        self.other.append(along(self.come, CORE))
        self.join()
        self.come = along(self.have, SECOND)

    def core(self):
        (self.come,) = self.order.hold([self.come])
        self.other.append(along(self.come, CORE))

    def finish(self, place):
        shape = (4, 2, 4, *self.have.shape[1:])
        self.whole = self.order(
            place_kernel, (place, self.have, self.come, *self.other), [SM] + [VM] * 5, whole(shape, BF), [], "place"
        )


class GatherDirect(Gather):
    def __init__(self, order, pack):
        self.order = order
        self.have = pack
        self.come = [along_z(pack, k) for k in Z_ORDER[1:]]

    def third(self):
        shape = (4, *self.have.shape[1:])
        self.have = self.order(four_kernel, (self.have, *self.come), [VM] * 4, whole(shape, BF), [], "four")
        self.first_axis()


def split(order, place, both, rows):
    *parts, taps = order(
        split_kernel,
        (place, both.have, both.come),
        [SM, VM, VM],
        (*[whole((4, count, SIDE), BF) for count in rows], whole((64, 1024), BF)),
        [pltpu.VMEM((4, 32, SIDE), F32), pltpu.VMEM((64, 1024), F32)],
        "split",
    )
    chains = []
    for part in parts:
        chains.append(Gather(order, None))
        chains[-1].have = part
        chains[-1].first_axis()
    return chains, taps


class Scatter:
    def __init__(self, order, keep, send):
        self.order = order
        self.keep = keep
        self.send = send
        self.moves = [
            lambda out: along(out, FIRST),
            lambda out: along(out, SECOND),
            lambda out: along_z(out, 1),
            lambda out: along_z(out, 2),
        ]

    def step(self):
        shape = (self.keep.shape[0] // 2, *self.keep.shape[1:])
        self.keep, out = self.order(
            step_kernel,
            (self.keep, self.come),
            [VM] * 2,
            (whole(shape, F32), whole(shape, BF)),
            [],
            "step",
        )
        self.come = self.moves.pop(0)(out)

    def start(self):
        (self.come,) = [along(part, CORE) for part in self.order.hold(self.send)]

    def settle(self):
        shape = self.keep.shape[1:]
        self.total = self.order(settle_kernel, (self.keep, self.come), [VM, VM], whole(shape, F32), [], "settle")


class TapSum(Scatter):
    def __init__(self, order, mix, taps):
        self.order = order
        self.moves = mix.moves[1:]
        self.keep, out = order(
            merge_taps_kernel,
            (mix.keep, mix.come, *taps),
            [VM] * 4,
            (whole((2, 128, SIDE), F32), whole((2, 128, SIDE), BF)),
            [],
            "merge_taps",
        )
        self.come = along_z(out, 1)

    def settle(self):
        self.total, self.low = self.order(
            settle_taps_kernel,
            (self.keep, self.come),
            [VM] * 2,
            (whole((64, SIDE), F32), whole((64, SIDE), BF)),
            [],
            "settle",
        )
        self.come = along(self.low, CORE)

    def taps(self, perm):
        self.low = self.order(
            tap_sum_kernel, (self.low, self.come), [VM] * 2, whole((64, SIDE), BF), [], "tap_sum"
        )
        self.come = along(self.low, perm)

    def final(self):
        total = self.order(tap_sum_kernel, (self.low, self.come), [VM] * 2, whole((64, SIDE), F32), [], "tap_sum")
        return total.reshape(2, 32, SIDE)


def fast_device(
    pixels,
    cotangent,
    image_plan,
    keep_mask,
    norm_gains,
    norm_biases,
    layer_scales,
    in_proj,
    depth_kernel,
    gated_weights,
    out_proj,
    up_proj,
    down_proj,
):
    pix, width = pixels.shape
    edge = math.isqrt(pix)
    per = gated_weights.shape[1]
    dp = lax.axis_index("dp")
    z = lax.axis_index("fsdp")
    me = dp * 4 + z
    phase = 64 * ((me * (per // 64)) % 8)
    place = jnp.stack([dp >> 1, dp & 1, z, me, phase, 32 * (me % 16)]).astype(jnp.int32)
    tables = [jnp.asarray(t, BF) for t in fourier_tables(edge)]
    count = depth_kernel.shape[1]
    order = Order()
    mix_ins = (place, in_proj, out_proj, gated_weights, norm_gains, norm_biases, layer_scales)
    mix_parts = [pltpu.VMEM(part.shape, BF) for part in mix_ins[3:]]
    tap_parts = [pltpu.VMEM(depth_kernel.shape[1:], BF), pltpu.VMEM((256, 128), F32)]

    def pack_mix(l):
        pack = order(
            partial(pack_mix_kernel, l),
            mix_ins,
            [SM] + [HB] * 6,
            whole((1, 64, SIDE), BF),
            mix_parts + [pltpu.SemaphoreType.DMA((7,))],
            "pack_mix",
            60 * 1024 * 1024,
        )
        return GatherDirect(order, pack)

    def pack_feed(l):
        pack = order(
            partial(pack_feed_kernel, l),
            (up_proj, down_proj, depth_kernel),
            [HB] * 3,
            whole((1, 160, SIDE), BF),
            tap_parts + [pltpu.SemaphoreType.DMA((6,))],
            "pack_feed",
        )
        return Gather(order, pack)

    def pack_both(l):
        pack = order(
            partial(pack_both_kernel, l),
            (*mix_ins, up_proj, down_proj, depth_kernel),
            [SM] + [HB] * 9,
            whole((1, 224, SIDE), BF),
            mix_parts + tap_parts + [pltpu.SemaphoreType.DMA((13,))],
            "pack_both",
        )
        return Gather(order, pack)

    def mix_forward(l, x, mix):
        ahead = ()
        return order(
            partial(mix_forward_kernel, l, edge, per),
            (image_plan, keep_mask, x, state[f"taps{l}"], mix.whole, *state["tables"][:3], *ahead),
            [SM, SM] + [VM] * (6 + len(ahead)),
            (
                whole((pix, width), F32),
                whole((pix, 128), F32),
                whole((pix, 1024), BF),
                whole((pix, 1024), BF),
                whole((pix, 1024), BF),
                whole((pix, width), BF),
                whole((2 * HALF, 1024), BF),
                whole((2 * HALF, 1024), BF),
                whole((HALF, SIDE), BF),
                whole((128, 128), BF),
                whole((128, 128), BF),
                whole((128, 256), BF),
                whole((8, SIDE), F32),
            ),
            [pltpu.VMEM((pix, 1024), BF)],
            "mix_forward",
        )

    def feed_forward(l, mixed, feed, last):
        return order(
            partial(feed_forward_kernel, l, edge, last),
            (image_plan, keep_mask, mixed[0], mixed[12], feed.whole),
            [SM, SM] + [VM] * 3,
            (
                whole((pix, width), BF if last else F32),
                whole((pix, 4 * SIDE), BF),
                whole((pix, 4 * SIDE), BF),
                whole((pix, width), BF),
            ),
            [pltpu.VMEM((pix, width), F32)],
            "feed_forward",
        )

    def feed_back(l, dx, mixed, fed, feed):
        return order(
            partial(feed_back_kernel, l, edge),
            (place, image_plan, keep_mask, dx, mixed[0], *fed[1:], mixed[12], feed.whole),
            [SM] * 3 + [VM] * 7,
            (
                whole((pix, width), F32),
                whole((16, 128, SIDE), BF),
                whole((16, 128, SIDE), BF),
                whole((8, SIDE), F32),
            ),
            [
                pltpu.VMEM((pix, width), F32),
                pltpu.VMEM((32, 16, SIDE), BF),
                pltpu.VMEM((4, 2, 4, 64, SIDE), BF),
            ],
            "feed_back",
        )

    def chain_back(l, dm1, mixed, small, mix):
        m1, a0, q, zs, ps, y, spec, kern, flat, g0, g1, g2, norms = mixed
        return order(
            partial(chain_back_kernel, l, edge),
            (image_plan, keep_mask, dm1, a0, q, zs, ps, y, flat, g0, g1, g2, norms, small, mix.whole),
            [SM] * 2 + [VM] * 13,
            (
                whole((pix, 1024), BF),
                whole((pix, 128), F32),
                whole((HALF, SIDE), BF),
                whole((SIDE, SIDE), BF),
            ),
            [],
            "chain_back",
        )

    def spectrum_back(mixed, dq, dhead):
        return order(
            spectrum_back_kernel,
            (place, mixed[6], mixed[7], dq, dhead, *state["tables"][:2], state["tables"][3]),
            [SM] + [VM] * 7,
            (whole((pix, 1024), BF), whole((4, 32, SIDE), BF)),
            [pltpu.VMEM((64, 1024 + 128), F32)],
            "spectrum_back",
        )

    def mix_back(dm1, x, mixed, da, dflat, dout, mix, ahead):
        return order(
            partial(mix_back_kernel, per),
            (place, dm1, x, mixed[12], da, dflat, dout, mix.whole, *ahead),
            [SM] + [VM] * (7 + len(ahead)),
            (whole((pix, width), F32), whole((16, 64, SIDE), BF), whole((16, 64, SIDE), BF)),
            [pltpu.VMEM((32, 16, SIDE), BF)],
            "mix_back",
        )

    state = {"x0": pixels, "dx2": cotangent}

    def load_tables():
        state["tables"] = order(
            tables_kernel,
            (image_plan, *tables),
            [SM] + [HB] * 4,
            tuple(whole(table.shape[1:], BF) for table in tables),
            [pltpu.SemaphoreType.DMA((4,))],
            "tables",
        )

    def pack(name):
        state[name] = {"a0": partial(pack_mix, 0), "b0": partial(pack_feed, 0), "c1": partial(pack_both, 1)}[name]()

    def gather(name, step):
        chain = state[name]
        if name == "c1" and step == 3:
            (state["a1"], state["b1"]), state["taps1"] = split(order, place, chain, (64, 128))
        elif name == "b0" and step == 3:
            (state["b0"],), state["taps0"] = split(order, place, chain, (128,))
        else:
            (chain.second, chain.third, chain.fourth)[step - 2]()

    def finish(name, step):
        if step == 5:
            state[name].core()
        else:
            state[name].finish(place)

    def forward_mix(l):
        state[f"mixed{l}"] = mix_forward(l, state[f"x{l}"], state[f"a{l}"])

    def forward_feed(l):
        state[f"fed{l}"] = feed_forward(l, state[f"mixed{l}"], state[f"b{l}"], l == 1)
        state[f"x{l + 1}"] = state[f"fed{l}"][0]

    def backward_feed(l):
        state["dm"], keep, *send, state["small"] = feed_back(
            l, state[f"dx{l + 1}"], state[f"mixed{l}"], state[f"fed{l}"], state[f"b{l}"]
        )
        state[f"feedsum{l}"] = Scatter(order, keep, send)

    def backward_chain(l):
        state["chain"] = chain_back(l, state["dm"], state[f"mixed{l}"], state["small"], state[f"a{l}"])

    def backward_spectrum(l):
        dq, dhead, dflat, dout = state["chain"]
        state["da"], state[f"dtaps{l}"] = spectrum_back(state[f"mixed{l}"], dq, dhead)

    def backward_mix(l):
        dq, dhead, dflat, dout = state["chain"]
        state[f"dx{l}"], keep, *send = mix_back(
            state["dm"],
            state[f"x{l}"],
            state[f"mixed{l}"],
            state["da"],
            dflat,
            dout,
            state[f"a{l}"],
            (state["b0"].whole,) if l == 1 else (),
        )
        state[f"mixsum{l}"] = Scatter(order, keep, send)

    def scatter(l, mix, step):
        chain = state[f"mixsum{l}" if mix else f"feedsum{l}"]
        if step == 0:
            chain.start()
        elif mix and l == 1 and step == 3:
            state["mixsum1"] = TapSum(order, chain, (state["dtaps0"], state["dtaps1"]))
        elif step == 5:
            chain.settle()
        else:
            chain.step()

    def sum_taps(step):
        if step == 3:
            state["taps"] = state["mixsum1"].final()
        else:
            state["mixsum1"].taps(AXIS_X if step == 1 else AXIS_Y)

    def copy_out():
        values = (state["x2"], state["dx0"])
        state["x2"], state["dx0"] = order(
            copy_kernel, values, [VM] * 2, tuple(whole(v.shape, v.dtype) for v in values), [], "copy_out"
        )

    events = {"T": load_tables, "o": copy_out}
    for name in ("a0", "b0", "c1"):
        events[name + "1"] = partial(pack, name)
    for name in ("a0", "b0", "c1", "a1", "b1"):
        for step in (5, 6):
            events[f"{name}{step}"] = partial(finish, name, step)
        for step in range(2, 5):
            events[f"{name}{step}"] = partial(gather, name, step)
    for l in range(2):
        for step in range(6):
            events[f"A{l}{step}"] = partial(scatter, l, True, step)
            events[f"B{l}{step}"] = partial(scatter, l, False, step)
        events[f"mf{l}"] = partial(forward_mix, l)
        events[f"ff{l}"] = partial(forward_feed, l)
        events[f"fb{l}"] = partial(backward_feed, l)
        events[f"cb{l}"] = partial(backward_chain, l)
        events[f"sb{l}"] = partial(backward_spectrum, l)
        events[f"mb{l}"] = partial(backward_mix, l)
    for step in (1, 2, 3):
        events[f"t{step}"] = partial(sum_taps, step)
    for name in FORWARD_ORDER + BACKWARD_ORDER:
        order.event = name
        events[name]()
    terms = [part for name in ("mix", "feed") for part in (state[f"{name}sum0"].keep, state[f"{name}sum0"].come)]
    terms += [state["mixsum1"].total, state["feedsum1"].total]
    result, dx = state["x2"], state["dx0"]
    taps_grad = state["taps"]
    taps_grad = jnp.concatenate([taps_grad[..., :count], taps_grad[..., 256 : 256 + count]], axis=1)
    taps_grad = jnp.swapaxes(taps_grad[:, :49], 1, 2)
    order.last += (taps_grad,)
    gain, bias, scale, in_grad, gated, out_grad, up, down = order(
        partial(unpack_kernel, 2),
        (place, *terms),
        [SM] + [VM] * len(terms),
        tuple(
            whole(ref.shape, F32)
            for ref in (
                norm_gains,
                norm_biases,
                layer_scales,
                in_proj,
                gated_weights,
                out_proj,
                up_proj,
                down_proj,
            )
        ),
        [],
        "unpack",
    )
    return (result, dx, gain, bias, scale, in_grad, taps_grad, gated, out_grad, up, down)


def fits(mesh):
    return dict(mesh.shape) == {"dp": 8, "fsdp": 4}


def layer_norm(values, gain_vec, bias_vec):
    center = values - jnp.mean(values, axis=-1, keepdims=True)
    spread = jnp.mean(center * center, axis=-1, keepdims=True)
    return center * lax.rsqrt(spread + 1e-06) * gain_vec + bias_vec


def branch_factors(layout_plan, keep_row, edge_cells, tile_edge):
    row_ids = jnp.arange(edge_cells, dtype=jnp.int32)[:, None]
    col_ids = jnp.arange(edge_cells, dtype=jnp.int32)[None, :]
    quarter = row_ids // tile_edge * 2 + col_ids // tile_edge
    image_ids = jnp.where(layout_plan[0] == 1, jnp.zeros_like(quarter), quarter)
    occupied = jnp.where(
        layout_plan[0] == 1, jnp.ones_like(quarter), (quarter < layout_plan[1]).astype(jnp.int32)
    )
    onehot = (image_ids.reshape(-1, 1) == jnp.arange(4, dtype=jnp.int32)[None, :]).astype(
        jnp.float32
    )
    keep_table = keep_row.reshape(4, -1).astype(jnp.float32)
    chosen = jnp.dot(onehot, keep_table, precision=lax.Precision.HIGHEST)
    return (image_ids, chosen * occupied.astype(jnp.float32).reshape(-1, 1) * 1.25)


def depthwise(values_in, kernel, image_ids):
    edge_cells = image_ids.shape[0]
    spatial = values_in.reshape(edge_cells, edge_cells, -1)
    padded = jnp.pad(spatial, ((3, 3), (3, 3), (0, 0)))
    padded_ids = jnp.pad(image_ids, 3, constant_values=-1)
    summed = jnp.zeros_like(spatial)
    for offset in range(49):
        row_off = offset // 7
        col_off = offset % 7
        nearby = padded[row_off : row_off + edge_cells, col_off : col_off + edge_cells]
        matched = (
            padded_ids[row_off : row_off + edge_cells, col_off : col_off + edge_cells] == image_ids
        ).astype(jnp.float32)
        summed = summed + nearby * matched[:, :, None] * kernel[:, offset]
    return summed.reshape(values_in.shape) / 3.0


def gated_widths(model_width):
    return [model_width // 16, model_width // 8, model_width // 4, model_width // 2, model_width]


def split_gated(flat_weights, model_width):
    widths = gated_widths(model_width)
    matrices = []
    cursor = 0
    for section_idx in range(4):
        amount = widths[section_idx] * widths[section_idx + 1]
        matrices.append(
            flat_weights[cursor : cursor + amount].reshape(
                widths[section_idx], widths[section_idx + 1]
            )
        )
        cursor = cursor + amount
    return matrices


def outer_sum(left_op, right_op):
    return lax.dot_general(
        left_op, right_op, (((0,), (0,)), ((), ())), preferred_element_type=jnp.float32
    )


def times_transpose(left_op, right_op):
    return lax.dot_general(
        left_op, right_op, (((1,), (1,)), ((), ())), preferred_element_type=jnp.float32
    )


def forward_block(residual, weights, kernel, image_ids, factors):
    in_weight, out_weight, up_weight, down_weight, gated_flat, gain_vec, bias_vec, scale_vec = (
        weights
    )
    model_width = residual.shape[1]
    widths = gated_widths(model_width)
    gain_full = gain_vec.astype(jnp.float32)
    bias_full = bias_vec.astype(jnp.float32)
    scale_full = scale_vec.astype(jnp.float32)
    normed = layer_norm(residual, gain_full[:model_width], bias_full[:model_width]).astype(
        jnp.bfloat16
    )
    mixed_all = jnp.dot(normed, in_weight, preferred_element_type=jnp.float32)
    scaled = depthwise(mixed_all[:, widths[0] :], kernel.astype(jnp.float32), image_ids)
    product = mixed_all[:, : widths[0]] * scaled[:, : widths[0]]
    lowered = []
    inners = []
    cursor = widths[0]
    for section_idx, matrix in enumerate(split_gated(gated_flat, model_width)):
        product_low = product.astype(jnp.bfloat16)
        inner_out = jnp.dot(product_low, matrix, preferred_element_type=jnp.float32)
        lowered.append(product_low)
        inners.append(inner_out)
        product = inner_out * scaled[:, cursor : cursor + widths[section_idx + 1]]
        cursor = cursor + widths[section_idx + 1]
    lowered.append(product.astype(jnp.bfloat16))
    branch = jnp.dot(lowered[4], out_weight, preferred_element_type=jnp.float32)
    middle = residual + factors[:, 0:1] * scale_full[:model_width] * branch
    normed_two = layer_norm(middle, gain_full[model_width:], bias_full[model_width:]).astype(
        jnp.bfloat16
    )
    hidden = jnp.dot(normed_two, up_weight, preferred_element_type=jnp.float32)
    activated = jax.nn.gelu(hidden).astype(jnp.bfloat16)
    expanded = jnp.dot(activated, down_weight, preferred_element_type=jnp.float32)
    output = middle + factors[:, 1:2] * scale_full[model_width:] * expanded
    retained = (
        residual,
        normed,
        mixed_all,
        scaled,
        lowered,
        inners,
        branch,
        middle,
        normed_two,
        hidden,
        activated,
        expanded,
    )
    return (output, retained)


def backward_block(grad_out, retained, weights, kernel, image_ids, factors):
    (
        residual,
        normed,
        mixed_all,
        scaled,
        lowered,
        inners,
        branch,
        middle,
        normed_two,
        hidden,
        activated,
        expanded,
    ) = retained
    in_weight, out_weight, up_weight, down_weight, gated_flat, gain_vec, bias_vec, scale_vec = (
        weights
    )
    model_width = residual.shape[1]
    widths = gated_widths(model_width)
    gain_full = gain_vec.astype(jnp.float32)
    bias_full = bias_vec.astype(jnp.float32)
    scale_full = scale_vec.astype(jnp.float32)
    first_factor = factors[:, 0:1]
    second_factor = factors[:, 1:2]
    scale_two_grad = jnp.sum(grad_out * second_factor * expanded, axis=0)
    expanded_grad = (grad_out * second_factor * scale_full[model_width:]).astype(jnp.bfloat16)
    down_weight_grad = outer_sum(activated, expanded_grad)
    activated_grad = times_transpose(expanded_grad, down_weight)
    unused_gelu, gelu_pull = jax.vjp(jax.nn.gelu, hidden)
    hidden_grad = gelu_pull(activated_grad)[0].astype(jnp.bfloat16)
    up_weight_grad = outer_sum(normed_two, hidden_grad)
    normed_two_grad = times_transpose(hidden_grad, up_weight)
    unused_two, second_pull = jax.vjp(
        layer_norm, middle, gain_full[model_width:], bias_full[model_width:]
    )
    middle_extra, gain_two_grad, bias_two_grad = second_pull(normed_two_grad)
    middle_grad = grad_out + middle_extra
    scale_one_grad = jnp.sum(middle_grad * first_factor * branch, axis=0)
    branch_grad = (middle_grad * first_factor * scale_full[:model_width]).astype(jnp.bfloat16)
    out_weight_grad = outer_sum(lowered[4], branch_grad)
    product_grad = times_transpose(branch_grad, out_weight)
    matrices = split_gated(gated_flat, model_width)
    starts = [0]
    for width_here in widths:
        starts.append(starts[-1] + width_here)
    gated_parts = [None, None, None, None]
    scaled_parts = [None, None, None, None, None]
    for section_idx in reversed(range(4)):
        scaled_part = scaled[:, starts[section_idx + 1] : starts[section_idx + 2]]
        inner_grad = (product_grad * scaled_part).astype(jnp.bfloat16)
        scaled_parts[section_idx + 1] = product_grad * inners[section_idx]
        gated_parts[section_idx] = outer_sum(lowered[section_idx], inner_grad)
        product_grad = times_transpose(inner_grad, matrices[section_idx])
    head_grad = product_grad * scaled[:, : widths[0]]
    scaled_parts[0] = product_grad * mixed_all[:, : widths[0]]
    scaled_grad = jnp.concatenate(scaled_parts, axis=1)
    unused_conv, conv_pull = jax.vjp(
        partial(depthwise, image_ids=image_ids),
        mixed_all[:, widths[0] :],
        kernel.astype(jnp.float32),
    )
    rest_grad, kernel_weight_grad = conv_pull(scaled_grad)
    mixed_grad = jnp.concatenate([head_grad, rest_grad], axis=1).astype(jnp.bfloat16)
    in_weight_grad = outer_sum(normed, mixed_grad)
    normed_grad = times_transpose(mixed_grad, in_weight)
    unused_one, first_pull = jax.vjp(
        layer_norm, residual, gain_full[:model_width], bias_full[:model_width]
    )
    residual_extra, gain_one_grad, bias_one_grad = first_pull(normed_grad)
    input_grad = middle_grad + residual_extra
    gated_grad = jnp.concatenate([matrix_grad.reshape(-1) for matrix_grad in gated_parts])
    weight_grads = (
        in_weight_grad,
        out_weight_grad,
        up_weight_grad,
        down_weight_grad,
        gated_grad,
        jnp.concatenate([gain_one_grad, gain_two_grad]),
        jnp.concatenate([bias_one_grad, bias_two_grad]),
        jnp.concatenate([scale_one_grad, scale_two_grad]),
    )
    return (input_grad, weight_grads, kernel_weight_grad)


def per_device(
    pixels,
    cotangent,
    image_plan,
    keep_mask,
    norm_gains,
    norm_biases,
    layer_scales,
    in_proj,
    depth_kernel,
    gated_weights,
    out_proj,
    up_proj,
    down_proj,
):
    tokens_here = pixels.shape[0]
    edge_cells = math.isqrt(tokens_here)
    tile_edge = edge_cells // 2
    layer_count = in_proj.shape[0]
    image_ids, factors = branch_factors(image_plan[0], keep_mask[0], edge_cells, tile_edge)
    residual = pixels.astype(jnp.float32)
    retained_all = []
    for layer_idx in range(layer_count):
        weights = (
            lax.all_gather(in_proj[layer_idx], ("dp", "fsdp"), axis=0, tiled=True),
            lax.all_gather(out_proj[layer_idx], ("dp", "fsdp"), axis=0, tiled=True),
            lax.all_gather(up_proj[layer_idx], ("dp", "fsdp"), axis=0, tiled=True),
            lax.all_gather(down_proj[layer_idx], ("dp", "fsdp"), axis=0, tiled=True),
            lax.all_gather(gated_weights[layer_idx], ("dp", "fsdp"), axis=0, tiled=True),
            lax.all_gather(norm_gains[layer_idx], ("dp", "fsdp"), axis=0, tiled=True),
            lax.all_gather(norm_biases[layer_idx], ("dp", "fsdp"), axis=0, tiled=True),
            lax.all_gather(layer_scales[layer_idx], ("dp", "fsdp"), axis=0, tiled=True),
        )
        kernel = lax.all_gather(depth_kernel[layer_idx], "fsdp", axis=0, tiled=True)
        residual, retained = forward_block(
            residual, weights, kernel, image_ids, factors[:, 2 * layer_idx : 2 * layer_idx + 2]
        )
        retained_all.append(retained)
    result = residual.astype(jnp.bfloat16)
    grad_now = cotangent.astype(jnp.float32)
    layer_grads = [None] * layer_count
    kernel_grads = [None] * layer_count
    for layer_idx in reversed(range(layer_count)):
        weights = (
            lax.all_gather(in_proj[layer_idx], ("dp", "fsdp"), axis=0, tiled=True),
            lax.all_gather(out_proj[layer_idx], ("dp", "fsdp"), axis=0, tiled=True),
            lax.all_gather(up_proj[layer_idx], ("dp", "fsdp"), axis=0, tiled=True),
            lax.all_gather(down_proj[layer_idx], ("dp", "fsdp"), axis=0, tiled=True),
            lax.all_gather(gated_weights[layer_idx], ("dp", "fsdp"), axis=0, tiled=True),
            lax.all_gather(norm_gains[layer_idx], ("dp", "fsdp"), axis=0, tiled=True),
            lax.all_gather(norm_biases[layer_idx], ("dp", "fsdp"), axis=0, tiled=True),
            lax.all_gather(layer_scales[layer_idx], ("dp", "fsdp"), axis=0, tiled=True),
        )
        kernel = lax.all_gather(depth_kernel[layer_idx], "fsdp", axis=0, tiled=True)
        grad_now, weight_grads, kernel_weight_grad = backward_block(
            grad_now,
            retained_all[layer_idx],
            weights,
            kernel,
            image_ids,
            factors[:, 2 * layer_idx : 2 * layer_idx + 2],
        )
        kernel_grads[layer_idx] = kernel_weight_grad
        layer_grads[layer_idx] = (
            lax.psum_scatter(weight_grads[0], ("dp", "fsdp"), scatter_dimension=0, tiled=True),
            lax.psum_scatter(weight_grads[1], ("dp", "fsdp"), scatter_dimension=0, tiled=True),
            lax.psum_scatter(weight_grads[2], ("dp", "fsdp"), scatter_dimension=0, tiled=True),
            lax.psum_scatter(weight_grads[3], ("dp", "fsdp"), scatter_dimension=0, tiled=True),
            lax.psum_scatter(weight_grads[4], ("dp", "fsdp"), scatter_dimension=0, tiled=True),
            lax.psum_scatter(weight_grads[5], ("dp", "fsdp"), scatter_dimension=0, tiled=True),
            lax.psum_scatter(weight_grads[6], ("dp", "fsdp"), scatter_dimension=0, tiled=True),
            lax.psum_scatter(weight_grads[7], ("dp", "fsdp"), scatter_dimension=0, tiled=True),
        )
    stacked = tuple(
        (
            jnp.stack([layer_grads[layer_idx][member] for layer_idx in range(layer_count)])
            for member in range(8)
        )
    )
    kernel_stack = jnp.stack(kernel_grads)
    kernel_share = lax.psum_scatter(
        kernel_stack.astype(jnp.bfloat16), "fsdp", scatter_dimension=1, tiled=True
    ).astype(jnp.float32)
    kernel_summed = lax.psum(kernel_share, "dp")
    return (
        result,
        grad_now,
        stacked[5],
        stacked[6],
        stacked[7],
        stacked[0],
        kernel_summed,
        stacked[4],
        stacked[1],
        stacked[2],
        stacked[3],
    )


def solution(mesh):
    in_specs = (
        P(("dp", "fsdp"), None),
        P(("dp", "fsdp"), None),
        P(("dp", "fsdp"), None),
        P(("dp", "fsdp"), None),
        P(None, ("dp", "fsdp")),
        P(None, ("dp", "fsdp")),
        P(None, ("dp", "fsdp")),
        P(None, ("dp", "fsdp"), None),
        P(None, "fsdp", None),
        P(None, ("dp", "fsdp")),
        P(None, ("dp", "fsdp"), None),
        P(None, ("dp", "fsdp"), None),
        P(None, ("dp", "fsdp"), None),
    )
    out_specs = (
        P(("dp", "fsdp"), None),
        P(("dp", "fsdp"), None),
        P(None, ("dp", "fsdp")),
        P(None, ("dp", "fsdp")),
        P(None, ("dp", "fsdp")),
        P(None, ("dp", "fsdp"), None),
        P(None, "fsdp", None),
        P(None, ("dp", "fsdp")),
        P(None, ("dp", "fsdp"), None),
        P(None, ("dp", "fsdp"), None),
        P(None, ("dp", "fsdp"), None),
    )
    return jax.shard_map(
        fast_device if fits(mesh) else per_device, mesh=mesh, in_specs=in_specs, out_specs=out_specs, check_vma=False
    )
```
